32 devices in a mesh: stream: 8 (over z, y), rep: 4 (over x, core).
Axes of the slice: x: 2, y: 2, z: 4, core: 2. Of those that a mesh axis runs over, the one named last changes fastest.
Arguments:
- queries: bfloat16 [4, 1024, 768], P('rep', 'stream'), may hold values from -6 to 6
- memory: bfloat16 [4, 8192, 768], P('rep', 'stream'), may hold values from -6 to 6
- routes: int32 [4, 64], P('rep', 'stream'), may hold values from 0 to 7, as said below
- w_self: bfloat16 [768, 2304], replicated, may hold values from -0.21875 to 0.21875
- w_self_out: bfloat16 [768, 768], replicated, may hold values from -2.5 to 2.5
- w_cross_q: bfloat16 [768, 768], replicated, may hold values from -0.21875 to 0.21875
- w_cross_kv: bfloat16 [768, 1536], replicated, may hold values from -0.21875 to 0.21875
- w_cross_out: bfloat16 [768, 768], replicated, may hold values from -3.5 to 3.5
- w_up: bfloat16 [768, 3072], replicated, may hold values from -0.21875 to 0.21875
- b_up: bfloat16 [3072], replicated, may hold values from -1.5 to 1.5
- w_down: bfloat16 [3072, 768], replicated, may hold values from -0.109375 to 0.109375
- b_down: bfloat16 [768], replicated, may hold values from -1.5 to 1.5
- gain_one: bfloat16 [768], replicated, may hold values from 0.5 to 1.5
- shift_one: bfloat16 [768], replicated, may hold values from -1.5 to 1.5
- gain_two: bfloat16 [768], replicated, may hold values from 0.5 to 1.5
- shift_two: bfloat16 [768], replicated, may hold values from -1.5 to 1.5
- gain_three: bfloat16 [768], replicated, may hold values from 0.5 to 1.5
- shift_three: bfloat16 [768], replicated, may hold values from -1.5 to 1.5
- cotangent: bfloat16 [4, 1024, 768], P('rep', 'stream'), may hold values from -6 to 6
Outputs:
- layer_out: bfloat16 [4, 1024, 768], P('rep', 'stream')
- d_queries: float32 [4, 1024, 768], P('rep', 'stream')
- d_memory: bfloat16 [4, 8192, 768], P('rep', 'stream')
- d_w_self: float32 [768, 2304], P('stream')
- d_w_self_out: float32 [768, 768], P('stream')
- d_w_cross_q: float32 [768, 768], P('stream')
- d_w_cross_kv: float32 [768, 1536], P('stream')
- d_w_cross_out: float32 [768, 768], P('stream')
- d_w_up: float32 [768, 3072], P('stream')
- d_b_up: float32 [3072], P('stream')
- d_w_down: float32 [3072, 768], P('stream')
- d_b_down: float32 [768], P('stream')
- d_gain_one: float32 [768], P('stream')
- d_shift_one: float32 [768], P('stream')
- d_gain_two: float32 [768], P('stream')
- d_shift_two: float32 [768], P('stream')
- d_gain_three: float32 [768], P('stream')
- d_shift_three: float32 [768], P('stream')
The draws below stay inside these ranges and needn't reach their ends.
Inputs may be any that keep to these rules, and one draw needn't show every extreme that they name: `routes`: of the 8 blocks of one device, exactly 2 are read by the group of the same index of stream in the same replica, and at most 2 by any one group.
All inputs are finite; a program needn't handle non-finite values.
Results may differ from the reference program's by a relative error of at most 0.025.
Values may be sent and summed in bfloat16 or wider, within the bound.
No kernel may reach another device: no remote copies, remote signals or barrier semaphores. Data moves between devices by JAX's collectives and lax.ppermute only.
A program may use at most 384 MiB of HBM per device.

```python
import jax
import jax.numpy as jnp
from jax import lax

D = 768
HEADS = 12
HEAD_DIM = 64
FF = 3072
GLEN = 128
BLK = 128
MBLK = 8
CAP = 2
REPLICAS = 4
QTOK = 1024
MTOK = 8192
N_STREAM = 8


def draw_routes(key, part):
    key = jax.random.fold_in(key, 11)
    key_noise, key_pull, key_order = jax.random.split(key, 3)
    slot_total = N_STREAM * CAP
    row_total = REPLICAS * N_STREAM
    noise = jax.random.randint(key_noise, (row_total, slot_total), 0, 65536)
    pull = jax.random.randint(key_pull, (REPLICAS, N_STREAM), 0, 2)
    pull_rows = jnp.repeat(jnp.repeat(pull, N_STREAM, axis=0), CAP, axis=1)
    slot_ids = jnp.arange(slot_total, dtype=jnp.int32)[None, :]
    own_index = (jnp.arange(row_total, dtype=jnp.int32) % N_STREAM)[:, None]
    scores = (pull_rows * 32768 + noise) * slot_total + slot_ids
    scores = jnp.where(slot_ids // CAP == own_index, -1, scores)
    picked = lax.top_k(scores, MBLK - CAP)[1]
    targets = jnp.concatenate([jnp.broadcast_to(own_index, (row_total, CAP)), picked // CAP], axis=1)
    order_keys = jax.random.randint(key_order, (row_total, MBLK), 0, 65536) * MBLK + jnp.arange(MBLK, dtype=jnp.int32)[None, :]
    order = jnp.argsort(order_keys, axis=1)
    targets = jnp.take_along_axis(targets, order, axis=1)
    return targets.reshape(REPLICAS, N_STREAM * MBLK).astype(jnp.int32)


def block_scale(rng, shape, cuts, least, high):
    def one(position, parts):
        heights = jax.random.uniform(jax.random.fold_in(jax.random.fold_in(rng, 6), position), (parts,), jnp.float32, least / len(cuts), high / len(cuts))
        return jnp.repeat(jnp.exp(heights), shape[position] // parts).reshape((-1,) + (1,) * (len(shape) - position - 1))

    factor_of = one(*cuts[0])
    for cut in cuts[1:]:
        factor_of = factor_of * one(*cut)
    return factor_of


def gaussian(stream_key, extent, scale, limit, shards=(), kind=jnp.bfloat16):
    values = jax.random.normal(stream_key, extent, jnp.float32) * scale
    if len(shards) > 0:
        values = block_scale(stream_key, extent, shards, -0.22, 0.18) * values
    return jnp.clip(values, min=-limit, max=limit).astype(kind)


def setup_inputs(seed: int = 0) -> dict:
    key_of = jax.random.split(jax.random.key(seed), 20)
    return {
        "queries": gaussian(key_of[0], (REPLICAS, QTOK, D), 1.0, 6.0, ((0, 4), (1, 8))),
        "memory": gaussian(key_of[1], (REPLICAS, MTOK, D), 1.0, 6.0, ((0, 4), (1, 8))),
        "routes": draw_routes(jax.random.fold_in(key_of[19], 71), 0),
        "w_self": gaussian(key_of[3], (D, 3 * D), D ** -0.5, 0.21875),
        "w_self_out": gaussian(key_of[4], (D, D), (max(1, D // 128)) ** -0.5, 2.5),
        "w_cross_q": gaussian(key_of[5], (D, D), D ** -0.5, 0.21875),
        "w_cross_kv": gaussian(key_of[6], (D, 2 * D), D ** -0.5, 0.21875),
        "w_cross_out": gaussian(key_of[7], (D, D), (max(1, D // 256)) ** -0.5, 3.5),
        "w_up": gaussian(key_of[8], (D, FF), D ** -0.5, 0.21875),
        "b_up": gaussian(key_of[9], (FF,), 0.3, 1.5),
        "w_down": gaussian(key_of[10], (FF, D), FF ** -0.5, 0.109375),
        "b_down": gaussian(key_of[11], (D,), 0.3, 1.5),
        "gain_one": jnp.clip(1.0 + 0.1 * jax.random.normal(key_of[12], (D,), jnp.float32), 0.5, 1.5).astype(jnp.bfloat16),
        "shift_one": gaussian(key_of[13], (D,), 0.3, 1.5),
        "gain_two": jnp.clip(1.0 + 0.1 * jax.random.normal(key_of[14], (D,), jnp.float32), 0.5, 1.5).astype(jnp.bfloat16),
        "shift_two": gaussian(key_of[15], (D,), 0.3, 1.5),
        "gain_three": jnp.clip(1.0 + 0.1 * jax.random.normal(key_of[16], (D,), jnp.float32), 0.5, 1.5).astype(jnp.bfloat16),
        "shift_three": gaussian(key_of[17], (D,), 0.3, 1.5),
        "cotangent": gaussian(key_of[18], (REPLICAS, QTOK, D), 1.0, 6.0, ((0, 4), (1, 8))),
    }


@jax.custom_vjp
def low(v):
    return lax.optimization_barrier(v.astype(jnp.bfloat16)).astype(jnp.float32)

@jax.custom_vjp
def low_back(v):
    return v

def low_keep(v):
    return (low(v), None)

def low_pass(kept, grad):
    return (grad,)

def back_keep(v):
    return (v, None)

def back_low(kept, grad):
    return (low(grad),)
low.defvjp(low_keep, low_pass)
low_back.defvjp(back_keep, back_low)

def product(left, right):
    return jnp.dot(left, right, precision=lax.Precision.HIGHEST)

def layer_norm(rows, gain, shift):
    centred = rows - lax.optimization_barrier(jnp.mean(rows, axis=-1, keepdims=True))
    spread = lax.optimization_barrier(jnp.mean(centred * centred, axis=-1, keepdims=True))
    return centred * lax.rsqrt(spread + 1e-05) * gain + shift

def attention(query, key_rows, value_rows, key_ok):
    count = query.shape[0]
    depth = key_rows.shape[0]
    query_heads = query.reshape(count, HEADS, HEAD_DIM)
    key_heads = key_rows.reshape(depth, HEADS, HEAD_DIM)
    value_heads = value_rows.reshape(depth, HEADS, HEAD_DIM)
    scores = jnp.einsum('ghe,khe->hgk', query_heads, key_heads, precision=lax.Precision.HIGHEST)
    scores = low_back(scores * HEAD_DIM ** (-0.5))
    if key_ok is not None:
        scores = jnp.where(key_ok[None, None, :], scores, -1e+30)
    weights_soft = low(jax.nn.softmax(scores, axis=-1))
    mixed = jnp.einsum('hgk,khe->ghe', weights_soft, value_heads, precision=lax.Precision.HIGHEST)
    return mixed.reshape(count, D)

def group_forward(tokens, keys_values, key_ok, params):
    w_self, w_self_out, w_cross_q, w_cross_kv, w_cross_out, w_up, b_up, w_down, b_down, gain_one, shift_one, gain_two, shift_two, gain_three, shift_three = params
    joined = low_back(low(product(tokens, w_self)))
    attended = low_back(low(attention(joined[:, :D], joined[:, D:2 * D], joined[:, 2 * D:], None)))
    branch_one = low_back(product(attended, w_self_out))
    normed_one = low(layer_norm(tokens + branch_one, gain_one, shift_one))
    query_cross = low_back(low(product(normed_one, w_cross_q)))
    crossed = low_back(low(attention(query_cross, keys_values[:, :D], keys_values[:, D:], key_ok)))
    branch_two = low_back(product(crossed, w_cross_out))
    normed_two = low(layer_norm(normed_one + branch_two, gain_two, shift_two))
    hidden_pre = low_back(product(normed_two, w_up) + b_up)
    hidden = low(jax.nn.gelu(hidden_pre, approximate=False))
    branch_three = low_back(product(hidden, w_down) + b_down)
    return layer_norm(normed_two + branch_three, gain_three, shift_three)

def slot_tables(routes):
    target = routes.reshape(REPLICAS * N_STREAM, MBLK)
    hit_table = (target[:, :, None] == jnp.arange(N_STREAM, dtype=jnp.int32)[None, None, :]).astype(jnp.int32)
    before = jnp.cumsum(hit_table, axis=1) - hit_table
    rank_in = lax.optimization_barrier(jnp.sum(before * hit_table, axis=2))
    slot_of_block = target * CAP + rank_in
    matched = (slot_of_block[:, None, :] == jnp.arange(N_STREAM * CAP, dtype=jnp.int32)[None, :, None]).astype(jnp.int32)
    block_at = lax.optimization_barrier(jnp.sum(matched * jnp.arange(MBLK, dtype=jnp.int32)[None, None, :], axis=2))
    live_slot = lax.optimization_barrier(jnp.sum(matched, axis=2))
    source_row = jnp.arange(REPLICAS * N_STREAM, dtype=jnp.int32)[:, None]
    global_block = source_row * MBLK + block_at
    global_block = global_block.reshape(REPLICAS, N_STREAM, N_STREAM, CAP).transpose(0, 2, 1, 3)
    live_slot = live_slot.reshape(REPLICAS, N_STREAM, N_STREAM, CAP).transpose(0, 2, 1, 3)
    return (global_block.reshape(REPLICAS * N_STREAM, N_STREAM * CAP).astype(jnp.int32), live_slot.reshape(REPLICAS * N_STREAM, N_STREAM * CAP).astype(jnp.int32))

def reference(queries, memory, routes, w_self, w_self_out, w_cross_q, w_cross_kv, w_cross_out, w_up, b_up, w_down, b_down, gain_one, shift_one, gain_two, shift_two, gain_three, shift_three, cotangent):
    index_table, live_table = slot_tables(routes)
    weights = tuple((item.astype(jnp.float32) for item in (w_self, w_self_out, w_cross_q, w_cross_kv, w_cross_out, w_up, b_up, w_down, b_down, gain_one, shift_one, gain_two, shift_two, gain_three, shift_three)))

    def forward(tokens_all, memory_all, *params):
        kv_all = low_back(low(product(memory_all.reshape(-1, D), params[3])))
        kv_all = kv_all.reshape(REPLICAS * N_STREAM * MBLK, BLK, 2 * D)

        def one_group(item):
            tokens, index_row, live_row = item
            keys_values = jnp.take(kv_all, index_row, axis=0).reshape(-1, 2 * D)
            key_ok = jnp.repeat(live_row, BLK) > 0
            return group_forward(tokens, keys_values, key_ok, params)
        outputs = lax.map(jax.checkpoint(one_group), (tokens_all.reshape(REPLICAS * N_STREAM, GLEN, D), index_table, live_table))
        return outputs.reshape(REPLICAS, N_STREAM * GLEN, D)
    result, pullback = jax.vjp(forward, queries.astype(jnp.float32), memory.astype(jnp.float32), *weights)
    grads = pullback(cotangent.astype(jnp.float32))
    return (result.astype(jnp.bfloat16), grads[0], grads[1].astype(jnp.bfloat16), grads[2], grads[3], grads[4], grads[5], grads[6], grads[7], grads[8], grads[9], grads[10], grads[11], grads[12], grads[13], grads[14], grads[15], grads[16])
```

```python
import functools

import jax
import jax.numpy as jnp
from jax import lax
from jax.experimental import pallas as pl
from jax.experimental.pallas import tpu as pltpu
from jax.sharding import PartitionSpec as P

HEADS = 12
HEAD_DIM = 64
BLK = 128


def matmul(left, right):
    return jnp.dot(left, right, preferred_element_type=jnp.float32)


def product_left(left, right):
    return lax.dot_general(
        left, right, (((0,), (0,)), ((), ())), preferred_element_type=jnp.float32
    )


def product_right(left, right):
    return lax.dot_general(
        left, right, (((1,), (1,)), ((), ())), preferred_element_type=jnp.float32
    )


def layer_norm(rows, gain, shift):
    centred = rows - jnp.mean(rows, axis=-1, keepdims=True)
    spread = jnp.mean(centred * centred, axis=-1, keepdims=True)
    return centred * lax.rsqrt(spread + 1e-05) * gain + shift


def split_heads(rows):
    return rows.reshape(rows.shape[0], HEADS, HEAD_DIM).transpose(1, 0, 2)


def join_heads(rows):
    return rows.transpose(1, 0, 2).reshape(rows.shape[1], HEADS * HEAD_DIM)


def masked_scores(query_head, key_head, key_ok):
    scores = product_right(query_head, key_head) * HEAD_DIM ** (-0.5)
    if key_ok is not None:
        scores = jnp.where(key_ok[None, :], scores, -1e30)
    return scores


def attend_forward(query, key_rows, value_rows, key_ok):

    def one_head(item):
        query_head, key_head, value_head = item
        scores = masked_scores(query_head, key_head, key_ok)
        row_max = jnp.max(scores, axis=1, keepdims=True)
        exponent = jnp.exp(scores - row_max)
        row_total = jnp.sum(exponent, axis=1, keepdims=True)
        probability = (exponent / row_total).astype(jnp.bfloat16)
        return (matmul(probability, value_head), (row_max + jnp.log(row_total))[:, 0])

    mixed, log_total = lax.map(
        one_head, (split_heads(query), split_heads(key_rows), split_heads(value_rows))
    )
    return (join_heads(mixed), log_total)


def attend_backward(query, key_rows, value_rows, key_ok, log_total, d_mixed):
    factor = HEAD_DIM ** (-0.5)

    def one_head(item):
        query_head, key_head, value_head, total_head, grad_head = item
        scores = masked_scores(query_head, key_head, key_ok)
        probability = jnp.exp(scores - total_head[:, None])
        d_prob = product_right(grad_head, value_head)
        d_scores = probability * (d_prob - jnp.sum(d_prob * probability, axis=1, keepdims=True))
        d_scores = d_scores.astype(jnp.bfloat16)
        d_query = matmul(d_scores, key_head) * factor
        d_key = product_left(d_scores, query_head) * factor
        d_value = product_left(probability.astype(jnp.bfloat16), grad_head)
        return (d_query, d_key, d_value)

    d_query, d_key, d_value = lax.map(
        one_head,
        (
            split_heads(query),
            split_heads(key_rows),
            split_heads(value_rows),
            log_total,
            split_heads(d_mixed),
        ),
    )
    return (join_heads(d_query), join_heads(d_key), join_heads(d_value))


def on_device(
    queries,
    memory,
    routes,
    w_self,
    w_self_out,
    w_cross_q,
    w_cross_kv,
    w_cross_out,
    w_up,
    b_up,
    w_down,
    b_down,
    gain_one,
    shift_one,
    gain_two,
    shift_two,
    gain_three,
    shift_three,
    cotangent,
):
    streams = lax.axis_size("stream")
    blocks = routes.shape[1]
    capacity = max(2, 2 * blocks // streams)
    slot_count = streams * capacity
    model_width = w_self_out.shape[0]
    target = routes[0]
    hit_table = (target[:, None] == jnp.arange(streams, dtype=jnp.int32)[None, :]).astype(jnp.int32)
    before = jnp.cumsum(hit_table, axis=0) - hit_table
    rank_in = jnp.sum(before * hit_table, axis=1)
    slot_of_block = target * capacity + rank_in
    matched = (slot_of_block[None, :] == jnp.arange(slot_count, dtype=jnp.int32)[:, None]).astype(
        jnp.int32
    )
    block_at = jnp.sum(matched * jnp.arange(blocks, dtype=jnp.int32)[None, :], axis=1)
    live_slot = jnp.sum(matched, axis=1)
    live_grid = live_slot.reshape(streams, capacity)
    filled = (live_slot > 0)[:, None, None]
    nothing = jnp.zeros((), jnp.bfloat16)
    memory_rows = memory[0]
    projected = (
        matmul(memory_rows, w_cross_kv).astype(jnp.bfloat16).reshape(blocks, BLK, 2 * model_width)
    )
    outgoing = jnp.where(filled, jnp.take(projected, block_at, axis=0), nothing)
    arrived, arrived_live = (
        lax.all_to_all(
            outgoing.reshape(streams, capacity, BLK, 2 * model_width),
            "stream",
            split_axis=0,
            concat_axis=0,
            tiled=True,
        ),
        lax.all_to_all(live_grid, "stream", split_axis=0, concat_axis=0, tiled=True),
    )
    keys_values = arrived.reshape(-1, 2 * model_width)
    key_ok = jnp.repeat(arrived_live.reshape(-1), BLK) > 0
    key_cross = keys_values[:, :model_width]
    value_cross = keys_values[:, model_width:]
    gain_a = gain_one.astype(jnp.float32)
    shift_a = shift_one.astype(jnp.float32)
    gain_b = gain_two.astype(jnp.float32)
    shift_b = shift_two.astype(jnp.float32)
    gain_c = gain_three.astype(jnp.float32)
    shift_c = shift_three.astype(jnp.float32)
    tokens = queries[0]
    joined = matmul(tokens, w_self).astype(jnp.bfloat16)
    query_self = joined[:, :model_width]
    key_self = joined[:, model_width : 2 * model_width]
    value_self = joined[:, 2 * model_width :]
    mixed_self, total_self = attend_forward(query_self, key_self, value_self, None)
    mixed_self = mixed_self.astype(jnp.bfloat16)
    residual_one = tokens.astype(jnp.float32) + matmul(mixed_self, w_self_out)
    normed_one = layer_norm(residual_one, gain_a, shift_a).astype(jnp.bfloat16)
    query_cross = matmul(normed_one, w_cross_q).astype(jnp.bfloat16)
    mixed_cross, total_cross = attend_forward(query_cross, key_cross, value_cross, key_ok)
    mixed_cross = mixed_cross.astype(jnp.bfloat16)
    residual_two = normed_one.astype(jnp.float32) + matmul(mixed_cross, w_cross_out)
    normed_two = layer_norm(residual_two, gain_b, shift_b).astype(jnp.bfloat16)
    hidden_pre = matmul(normed_two, w_up) + b_up.astype(jnp.float32)
    hidden = jax.nn.gelu(hidden_pre, approximate=False).astype(jnp.bfloat16)
    residual_three = (
        normed_two.astype(jnp.float32) + matmul(hidden, w_down) + b_down.astype(jnp.float32)
    )
    layer_out = layer_norm(residual_three, gain_c, shift_c).astype(jnp.bfloat16)
    grad_out = cotangent[0].astype(jnp.float32)
    norm_three_pull = jax.vjp(layer_norm, residual_three, gain_c, shift_c)[1]
    d_residual_three, d_gain_c, d_shift_c = norm_three_pull(grad_out)
    d_branch_three = d_residual_three.astype(jnp.bfloat16)
    d_b_down = jnp.sum(d_branch_three.astype(jnp.float32), axis=0)
    d_w_down = product_left(hidden, d_branch_three)
    d_hidden = product_right(d_branch_three, w_down)
    gelu_pull = jax.vjp(lambda value: jax.nn.gelu(value, approximate=False), hidden_pre)[1]
    d_hidden_pre = gelu_pull(d_hidden)[0].astype(jnp.bfloat16)
    d_b_up = jnp.sum(d_hidden_pre.astype(jnp.float32), axis=0)
    d_w_up = product_left(normed_two, d_hidden_pre)
    d_normed_two = d_residual_three + product_right(d_hidden_pre, w_up)
    norm_two_pull = jax.vjp(layer_norm, residual_two, gain_b, shift_b)[1]
    d_residual_two, d_gain_b, d_shift_b = norm_two_pull(d_normed_two)
    d_branch_two = d_residual_two.astype(jnp.bfloat16)
    d_w_cross_out = product_left(mixed_cross, d_branch_two)
    d_mixed_cross = product_right(d_branch_two, w_cross_out).astype(jnp.bfloat16)
    d_query_cross, d_key_cross, d_value_cross = attend_backward(
        query_cross, key_cross, value_cross, key_ok, total_cross, d_mixed_cross
    )
    d_query_cross = d_query_cross.astype(jnp.bfloat16)
    d_keys_values = jnp.concatenate([d_key_cross, d_value_cross], axis=1).astype(jnp.bfloat16)
    d_w_cross_q = product_left(normed_one, d_query_cross)
    d_normed_one = d_residual_two + product_right(d_query_cross, w_cross_q)
    norm_one_pull = jax.vjp(layer_norm, residual_one, gain_a, shift_a)[1]
    d_residual_one, d_gain_a, d_shift_a = norm_one_pull(d_normed_one)
    d_branch_one = d_residual_one.astype(jnp.bfloat16)
    d_w_self_out = product_left(mixed_self, d_branch_one)
    d_mixed_self = product_right(d_branch_one, w_self_out).astype(jnp.bfloat16)
    d_query_self, d_key_self, d_value_self = attend_backward(
        query_self, key_self, value_self, None, total_self, d_mixed_self
    )
    d_joined = jnp.concatenate([d_query_self, d_key_self, d_value_self], axis=1).astype(
        jnp.bfloat16
    )
    d_w_self = product_left(tokens, d_joined)
    d_tokens = d_residual_one + product_right(d_joined, w_self)
    returned = lax.all_to_all(
        d_keys_values.reshape(streams, capacity, BLK, 2 * model_width),
        "stream",
        split_axis=0,
        concat_axis=0,
        tiled=True,
    )
    d_block_rows = jnp.take(
        returned.reshape(slot_count, BLK, 2 * model_width), slot_of_block, axis=0
    ).reshape(-1, 2 * model_width)
    d_w_cross_kv = product_left(memory_rows, d_block_rows)
    d_memory = product_right(d_block_rows, w_cross_kv).astype(jnp.bfloat16)
    gradients = (
        d_w_self,
        d_w_self_out,
        d_w_cross_q,
        d_w_cross_kv,
        d_w_cross_out,
        d_w_up,
        d_b_up,
        d_w_down,
        d_b_down,
        d_gain_a,
        d_shift_a,
        d_gain_b,
        d_shift_b,
        d_gain_c,
        d_shift_c,
    )
    shapes = [item.shape for item in gradients]
    flat = [item.reshape(-1) for item in gradients]
    (
        share_self,
        share_self_out,
        share_cross_q,
        share_cross_kv,
        share_cross_out,
        share_up,
        share_b_up,
        share_down,
        share_b_down,
        share_gain_a,
        share_shift_a,
        share_gain_b,
        share_shift_b,
        share_gain_c,
        share_shift_c,
    ) = (
        lax.psum_scatter(flat[0], "stream", scatter_dimension=0, tiled=True),
        lax.psum_scatter(flat[1], "stream", scatter_dimension=0, tiled=True),
        lax.psum_scatter(flat[2], "stream", scatter_dimension=0, tiled=True),
        lax.psum_scatter(flat[3], "stream", scatter_dimension=0, tiled=True),
        lax.psum_scatter(flat[4], "stream", scatter_dimension=0, tiled=True),
        lax.psum_scatter(flat[5], "stream", scatter_dimension=0, tiled=True),
        lax.psum_scatter(flat[6], "stream", scatter_dimension=0, tiled=True),
        lax.psum_scatter(flat[7], "stream", scatter_dimension=0, tiled=True),
        lax.psum_scatter(flat[8], "stream", scatter_dimension=0, tiled=True),
        lax.psum_scatter(flat[9], "stream", scatter_dimension=0, tiled=True),
        lax.psum_scatter(flat[10], "stream", scatter_dimension=0, tiled=True),
        lax.psum_scatter(flat[11], "stream", scatter_dimension=0, tiled=True),
        lax.psum_scatter(flat[12], "stream", scatter_dimension=0, tiled=True),
        lax.psum_scatter(flat[13], "stream", scatter_dimension=0, tiled=True),
        lax.psum_scatter(flat[14], "stream", scatter_dimension=0, tiled=True),
    )
    summed = (
        lax.psum(share_self.astype(jnp.bfloat16), "rep").astype(jnp.float32),
        lax.psum(share_self_out.astype(jnp.bfloat16), "rep").astype(jnp.float32),
        lax.psum(share_cross_q.astype(jnp.bfloat16), "rep").astype(jnp.float32),
        lax.psum(share_cross_kv.astype(jnp.bfloat16), "rep").astype(jnp.float32),
        lax.psum(share_cross_out.astype(jnp.bfloat16), "rep").astype(jnp.float32),
        lax.psum(share_up.astype(jnp.bfloat16), "rep").astype(jnp.float32),
        lax.psum(share_b_up.astype(jnp.bfloat16), "rep").astype(jnp.float32),
        lax.psum(share_down.astype(jnp.bfloat16), "rep").astype(jnp.float32),
        lax.psum(share_b_down.astype(jnp.bfloat16), "rep").astype(jnp.float32),
        lax.psum(share_gain_a.astype(jnp.bfloat16), "rep").astype(jnp.float32),
        lax.psum(share_shift_a.astype(jnp.bfloat16), "rep").astype(jnp.float32),
        lax.psum(share_gain_b.astype(jnp.bfloat16), "rep").astype(jnp.float32),
        lax.psum(share_shift_b.astype(jnp.bfloat16), "rep").astype(jnp.float32),
        lax.psum(share_gain_c.astype(jnp.bfloat16), "rep").astype(jnp.float32),
        lax.psum(share_shift_c.astype(jnp.bfloat16), "rep").astype(jnp.float32),
    )
    results = [
        part.reshape((shape[0] // streams,) + tuple(shape[1:]))
        for part, shape in zip(summed, shapes)
    ]
    return (
        layer_out[None],
        d_tokens[None],
        d_memory[None],
        results[0],
        results[1],
        results[2],
        results[3],
        results[4],
        results[5],
        results[6],
        results[7],
        results[8],
        results[9],
        results[10],
        results[11],
        results[12],
        results[13],
        results[14],
    )


PAIRS = HEADS // 2
LANES = 2 * HEAD_DIM
FACTOR = HEAD_DIM ** (-0.5)
BF = jnp.bfloat16
F32 = jnp.float32
AXES = ("stream", "rep")


def whole_in_vmem(count):
    return [pl.BlockSpec(memory_space=pltpu.VMEM)] * count


def local_kernel(body, out_shape, scalars=(), arrays=(), scratch=(), flops=0, limit=52):
    moved = sum(a.size * a.dtype.itemsize for a in arrays)
    moved += sum(o.size * o.dtype.itemsize for o in out_shape)
    return pl.pallas_call(
        body,
        out_shape=list(out_shape),
        in_specs=[pl.BlockSpec(memory_space=pltpu.SMEM)] * len(scalars) + whole_in_vmem(len(arrays)),
        out_specs=whole_in_vmem(len(out_shape)),
        scratch_shapes=list(scratch),
        compiler_params=pltpu.CompilerParams(vmem_limit_bytes=limit * 1024 * 1024),
        cost_estimate=pl.CostEstimate(flops=flops, bytes_accessed=moved, transcendentals=0),
    )(*scalars, *arrays)


def like(shape, dtype):
    return jax.ShapeDtypeStruct(shape, dtype)


def dot_nn(left, right):
    return lax.dot_general(left, right, (((1,), (0,)), ((), ())), preferred_element_type=F32)


def dot_nt(left, right):
    return lax.dot_general(left, right, (((1,), (1,)), ((), ())), preferred_element_type=F32)


def head_masks(rows):
    lane = lax.broadcasted_iota(jnp.int32, (rows, LANES), 1)
    return lane < HEAD_DIM


def stack_heads(pair, first, scale):
    wide = pair.astype(F32) * scale
    zero = jnp.zeros_like(wide)
    return jnp.concatenate(
        [jnp.where(first, wide, zero), jnp.where(first, zero, wide)], axis=0
    ).astype(BF)


def unstack_heads(both, first):
    rows = both.shape[0] // 2
    return jnp.where(first, both[:rows], both[rows:])


def norm_parts(rows):
    centred = rows - jnp.mean(rows, axis=1, keepdims=True)
    spread = jnp.mean(centred * centred, axis=1, keepdims=True)
    inverse = lax.rsqrt(spread + 1e-05)
    return centred * inverse, inverse


def norm_pull(grad, hat, inverse, gain):
    scaled = grad * gain
    inner = scaled - jnp.mean(scaled, axis=1, keepdims=True)
    inner = inner - hat * jnp.mean(scaled * hat, axis=1, keepdims=True)
    return (
        inverse * inner,
        jnp.sum(grad * hat, axis=0, keepdims=True),
        jnp.sum(grad, axis=0, keepdims=True),
    )


def deal_blocks(routes_ref, memory_ref, out_ref):
    out_ref[...] = jnp.zeros_like(out_ref)
    blocks = memory_ref.shape[0] // BLK
    width = memory_ref.shape[1]
    for b in range(blocks):
        group = routes_ref[0, b]
        rank = jnp.int32(0)
        for earlier in range(b):
            rank = rank + (routes_ref[0, earlier] == group).astype(jnp.int32)
        row = pl.multiple_of(rank * BLK, BLK)
        lane = pl.multiple_of(rank * (width // 2), LANES)
        out_ref[group, pl.ds(row, BLK), :] = memory_ref[b * BLK : (b + 1) * BLK, :]
        out_ref[group, 2 * BLK : 2 * BLK + 16, pl.ds(lane, width // 2)] = jnp.ones(
            (16, width // 2), BF
        )


def self_forward(tok, w_in, w_out, w_q, gain, shift, joined, r1, qc, turned):
    width = tok.shape[1]
    rows = tok.shape[0]
    joined[...] = dot_nn(tok[...], w_in[...]).astype(BF)
    first = head_masks(rows)
    mixed = []
    for j in range(PAIRS):
        at = j * LANES
        q2 = stack_heads(joined[:, at : at + LANES], first, FACTOR)
        key = joined[:, width + at : width + at + LANES]
        value = joined[:, 2 * width + at : 2 * width + at + LANES]
        scores = dot_nt(q2, key)
        power = jnp.exp(scores - jnp.max(scores, axis=1, keepdims=True))
        prob = (power / jnp.sum(power, axis=1, keepdims=True)).astype(BF)
        mixed.append(unstack_heads(dot_nn(prob, value), first).astype(BF))
    o1 = jnp.concatenate(mixed, axis=1)
    res = tok[...].astype(F32) + dot_nn(o1, w_out[...])
    r1[...] = res
    hat, _ = norm_parts(res)
    h1 = (hat * gain[...].astype(F32) + shift[...].astype(F32)).astype(BF)
    qc[...] = dot_nn(h1, w_q[...]).astype(BF)
    turned[0:width, :] = tok[...].T
    turned[width : 2 * width, :] = o1.T
    turned[2 * width : 3 * width, :] = h1.T


def cross_forward(qc, parcels, w_kv, o2, kv, sums, s_ref, p_ref, bias_ref):
    width = qc.shape[1]
    rows = qc.shape[0]
    sources = parcels.shape[0]
    span = 2 * BLK
    first = head_masks(rows)
    for k in range(sources):
        kv[k * span : (k + 1) * span, :] = dot_nn(parcels[k, 0:span, :], w_kv[...]).astype(BF)
        for c in range(2):
            flag = parcels[k, span : span + 16, c * (width // 2) : c * (width // 2) + BLK]
            bias_ref[:, k * span + c * BLK : k * span + (c + 1) * BLK] = jnp.where(
                flag[0:8].astype(F32) > 0.5, 0.0, -1e30
            )
    lane = lax.broadcasted_iota(jnp.int32, (2 * rows, LANES), 1)
    sums[...] = jnp.zeros_like(sums)

    def one_pair(j, carry):
        at = pl.multiple_of(j * LANES, LANES)
        q2 = stack_heads(qc[:, pl.ds(at, LANES)], first, FACTOR)
        top = None
        for k in range(sources):
            key = kv[k * span : (k + 1) * span, pl.ds(at, LANES)]
            scores = dot_nt(q2, key) + bias_ref[0:1, k * span : (k + 1) * span]
            s_ref[:, k * span : (k + 1) * span] = scores
            most = jnp.maximum(scores[:, :LANES], scores[:, LANES:])
            top = most if top is None else jnp.maximum(top, most)
        peak = jnp.max(top, axis=1, keepdims=True)
        total = None
        for k in range(sources):
            power = jnp.exp(s_ref[:, k * span : (k + 1) * span] - peak)
            p_ref[:, k * span : (k + 1) * span] = power.astype(BF)
            part = power[:, :LANES] + power[:, LANES:]
            total = part if total is None else total + part
        total = jnp.sum(total, axis=1, keepdims=True)
        value = kv[:, pl.ds(pl.multiple_of(width + j * LANES, LANES), LANES)]
        both = dot_nn(p_ref[...], value) / total
        o2[:, pl.ds(at, LANES)] = unstack_heads(both, first).astype(BF)
        sums[...] = jnp.where(lane == j, peak + jnp.log(total), sums[...])
        return carry

    lax.fori_loop(0, PAIRS, one_pair, 0)


def feed_forward(
    rep_ref, o2, tok_h1, sums, w_co, w_up, w_down, b_up, b_down, vec, cot,
    layer_out, dr2, do2, both_sums, turned_sums, small, small_up,
    full_rows, xg0, xg1, xg2, xg3, xa0, xa1, xa2, xa3,
    slope, acts, dus,
):
    width = o2.shape[1]
    rows = o2.shape[0]
    hidden = w_up.shape[1]
    quarter = hidden // 4
    rep = rep_ref[0]
    gain2, shift2, gain3, shift3 = (vec[i : i + 1, :].astype(F32) for i in range(4))
    res2 = tok_h1[...].astype(F32) + dot_nn(o2[...], w_co[...])
    hat2, inv2 = norm_parts(res2)
    h2 = (hat2 * gain2 + shift2).astype(BF)
    full_rows[0:width, :] = h2.T
    full_rows[width : 2 * width, :] = o2[...].T
    total = None
    for c in range(4):
        cols = slice(c * quarter, (c + 1) * quarter)
        u = dot_nn(h2, w_up[:, cols]) + b_up[:, cols].astype(F32)
        cdf = 0.5 + 0.5 * lax.erf(u * 0.7071067811865476)
        act = (u * cdf).astype(BF)
        slope[:, cols] = cdf + u * (jnp.exp(u * u * -0.5) * 0.3989422804014327)
        acts[cols, :] = act.T
        part = dot_nn(act, w_down[cols, :])
        total = part if total is None else total + part
    res3 = h2.astype(F32) + total + b_down[...].astype(F32)
    hat3, inv3 = norm_parts(res3)
    layer_out[...] = (hat3 * gain3 + shift3).astype(BF)
    dr3, d_gain3, d_shift3 = norm_pull(cot[...].astype(F32), hat3, inv3, gain3)
    dy3 = dr3.astype(BF)
    small[0:1, :] = jnp.sum(dy3.astype(F32), axis=0, keepdims=True)
    small[3:4, :] = d_gain3
    small[4:5, :] = d_shift3
    back = None
    for c in range(4):
        cols = slice(c * quarter, (c + 1) * quarter)
        du = (dot_nt(dy3, w_down[cols, :]) * slope[:, cols]).astype(BF)
        small_up[:, cols] = jnp.sum(du.astype(F32), axis=0, keepdims=True)
        dus[c] = du
        part = dot_nt(du, w_up[:, cols])
        back = part if back is None else back + part
    grad2, d_gain2, d_shift2 = norm_pull(dr3 + back, hat2, inv2, gain2)
    small[1:2, :] = d_gain2
    small[2:3, :] = d_shift2
    small[5:8, :] = jnp.zeros((3, width), F32)
    dr2[...] = grad2
    dy2 = grad2.astype(BF)
    grad_mixed = dot_nt(dy2, w_co[...]).astype(BF)
    do2[...] = grad_mixed
    lane = lax.broadcasted_iota(jnp.int32, (2 * rows, LANES), 1)
    first = head_masks(rows)
    packed = sums[...]
    for j in range(PAIRS):
        at = slice(j * LANES, (j + 1) * LANES)
        prod = grad_mixed[:, at].astype(F32) * o2[:, at].astype(F32)
        zero = jnp.zeros_like(prod)
        two = jnp.concatenate([jnp.where(first, prod, zero), jnp.where(first, zero, prod)], axis=0)
        packed = jnp.where(lane == 8 + j, jnp.sum(two, axis=1, keepdims=True), packed)
    both_sums[...] = packed
    turned_sums[...] = packed.T[0:16, :]
    share = width // 4
    dy2_of = [dy2[:, i * share : (i + 1) * share] for i in range(4)]
    acts_rows = width // 8
    for k, (xg, xa) in enumerate(((xg0, xa0), (xg1, xa1), (xg2, xa2), (xg3, xa3))):
        peer = rep ^ k
        xg[:, 0:quarter] = dus[peer]
        piece = dy2_of[0]
        for i in range(1, 4):
            piece = jnp.where(peer == i, dy2_of[i], piece)
        xg[:, quarter : quarter + share] = piece
        for s in range(8):
            row = pl.multiple_of(s * 4 * acts_rows + peer * acts_rows, acts_rows)
            xa[s * acts_rows : (s + 1) * acts_rows, :] = acts[pl.ds(row, acts_rows), :]
    full_rows[2 * width : 3 * width, :] = dy3.T


def cross_self_backward(
    rep_ref, qc, do2, kv, parcels, sums, dr2, r1, joined, w_q, w_out, w_in, gain,
    d_tok, small, yq0, yq1, yq2, yq3, za0, za1, za2, za3,
    bias_ref, dqc_ref, da_ref, quarters,
):
    width = qc.shape[1]
    rows = qc.shape[0]
    sources = parcels.shape[0]
    span = 2 * BLK
    rep = rep_ref[0]
    first = head_masks(rows)
    for k in range(sources):
        for c in range(2):
            flag = parcels[k, span : span + 16, c * (width // 2) : c * (width // 2) + BLK]
            bias_ref[:, k * span + c * BLK : k * span + (c + 1) * BLK] = jnp.where(
                flag[0:8].astype(F32) > 0.5, 0.0, -1e30
            )
    lane = lax.broadcasted_iota(jnp.int32, (2 * rows, LANES), 1)

    def one_pair(j, carry):
        at = pl.multiple_of(j * LANES, LANES)
        q2 = stack_heads(qc[:, pl.ds(at, LANES)], first, FACTOR)
        g2 = stack_heads(do2[:, pl.ds(at, LANES)], first, 1.0)
        packed = sums[...]
        log_sum = jnp.sum(jnp.where(lane == j, packed, 0.0), axis=1, keepdims=True)
        delta = jnp.sum(jnp.where(lane == j + 8, packed, 0.0), axis=1, keepdims=True)
        total = None
        for k in range(sources):
            key = kv[k * span : (k + 1) * span, pl.ds(at, LANES)]
            value = kv[
                k * span : (k + 1) * span, pl.ds(pl.multiple_of(width + j * LANES, LANES), LANES)
            ]
            scores = dot_nt(q2, key) + bias_ref[0:1, k * span : (k + 1) * span]
            prob = jnp.exp(scores - log_sum)
            grad = (prob * (dot_nt(g2, value) - delta)).astype(BF)
            part = dot_nn(grad, key)
            total = part if total is None else total + part
        dqc_ref[:, pl.ds(at, LANES)] = (unstack_heads(total, first) * FACTOR).astype(BF)
        return carry

    lax.fori_loop(0, PAIRS, one_pair, 0)
    dqc = dqc_ref[...]
    grad1 = dr2[...] + dot_nt(dqc, w_q[...])
    hat1, inv1 = norm_parts(r1[...])
    dr1, d_gain1, d_shift1 = norm_pull(grad1, hat1, inv1, gain[...].astype(F32))
    small[0:1, :] = d_gain1
    small[1:2, :] = d_shift1
    small[2:8, :] = jnp.zeros((6, width), F32)
    dy1 = dr1.astype(BF)
    do1 = dot_nt(dy1, w_out[...]).astype(BF)
    for j in range(PAIRS):
        at = slice(j * LANES, (j + 1) * LANES)
        key_at = slice(width + j * LANES, width + (j + 1) * LANES)
        value_at = slice(2 * width + j * LANES, 2 * width + (j + 1) * LANES)
        q2 = stack_heads(joined[:, at], first, FACTOR)
        g2 = stack_heads(do1[:, at], first, 1.0)
        key, value = joined[:, key_at], joined[:, value_at]
        scores = dot_nt(q2, key)
        power = jnp.exp(scores - jnp.max(scores, axis=1, keepdims=True))
        prob = power / jnp.sum(power, axis=1, keepdims=True)
        d_prob = dot_nt(g2, value)
        d_scores = (prob * (d_prob - jnp.sum(d_prob * prob, axis=1, keepdims=True))).astype(BF)
        da_ref[:, at] = (unstack_heads(dot_nn(d_scores, key), first) * FACTOR).astype(BF)
        da_ref[:, key_at] = product_left(d_scores, q2).astype(BF)
        da_ref[:, value_at] = product_left(prob.astype(BF), g2).astype(BF)
    d_tok[...] = dr1 + dot_nt(da_ref[...], w_in[...])
    third = 3 * width // 4
    share = width // 4
    da = da_ref[...]
    for i in range(4):
        quarters[i, :, 0:third] = da[:, i * third : (i + 1) * third]
        quarters[i, :, third : third + share] = dy1[:, i * share : (i + 1) * share]
        quarters[i, :, width : width + share] = dqc[:, i * share : (i + 1) * share]
    for k, (yq, za) in enumerate(((yq0, za0), (yq1, za1), (yq2, za2), (yq3, za3))):
        yq[...] = quarters[rep ^ k, :, width : width + share]
        za[...] = quarters[rep ^ k, :, 0:width]


def owner_backward(where_ref, *refs):
    groups = 8
    qc, do2, sums = refs[0:groups], refs[groups : 2 * groups], refs[2 * groups : 3 * groups]
    kv, dkv, q_ref, g_ref, sum_ref = refs[3 * groups :]
    rows, width = qc[0].shape
    first = head_masks(rows)
    for k in range(groups):
        sum_ref[k] = sums[k][...]
        for j in range(PAIRS):
            at = slice(j * LANES, (j + 1) * LANES)
            q_ref[k, j] = stack_heads(qc[k][:, at], first, FACTOR)
            g_ref[k, j] = stack_heads(do2[k][:, at], first, 1.0)
    blocks = kv.shape[0] // BLK

    def one_block(b, carry):
        group = where_ref[b]
        row = pl.multiple_of(b * BLK, BLK)

        for j in range(PAIRS):
            key_at = slice(j * LANES, (j + 1) * LANES)
            value_at = slice(width + j * LANES, width + (j + 1) * LANES)
            key = kv[pl.ds(row, BLK), key_at]
            value = kv[pl.ds(row, BLK), value_at]
            q2 = q_ref[group, j]
            g2 = g_ref[group, j]
            log_sum = sum_ref[group, j : j + 1, :]
            delta = sum_ref[group, 8 + j : 9 + j, :]
            prob = jnp.exp(dot_nt(key, q2) - log_sum)
            grad = (prob * (dot_nt(value, g2) - delta)).astype(BF)
            dkv[pl.ds(row, BLK), key_at] = dot_nn(grad, q2).astype(BF)
            dkv[pl.ds(row, BLK), value_at] = dot_nn(prob.astype(BF), g2).astype(BF)
        return carry

    lax.fori_loop(0, blocks, one_block, 0)


def weight_blocks(plan, y_ref, *refs):
    send, keep, left_all, right_all = refs[-4:]
    arrays = refs[:-4]
    y = y_ref[0]
    tall = send.shape[1]
    width = left_all.shape[0]
    for lefts, row, rights, col, cols, to in plan:
        for k, (a, g) in enumerate(zip(lefts, rights)):
            rows = arrays[g].shape[0]
            left_all[:, k * rows : (k + 1) * rows] = arrays[a][row : row + width, :]
            right_all[k * rows : (k + 1) * rows, 0:cols] = arrays[g][:, col : col + cols]
        right = right_all[:, 0:cols]
        for z in range(4):
            for out, bit in ((send, 1 - y), (keep, y)):
                at = pl.multiple_of((2 * z + bit) * tall, 16)
                out[z, :, to : to + cols] = dot_nn(left_all[pl.ds(at, tall), :], right).astype(BF)


def fast_on_device(
    queries, memory, routes, w_self, w_self_out, w_cross_q, w_cross_kv, w_cross_out, w_up, b_up,
    w_down, b_down, gain_one, shift_one, gain_two, shift_two, gain_three, shift_three, cotangent,
):
    streams, reps = lax.axis_size("stream"), lax.axis_size("rep")
    me, rep = lax.axis_index("stream"), lax.axis_index("rep")
    width = w_self_out.shape[0]
    hidden = w_up.shape[1]
    tokens = queries[0]
    rows = tokens.shape[0]
    memory_rows = memory[0]
    y_bit, z_low, z_high = me % 2, (me // 2) % 2, me // 4
    rep_scalar = rep.reshape(1).astype(jnp.int32)
    y_scalar = y_bit.reshape(1).astype(jnp.int32)

    def hop(array, stream_flip=0, rep_flip=0):
        pairs = [
            (s * reps + r, (s ^ stream_flip) * reps + (r ^ rep_flip))
            for s in range(streams)
            for r in range(reps)
        ]
        return lax.ppermute(array, AXES, pairs)

    def rep_full(array):
        far = hop(array, 0, 2)
        return [array, hop(array, 0, 1), far, hop(far, 0, 1)]

    def rep_each(parts):
        return [parts[0]] + [hop(parts[k], 0, k) for k in range(1, 4)]

    def stream_full(array):
        along = [array] + [hop(array, k) for k in (2, 4, 6)]
        across = [hop(part, 1) for part in along]
        return [along[k // 2] if k % 2 == 0 else across[k // 2] for k in range(8)]

    def scatter(send, keep):
        tall, wide = send.shape[1:]
        got = hop(send, 1)
        total = (keep.astype(F32) + got.astype(F32)).astype(BF).reshape(2, 2, tall, wide)
        give = lax.dynamic_index_in_dim(total, 1 - z_low, 1, keepdims=False)
        mine = lax.dynamic_index_in_dim(total, z_low, 1, keepdims=False)
        got = hop(give, 2)
        total = (mine.astype(F32) + got.astype(F32)).astype(BF)
        give = lax.dynamic_index_in_dim(total, 1 - z_high, 0, keepdims=False)
        mine = lax.dynamic_index_in_dim(total, z_high, 0, keepdims=False)
        got = hop(give, 4)
        return (mine.astype(F32) + got.astype(F32)).astype(BF)

    def gather_quarters(piece):
        pieces = jnp.stack(rep_full(piece))
        order = jnp.arange(4, dtype=jnp.int32) ^ rep
        return jnp.take(pieces, order, axis=0).astype(F32)

    (parcels_out,) = local_kernel(
        deal_blocks,
        [like((streams, 2 * BLK + 16, width), BF)],
        scalars=[routes],
        arrays=[memory_rows],
    )
    parcels = lax.all_to_all(parcels_out, "stream", split_axis=0, concat_axis=0, tiled=True)

    row_of = lambda v: v.reshape(1, -1)
    joined, r1, qc, turned1 = local_kernel(
        self_forward,
        [
            like((rows, 3 * width), BF),
            like((rows, width), F32),
            like((rows, width), BF),
            like((3 * width, rows), BF),
        ],
        arrays=[tokens, w_self, w_self_out, w_cross_q, row_of(gain_one), row_of(shift_one)],
        flops=2 * rows * width * width * 5,
    )
    early = rep_full(turned1)
    h1 = turned1[2 * width :, :].T
    kv_own = matmul(memory_rows, w_cross_kv).astype(BF)

    keys = streams * 2 * BLK
    o2, kv, sums = local_kernel(
        cross_forward,
        [like((rows, width), BF), like((keys, 2 * width), BF), like((2 * rows, LANES), F32)],
        arrays=[qc, parcels, w_cross_kv],
        scratch=[
            pltpu.VMEM((2 * rows, keys), F32),
            pltpu.VMEM((2 * rows, keys), BF),
            pltpu.VMEM((8, keys), F32),
        ],
        flops=2 * keys * width * width * 2,
    )
    qc_all = stream_full(lax.optimization_barrier((qc, parcels))[0])

    vec = jnp.concatenate([row_of(v) for v in (gain_two, shift_two, gain_three, shift_three)])
    share = width // 4
    results = local_kernel(
        feed_forward,
        [
            like((rows, width), BF),
            like((rows, width), F32),
            like((rows, width), BF),
            like((2 * rows, LANES), F32),
            like((16, 2 * rows), F32),
            like((8, width), F32),
            like((1, hidden), F32),
            like((3 * width, rows), BF),
        ]
        + [like((rows, hidden // 4 + share), BF)] * 4
        + [like((hidden // 4, rows), BF)] * 4,
        scalars=[rep_scalar],
        arrays=[
            o2, h1, sums, w_cross_out, w_up, w_down, row_of(b_up), row_of(b_down), vec,
            cotangent[0],
        ],
        scratch=[
            pltpu.VMEM((rows, hidden), F32),
            pltpu.VMEM((hidden, rows), BF),
            pltpu.VMEM((4, rows, hidden // 4), BF),
        ],
        flops=2 * rows * width * (4 * hidden + 2 * width),
    )
    layer_out, dr2, do2, sums2, turned_sums, small_ff, small_up, full_rows = results[:8]
    xg, xa = results[8:12], results[12:16]
    do2_all = stream_full(do2)
    sums_all = stream_full(turned_sums)
    full_all = rep_full(full_rows)
    xg_all = rep_each(xg)
    xa_all = rep_each(xa)

    def blocks_of(plan, arrays, wide):
        return local_kernel(
            functools.partial(weight_blocks, plan),
            [like((4, width // streams, wide), BF)] * 2,
            scalars=[y_scalar],
            arrays=arrays,
            scratch=[pltpu.VMEM((width, 4 * rows), BF), pltpu.VMEM((4 * rows, width), BF)],
            flops=2 * 4 * rows * width * wide,
        )

    dy3_all = [part[2 * width :, :].T for part in full_all]
    ff_send, ff_keep = blocks_of(
        [
            ((0, 1, 2, 3), 0, (8, 9, 10, 11), 0, hidden // 4, 0),
            ((4, 5, 6, 7), 0, (12, 13, 14, 15), 0, width, hidden // 4),
        ],
        full_all + xa_all + xg_all + dy3_all,
        hidden // 4 + width,
    )
    ff_piece = scatter(ff_send, ff_keep)

    d_tokens, small_self, *exports = local_kernel(
        cross_self_backward,
        [like((rows, width), F32), like((8, width), F32)]
        + [like((rows, share), BF)] * 4
        + [like((rows, width), BF)] * 4,
        scalars=[rep_scalar],
        arrays=[
            qc, do2, kv, parcels, sums2, dr2, r1, joined, w_cross_q, w_self_out, w_self,
            row_of(gain_one),
        ],
        scratch=[
            pltpu.VMEM((8, keys), F32),
            pltpu.VMEM((rows, width), BF),
            pltpu.VMEM((rows, 3 * width), BF),
            pltpu.VMEM((4, rows, width + share), BF),
        ],
        flops=2 * rows * width * (5 * width + 6 * keys),
    )
    dqc_all = rep_each(exports[:4])
    da_all = rep_each(exports[4:])

    where = (routes[0] ^ me).astype(jnp.int32)
    (dkv,) = local_kernel(
        owner_backward,
        [like((memory_rows.shape[0], 2 * width), BF)],
        scalars=[where],
        arrays=qc_all + do2_all + sums_all + [kv_own],
        scratch=[
            pltpu.VMEM((streams, PAIRS, 2 * rows, LANES), BF),
            pltpu.VMEM((streams, PAIRS, 2 * rows, LANES), BF),
            pltpu.VMEM((streams, 16, 2 * rows), F32),
        ],
        flops=2 * memory_rows.shape[0] * rows * 8 * width,
    )
    d_memory = product_right(dkv, w_cross_kv).astype(BF)

    kv_wide = 2 * width // 4
    d_kv = product_left(memory_rows, dkv).astype(BF).reshape(width, 4, kv_wide)
    order = jnp.arange(4, dtype=jnp.int32) ^ rep
    d_kv = jnp.take(d_kv, order, axis=1).transpose(1, 0, 2)
    got = hop(jnp.stack([d_kv[1], d_kv[3]]), 0, 1)
    near = d_kv[0].astype(F32) + got[0].astype(F32)
    far = (d_kv[2].astype(F32) + got[1].astype(F32)).astype(BF)
    mine = (near + hop(far, 0, 2).astype(F32)).astype(BF)
    mine = mine.reshape(4, 2, width // streams, kv_wide)
    kv_keep = lax.dynamic_index_in_dim(mine, y_bit, 1, keepdims=False)
    kv_send = lax.dynamic_index_in_dim(mine, 1 - y_bit, 1, keepdims=False)
    kv_piece = scatter(kv_send, kv_keep)

    rest_send, rest_keep = blocks_of(
        [
            ((0, 1, 2, 3), 0, (12, 13, 14, 15), 0, 3 * share, 0),
            ((0, 1, 2, 3), width, (12, 13, 14, 15), 3 * share, share, 3 * share),
            ((0, 1, 2, 3), 2 * width, (8, 9, 10, 11), 0, share, 4 * share),
            ((4, 5, 6, 7), width, (16, 17, 18, 19), hidden // 4, share, 5 * share),
        ],
        early + full_all + dqc_all + da_all + xg_all,
        6 * share,
    )
    rest_piece = scatter(rest_send, rest_keep)

    ff_quarters = gather_quarters(ff_piece)
    kv_quarters = gather_quarters(kv_piece)
    rest_quarters = gather_quarters(rest_piece)

    def columns(quarters, start, wide):
        return quarters[:, :, start : start + wide].transpose(1, 0, 2).reshape(-1, 4 * wide)

    small = jnp.concatenate([small_ff[0:5], small_self[0:2], small_up.reshape(4, width)])
    small = lax.psum(small, AXES)
    tall = width // streams
    piece = lambda row: lax.dynamic_slice_in_dim(small[row], me * tall, tall, 0)
    d_b_up = lax.dynamic_slice_in_dim(
        small[7:11].reshape(-1), me * (hidden // streams), hidden // streams, 0
    )
    return (
        layer_out[None],
        d_tokens[None],
        d_memory[None],
        columns(rest_quarters, 0, 3 * share),
        columns(rest_quarters, 3 * share, share),
        columns(rest_quarters, 4 * share, share),
        columns(kv_quarters, 0, kv_wide),
        columns(rest_quarters, 5 * share, share),
        columns(ff_quarters, 0, hidden // 4),
        d_b_up,
        ff_quarters[:, :, hidden // 4 :].reshape(-1, width),
        piece(0),
        piece(5),
        piece(6),
        piece(1),
        piece(2),
        piece(3),
        piece(4),
    )


def solution(mesh):
    in_specs = (
        P("rep", "stream", None),
        P("rep", "stream", None),
        P("rep", "stream"),
        P(),
        P(),
        P(),
        P(),
        P(),
        P(),
        P(),
        P(),
        P(),
        P(),
        P(),
        P(),
        P(),
        P(),
        P(),
        P("rep", "stream", None),
    )
    out_specs = (
        P("rep", "stream", None),
        P("rep", "stream", None),
        P("rep", "stream", None),
        P("stream", None),
        P("stream", None),
        P("stream", None),
        P("stream", None),
        P("stream", None),
        P("stream", None),
        P("stream"),
        P("stream", None),
        P("stream"),
        P("stream"),
        P("stream"),
        P("stream"),
        P("stream"),
        P("stream"),
        P("stream"),
    )
    small_slice = (mesh.shape["stream"], mesh.shape["rep"]) == (8, 4)
    return jax.shard_map(
        fast_on_device if small_slice else on_device, mesh=mesh, in_specs=in_specs, out_specs=out_specs, check_vma=False
    )
```

```python
import functools

import jax
import jax.numpy as jnp
from jax import lax
from jax.experimental import pallas as pl
from jax.experimental.pallas import tpu as pltpu
from jax.sharding import PartitionSpec as P

HEADS = 12
HEAD_DIM = 64
BLK = 128


def matmul(left, right):
    return jnp.dot(left, right, preferred_element_type=jnp.float32)


def product_left(left, right):
    return lax.dot_general(
        left, right, (((0,), (0,)), ((), ())), preferred_element_type=jnp.float32
    )


def product_right(left, right):
    return lax.dot_general(
        left, right, (((1,), (1,)), ((), ())), preferred_element_type=jnp.float32
    )


def layer_norm(rows, gain, shift):
    centred = rows - jnp.mean(rows, axis=-1, keepdims=True)
    spread = jnp.mean(centred * centred, axis=-1, keepdims=True)
    return centred * lax.rsqrt(spread + 1e-05) * gain + shift


def split_heads(rows):
    return rows.reshape(rows.shape[0], HEADS, HEAD_DIM).transpose(1, 0, 2)


def join_heads(rows):
    return rows.transpose(1, 0, 2).reshape(rows.shape[1], HEADS * HEAD_DIM)


def masked_scores(query_head, key_head, key_ok):
    scores = product_right(query_head, key_head) * HEAD_DIM ** (-0.5)
    if key_ok is not None:
        scores = jnp.where(key_ok[None, :], scores, -1e30)
    return scores


def attend_forward(query, key_rows, value_rows, key_ok):

    def one_head(item):
        query_head, key_head, value_head = item
        scores = masked_scores(query_head, key_head, key_ok)
        row_max = jnp.max(scores, axis=1, keepdims=True)
        exponent = jnp.exp(scores - row_max)
        row_total = jnp.sum(exponent, axis=1, keepdims=True)
        probability = (exponent / row_total).astype(jnp.bfloat16)
        return (matmul(probability, value_head), (row_max + jnp.log(row_total))[:, 0])

    mixed, log_total = lax.map(
        one_head, (split_heads(query), split_heads(key_rows), split_heads(value_rows))
    )
    return (join_heads(mixed), log_total)


def attend_backward(query, key_rows, value_rows, key_ok, log_total, d_mixed):
    factor = HEAD_DIM ** (-0.5)

    def one_head(item):
        query_head, key_head, value_head, total_head, grad_head = item
        scores = masked_scores(query_head, key_head, key_ok)
        probability = jnp.exp(scores - total_head[:, None])
        d_prob = product_right(grad_head, value_head)
        d_scores = probability * (d_prob - jnp.sum(d_prob * probability, axis=1, keepdims=True))
        d_scores = d_scores.astype(jnp.bfloat16)
        d_query = matmul(d_scores, key_head) * factor
        d_key = product_left(d_scores, query_head) * factor
        d_value = product_left(probability.astype(jnp.bfloat16), grad_head)
        return (d_query, d_key, d_value)

    d_query, d_key, d_value = lax.map(
        one_head,
        (
            split_heads(query),
            split_heads(key_rows),
            split_heads(value_rows),
            log_total,
            split_heads(d_mixed),
        ),
    )
    return (join_heads(d_query), join_heads(d_key), join_heads(d_value))


def on_device(
    queries,
    memory,
    routes,
    w_self,
    w_self_out,
    w_cross_q,
    w_cross_kv,
    w_cross_out,
    w_up,
    b_up,
    w_down,
    b_down,
    gain_one,
    shift_one,
    gain_two,
    shift_two,
    gain_three,
    shift_three,
    cotangent,
):
    streams = lax.axis_size("stream")
    blocks = routes.shape[1]
    capacity = max(2, 2 * blocks // streams)
    slot_count = streams * capacity
    model_width = w_self_out.shape[0]
    target = routes[0]
    hit_table = (target[:, None] == jnp.arange(streams, dtype=jnp.int32)[None, :]).astype(jnp.int32)
    before = jnp.cumsum(hit_table, axis=0) - hit_table
    rank_in = jnp.sum(before * hit_table, axis=1)
    slot_of_block = target * capacity + rank_in
    matched = (slot_of_block[None, :] == jnp.arange(slot_count, dtype=jnp.int32)[:, None]).astype(
        jnp.int32
    )
    block_at = jnp.sum(matched * jnp.arange(blocks, dtype=jnp.int32)[None, :], axis=1)
    live_slot = jnp.sum(matched, axis=1)
    live_grid = live_slot.reshape(streams, capacity)
    filled = (live_slot > 0)[:, None, None]
    nothing = jnp.zeros((), jnp.bfloat16)
    memory_rows = memory[0]
    projected = (
        matmul(memory_rows, w_cross_kv).astype(jnp.bfloat16).reshape(blocks, BLK, 2 * model_width)
    )
    outgoing = jnp.where(filled, jnp.take(projected, block_at, axis=0), nothing)
    arrived, arrived_live = (
        lax.all_to_all(
            outgoing.reshape(streams, capacity, BLK, 2 * model_width),
            "stream",
            split_axis=0,
            concat_axis=0,
            tiled=True,
        ),
        lax.all_to_all(live_grid, "stream", split_axis=0, concat_axis=0, tiled=True),
    )
    keys_values = arrived.reshape(-1, 2 * model_width)
    key_ok = jnp.repeat(arrived_live.reshape(-1), BLK) > 0
    key_cross = keys_values[:, :model_width]
    value_cross = keys_values[:, model_width:]
    gain_a = gain_one.astype(jnp.float32)
    shift_a = shift_one.astype(jnp.float32)
    gain_b = gain_two.astype(jnp.float32)
    shift_b = shift_two.astype(jnp.float32)
    gain_c = gain_three.astype(jnp.float32)
    shift_c = shift_three.astype(jnp.float32)
    tokens = queries[0]
    joined = matmul(tokens, w_self).astype(jnp.bfloat16)
    query_self = joined[:, :model_width]
    key_self = joined[:, model_width : 2 * model_width]
    value_self = joined[:, 2 * model_width :]
    mixed_self, total_self = attend_forward(query_self, key_self, value_self, None)
    mixed_self = mixed_self.astype(jnp.bfloat16)
    residual_one = tokens.astype(jnp.float32) + matmul(mixed_self, w_self_out)
    normed_one = layer_norm(residual_one, gain_a, shift_a).astype(jnp.bfloat16)
    query_cross = matmul(normed_one, w_cross_q).astype(jnp.bfloat16)
    mixed_cross, total_cross = attend_forward(query_cross, key_cross, value_cross, key_ok)
    mixed_cross = mixed_cross.astype(jnp.bfloat16)
    residual_two = normed_one.astype(jnp.float32) + matmul(mixed_cross, w_cross_out)
    normed_two = layer_norm(residual_two, gain_b, shift_b).astype(jnp.bfloat16)
    hidden_pre = matmul(normed_two, w_up) + b_up.astype(jnp.float32)
    hidden = jax.nn.gelu(hidden_pre, approximate=False).astype(jnp.bfloat16)
    residual_three = (
        normed_two.astype(jnp.float32) + matmul(hidden, w_down) + b_down.astype(jnp.float32)
    )
    layer_out = layer_norm(residual_three, gain_c, shift_c).astype(jnp.bfloat16)
    grad_out = cotangent[0].astype(jnp.float32)
    norm_three_pull = jax.vjp(layer_norm, residual_three, gain_c, shift_c)[1]
    d_residual_three, d_gain_c, d_shift_c = norm_three_pull(grad_out)
    d_branch_three = d_residual_three.astype(jnp.bfloat16)
    d_b_down = jnp.sum(d_branch_three.astype(jnp.float32), axis=0)
    d_w_down = product_left(hidden, d_branch_three)
    d_hidden = product_right(d_branch_three, w_down)
    gelu_pull = jax.vjp(lambda value: jax.nn.gelu(value, approximate=False), hidden_pre)[1]
    d_hidden_pre = gelu_pull(d_hidden)[0].astype(jnp.bfloat16)
    d_b_up = jnp.sum(d_hidden_pre.astype(jnp.float32), axis=0)
    d_w_up = product_left(normed_two, d_hidden_pre)
    d_normed_two = d_residual_three + product_right(d_hidden_pre, w_up)
    norm_two_pull = jax.vjp(layer_norm, residual_two, gain_b, shift_b)[1]
    d_residual_two, d_gain_b, d_shift_b = norm_two_pull(d_normed_two)
    d_branch_two = d_residual_two.astype(jnp.bfloat16)
    d_w_cross_out = product_left(mixed_cross, d_branch_two)
    d_mixed_cross = product_right(d_branch_two, w_cross_out).astype(jnp.bfloat16)
    d_query_cross, d_key_cross, d_value_cross = attend_backward(
        query_cross, key_cross, value_cross, key_ok, total_cross, d_mixed_cross
    )
    d_query_cross = d_query_cross.astype(jnp.bfloat16)
    d_keys_values = jnp.concatenate([d_key_cross, d_value_cross], axis=1).astype(jnp.bfloat16)
    d_w_cross_q = product_left(normed_one, d_query_cross)
    d_normed_one = d_residual_two + product_right(d_query_cross, w_cross_q)
    norm_one_pull = jax.vjp(layer_norm, residual_one, gain_a, shift_a)[1]
    d_residual_one, d_gain_a, d_shift_a = norm_one_pull(d_normed_one)
    d_branch_one = d_residual_one.astype(jnp.bfloat16)
    d_w_self_out = product_left(mixed_self, d_branch_one)
    d_mixed_self = product_right(d_branch_one, w_self_out).astype(jnp.bfloat16)
    d_query_self, d_key_self, d_value_self = attend_backward(
        query_self, key_self, value_self, None, total_self, d_mixed_self
    )
    d_joined = jnp.concatenate([d_query_self, d_key_self, d_value_self], axis=1).astype(
        jnp.bfloat16
    )
    d_w_self = product_left(tokens, d_joined)
    d_tokens = d_residual_one + product_right(d_joined, w_self)
    returned = lax.all_to_all(
        d_keys_values.reshape(streams, capacity, BLK, 2 * model_width),
        "stream",
        split_axis=0,
        concat_axis=0,
        tiled=True,
    )
    d_block_rows = jnp.take(
        returned.reshape(slot_count, BLK, 2 * model_width), slot_of_block, axis=0
    ).reshape(-1, 2 * model_width)
    d_w_cross_kv = product_left(memory_rows, d_block_rows)
    d_memory = product_right(d_block_rows, w_cross_kv).astype(jnp.bfloat16)
    gradients = (
        d_w_self,
        d_w_self_out,
        d_w_cross_q,
        d_w_cross_kv,
        d_w_cross_out,
        d_w_up,
        d_b_up,
        d_w_down,
        d_b_down,
        d_gain_a,
        d_shift_a,
        d_gain_b,
        d_shift_b,
        d_gain_c,
        d_shift_c,
    )
    shapes = [item.shape for item in gradients]
    flat = [item.reshape(-1) for item in gradients]
    (
        share_self,
        share_self_out,
        share_cross_q,
        share_cross_kv,
        share_cross_out,
        share_up,
        share_b_up,
        share_down,
        share_b_down,
        share_gain_a,
        share_shift_a,
        share_gain_b,
        share_shift_b,
        share_gain_c,
        share_shift_c,
    ) = (
        lax.psum_scatter(flat[0], "stream", scatter_dimension=0, tiled=True),
        lax.psum_scatter(flat[1], "stream", scatter_dimension=0, tiled=True),
        lax.psum_scatter(flat[2], "stream", scatter_dimension=0, tiled=True),
        lax.psum_scatter(flat[3], "stream", scatter_dimension=0, tiled=True),
        lax.psum_scatter(flat[4], "stream", scatter_dimension=0, tiled=True),
        lax.psum_scatter(flat[5], "stream", scatter_dimension=0, tiled=True),
        lax.psum_scatter(flat[6], "stream", scatter_dimension=0, tiled=True),
        lax.psum_scatter(flat[7], "stream", scatter_dimension=0, tiled=True),
        lax.psum_scatter(flat[8], "stream", scatter_dimension=0, tiled=True),
        lax.psum_scatter(flat[9], "stream", scatter_dimension=0, tiled=True),
        lax.psum_scatter(flat[10], "stream", scatter_dimension=0, tiled=True),
        lax.psum_scatter(flat[11], "stream", scatter_dimension=0, tiled=True),
        lax.psum_scatter(flat[12], "stream", scatter_dimension=0, tiled=True),
        lax.psum_scatter(flat[13], "stream", scatter_dimension=0, tiled=True),
        lax.psum_scatter(flat[14], "stream", scatter_dimension=0, tiled=True),
    )
    summed = (
        lax.psum(share_self.astype(jnp.bfloat16), "rep").astype(jnp.float32),
        lax.psum(share_self_out.astype(jnp.bfloat16), "rep").astype(jnp.float32),
        lax.psum(share_cross_q.astype(jnp.bfloat16), "rep").astype(jnp.float32),
        lax.psum(share_cross_kv.astype(jnp.bfloat16), "rep").astype(jnp.float32),
        lax.psum(share_cross_out.astype(jnp.bfloat16), "rep").astype(jnp.float32),
        lax.psum(share_up.astype(jnp.bfloat16), "rep").astype(jnp.float32),
        lax.psum(share_b_up.astype(jnp.bfloat16), "rep").astype(jnp.float32),
        lax.psum(share_down.astype(jnp.bfloat16), "rep").astype(jnp.float32),
        lax.psum(share_b_down.astype(jnp.bfloat16), "rep").astype(jnp.float32),
        lax.psum(share_gain_a.astype(jnp.bfloat16), "rep").astype(jnp.float32),
        lax.psum(share_shift_a.astype(jnp.bfloat16), "rep").astype(jnp.float32),
        lax.psum(share_gain_b.astype(jnp.bfloat16), "rep").astype(jnp.float32),
        lax.psum(share_shift_b.astype(jnp.bfloat16), "rep").astype(jnp.float32),
        lax.psum(share_gain_c.astype(jnp.bfloat16), "rep").astype(jnp.float32),
        lax.psum(share_shift_c.astype(jnp.bfloat16), "rep").astype(jnp.float32),
    )
    results = [
        part.reshape((shape[0] // streams,) + tuple(shape[1:]))
        for part, shape in zip(summed, shapes)
    ]
    return (
        layer_out[None],
        d_tokens[None],
        d_memory[None],
        results[0],
        results[1],
        results[2],
        results[3],
        results[4],
        results[5],
        results[6],
        results[7],
        results[8],
        results[9],
        results[10],
        results[11],
        results[12],
        results[13],
        results[14],
    )


PAIRS = HEADS // 2
LANES = 2 * HEAD_DIM
FACTOR = HEAD_DIM ** (-0.5)
BF = jnp.bfloat16
F32 = jnp.float32
AXES = ("stream", "rep")


def whole_in_vmem(count):
    return [pl.BlockSpec(memory_space=pltpu.VMEM)] * count


def local_kernel(body, out_shape, scalars=(), arrays=(), scratch=(), cost=2, limit=52):
    return pl.pallas_call(
        body,
        out_shape=list(out_shape),
        in_specs=[pl.BlockSpec(memory_space=pltpu.SMEM)] * len(scalars) + whole_in_vmem(len(arrays)),
        out_specs=whole_in_vmem(len(out_shape)),
        scratch_shapes=list(scratch),
        compiler_params=pltpu.CompilerParams(vmem_limit_bytes=limit * 1024 * 1024),
        cost_estimate=pl.CostEstimate(
            flops=int(cost * 1.15e9), bytes_accessed=int(cost * 1e5), transcendentals=0
        ),
    )(*scalars, *arrays)


def like(shape, dtype):
    return jax.ShapeDtypeStruct(shape, dtype)


def dot_nn(left, right):
    return lax.dot_general(left, right, (((1,), (0,)), ((), ())), preferred_element_type=F32)


def dot_nt(left, right):
    return lax.dot_general(left, right, (((1,), (1,)), ((), ())), preferred_element_type=F32)


def head_masks(rows):
    lane = lax.broadcasted_iota(jnp.int32, (rows, LANES), 1)
    return lane < HEAD_DIM


def stack_heads(pair, first, scale):
    one = jnp.where(first, scale, 0.0).astype(BF)
    two = jnp.where(first, 0.0, scale).astype(BF)
    return jnp.concatenate([pair * one, pair * two], axis=0)


def unstack_heads(both, first):
    rows = both.shape[0] // 2
    return jnp.where(first, both[:rows], both[rows:])


def norm_parts(rows):
    centred = rows - jnp.mean(rows, axis=1, keepdims=True)
    spread = jnp.mean(centred * centred, axis=1, keepdims=True)
    inverse = lax.rsqrt(spread + 1e-05)
    return centred * inverse, inverse


def norm_pull(grad, hat, inverse, gain):
    scaled = grad * gain
    inner = scaled - jnp.mean(scaled, axis=1, keepdims=True)
    inner = inner - hat * jnp.mean(scaled * hat, axis=1, keepdims=True)
    return (
        inverse * inner,
        jnp.sum(grad * hat, axis=0, keepdims=True),
        jnp.sum(grad, axis=0, keepdims=True),
    )


def deal_blocks(routes_ref, memory_ref, out_ref):
    out_ref[...] = jnp.zeros_like(out_ref)
    blocks = memory_ref.shape[0] // BLK
    width = memory_ref.shape[1]
    for b in range(blocks):
        group = routes_ref[0, b]
        rank = jnp.int32(0)
        for earlier in range(b):
            rank = rank + (routes_ref[0, earlier] == group).astype(jnp.int32)
        row = pl.multiple_of(rank * BLK, BLK)
        lane = pl.multiple_of(rank * (width // 2), LANES)
        out_ref[group, pl.ds(row, BLK), :] = memory_ref[b * BLK : (b + 1) * BLK, :]
        out_ref[group, 2 * BLK : 2 * BLK + 16, pl.ds(lane, width // 2)] = jnp.ones(
            (16, width // 2), BF
        )


def self_forward(tok, w_in, w_out, w_q, gain, shift, joined, r1, h1_out, qc, turned):
    width = tok.shape[1]
    rows = tok.shape[0]
    joined[...] = dot_nn(tok[...], w_in[...]).astype(BF)
    first = head_masks(rows)
    mixed = []
    for j in range(PAIRS):
        at = j * LANES
        q2 = stack_heads(joined[:, at : at + LANES], first, FACTOR)
        key = joined[:, width + at : width + at + LANES]
        value = joined[:, 2 * width + at : 2 * width + at + LANES]
        scores = dot_nt(q2, key)
        power = jnp.exp(scores - jnp.max(scores, axis=1, keepdims=True))
        prob = (power / jnp.sum(power, axis=1, keepdims=True)).astype(BF)
        mixed.append(unstack_heads(dot_nn(prob, value), first).astype(BF))
    o1 = jnp.concatenate(mixed, axis=1)
    res = tok[...].astype(F32) + dot_nn(o1, w_out[...])
    r1[...] = res
    hat, _ = norm_parts(res)
    h1 = (hat * gain[...].astype(F32) + shift[...].astype(F32)).astype(BF)
    h1_out[...] = h1
    qc[...] = dot_nn(h1, w_q[...]).astype(BF)
    turned[0:width, :] = tok[...].T
    turned[width : 2 * width, :] = o1.T
    turned[2 * width : 3 * width, :] = h1.T


def cross_forward(qc, parcels, w_kv, o2, kv, sums, s_ref, p_ref, bias_ref):
    width = qc.shape[1]
    rows = qc.shape[0]
    sources = parcels.shape[0]
    span = 2 * BLK
    first = head_masks(rows)
    for k in range(sources):
        kv[k * span : (k + 1) * span, :] = dot_nn(parcels[k, 0:span, :], w_kv[...]).astype(BF)
        for c in range(2):
            flag = parcels[k, span : span + 16, c * (width // 2) : c * (width // 2) + BLK]
            bias_ref[:, k * span + c * BLK : k * span + (c + 1) * BLK] = jnp.where(
                flag[0:8].astype(F32) > 0.5, 0.0, -1e30
            )
    lane = lax.broadcasted_iota(jnp.int32, (2 * rows, LANES), 1)
    sums[...] = jnp.zeros_like(sums)

    def one_pair(j, carry):
        at = pl.multiple_of(j * LANES, LANES)
        q2 = stack_heads(qc[:, pl.ds(at, LANES)], first, FACTOR)
        top = None
        for k in range(sources):
            key = kv[k * span : (k + 1) * span, pl.ds(at, LANES)]
            scores = dot_nt(q2, key) + bias_ref[0:1, k * span : (k + 1) * span]
            s_ref[:, k * span : (k + 1) * span] = scores
            most = jnp.maximum(scores[:, :LANES], scores[:, LANES:])
            top = most if top is None else jnp.maximum(top, most)
        peak = jnp.max(top, axis=1, keepdims=True)
        total = None
        for k in range(sources):
            power = jnp.exp(s_ref[:, k * span : (k + 1) * span] - peak)
            p_ref[:, k * span : (k + 1) * span] = power.astype(BF)
            part = power[:, :LANES] + power[:, LANES:]
            total = part if total is None else total + part
        total = jnp.sum(total, axis=1, keepdims=True)
        value = kv[:, pl.ds(pl.multiple_of(width + j * LANES, LANES), LANES)]
        both = dot_nn(p_ref[...], value) / total
        o2[:, pl.ds(at, LANES)] = unstack_heads(both, first).astype(BF)
        sums[...] = jnp.where(lane == j, peak + jnp.log(total), sums[...])
        return carry

    lax.fori_loop(0, PAIRS, one_pair, 0)


def feed_forward(
    rep_ref, o2, tok_h1, sums, w_co, w_up, w_down, b_up, b_down, vec, cot,
    layer_out, dr2, do2, both_sums, small, small_up, parcel0, parcel1, parcel2, parcel3,
    slope, acts, dus,
):
    width = o2.shape[1]
    rows = o2.shape[0]
    hidden = w_up.shape[1]
    quarter = hidden // 4
    rep = rep_ref[0]
    gain2, shift2, gain3, shift3 = (vec[i : i + 1, :].astype(F32) for i in range(4))
    res2 = tok_h1[...].astype(F32) + dot_nn(o2[...], w_co[...])
    hat2, inv2 = norm_parts(res2)
    h2 = (hat2 * gain2 + shift2).astype(BF)
    for parcel in (parcel1, parcel2):
        parcel[0:width, :] = h2.T
        parcel[width : 2 * width, :] = o2[...].T
    total = None
    for c in range(4):
        cols = slice(c * quarter, (c + 1) * quarter)
        u = dot_nn(h2, w_up[:, cols]) + b_up[:, cols].astype(F32)
        cdf = 0.5 + 0.5 * lax.erf(u * 0.7071067811865476)
        act = (u * cdf).astype(BF)
        slope[:, cols] = cdf + u * (jnp.exp(u * u * -0.5) * 0.3989422804014327)
        acts[cols, :] = act.T
        part = dot_nn(act, w_down[cols, :])
        total = part if total is None else total + part
    res3 = h2.astype(F32) + total + b_down[...].astype(F32)
    hat3, inv3 = norm_parts(res3)
    layer_out[...] = (hat3 * gain3 + shift3).astype(BF)
    dr3, d_gain3, d_shift3 = norm_pull(cot[...].astype(F32), hat3, inv3, gain3)
    dy3 = dr3.astype(BF)
    small[0:1, :] = jnp.sum(dy3.astype(F32), axis=0, keepdims=True)
    small[3:4, :] = d_gain3
    small[4:5, :] = d_shift3
    back = None
    for c in range(4):
        cols = slice(c * quarter, (c + 1) * quarter)
        du = (dot_nt(dy3, w_down[cols, :]) * slope[:, cols]).astype(BF)
        small_up[:, cols] = jnp.sum(du.astype(F32), axis=0, keepdims=True)
        dus[cols, :] = du.T
        part = dot_nt(du, w_up[:, cols])
        back = part if back is None else back + part
    grad2, d_gain2, d_shift2 = norm_pull(dr3 + back, hat2, inv2, gain2)
    small[1:2, :] = d_gain2
    small[2:3, :] = d_shift2
    small[5:8, :] = jnp.zeros((3, width), F32)
    dr2[...] = grad2
    dy2 = grad2.astype(BF)
    grad_mixed = dot_nt(dy2, w_co[...]).astype(BF)
    do2[0:rows, :] = grad_mixed
    lane = lax.broadcasted_iota(jnp.int32, (2 * rows, LANES), 1)
    first = head_masks(rows)
    packed = sums[...]
    for j in range(PAIRS):
        at = slice(j * LANES, (j + 1) * LANES)
        prod = grad_mixed[:, at].astype(F32) * o2[:, at].astype(F32)
        zero = jnp.zeros_like(prod)
        two = jnp.concatenate([jnp.where(first, prod, zero), jnp.where(first, zero, prod)], axis=0)
        packed = jnp.where(lane == 8 + j, jnp.sum(two, axis=1, keepdims=True), packed)
    both_sums[...] = packed
    turned = packed.T[0:16, :]
    high = turned.astype(BF)
    rest = turned - high.astype(F32)
    middle = rest.astype(BF)
    low = (rest - middle.astype(F32)).astype(BF)
    do2[rows : rows + 16, :] = jnp.concatenate([high, middle, low], axis=1)
    share = width // 4
    dy2_turned = dy2.T
    dy3_turned = dy3.T
    strip = quarter // 8
    for k, parcel in enumerate((parcel0, parcel1, parcel2, parcel3)):
        peer = rep ^ k
        base = 0
        if k in (1, 2):
            parcel[2 * width : 3 * width, :] = dy3_turned
            base = 3 * width
        for s in range(8):
            row = pl.multiple_of(s * 4 * strip + peer * strip, strip)
            parcel[base + s * strip : base + (s + 1) * strip, :] = acts[pl.ds(row, strip), :]
        row = pl.multiple_of(peer * quarter, quarter)
        parcel[base + quarter : base + 2 * quarter, :] = dus[pl.ds(row, quarter), :]
        piece = dy2_turned[0:share]
        for i in range(1, 4):
            piece = jnp.where(peer == i, dy2_turned[i * share : (i + 1) * share], piece)
        parcel[base + 2 * quarter : base + 2 * quarter + share, :] = piece


def cross_backward(qc, do2, kv, parcels, sums, dqc, bias_ref):
    width = qc.shape[1]
    rows = qc.shape[0]
    sources = parcels.shape[0]
    span = 2 * BLK
    first = head_masks(rows)
    for k in range(sources):
        for c in range(2):
            flag = parcels[k, span : span + 16, c * (width // 2) : c * (width // 2) + BLK]
            bias_ref[:, k * span + c * BLK : k * span + (c + 1) * BLK] = jnp.where(
                flag[0:8].astype(F32) > 0.5, 0.0, -1e30
            )
    lane = lax.broadcasted_iota(jnp.int32, (2 * rows, LANES), 1)

    def one_pair(j, carry):
        at = pl.multiple_of(j * LANES, LANES)
        q2 = stack_heads(qc[:, pl.ds(at, LANES)], first, FACTOR)
        g2 = stack_heads(do2[0:rows, pl.ds(at, LANES)], first, 1.0)
        packed = sums[...]
        log_sum = jnp.sum(jnp.where(lane == j, packed, 0.0), axis=1, keepdims=True)
        delta = jnp.sum(jnp.where(lane == j + 8, packed, 0.0), axis=1, keepdims=True)
        total = None
        for k in range(sources):
            key = kv[k * span : (k + 1) * span, pl.ds(at, LANES)]
            value = kv[
                k * span : (k + 1) * span, pl.ds(pl.multiple_of(width + j * LANES, LANES), LANES)
            ]
            scores = dot_nt(q2, key) + bias_ref[0:1, k * span : (k + 1) * span]
            prob = jnp.exp(scores - log_sum)
            grad = (prob * (dot_nt(g2, value) - delta)).astype(BF)
            part = dot_nn(grad, key)
            total = part if total is None else total + part
        dqc[:, pl.ds(at, LANES)] = (unstack_heads(total, first) * FACTOR).astype(BF)
        return carry

    lax.fori_loop(0, PAIRS, one_pair, 0)


def self_backward(
    rep_ref, dqc_ref, dr2, r1, joined, w_q, w_out, w_in, gain,
    d_tok, small, out0, out1, out2, out3,
    da_ref, quarters,
):
    rows, width = dqc_ref.shape
    rep = rep_ref[0]
    first = head_masks(rows)
    dqc = dqc_ref[...]
    grad1 = dr2[...] + dot_nt(dqc, w_q[...])
    hat1, inv1 = norm_parts(r1[...])
    dr1, d_gain1, d_shift1 = norm_pull(grad1, hat1, inv1, gain[...].astype(F32))
    small[0:1, :] = d_gain1
    small[1:2, :] = d_shift1
    small[2:8, :] = jnp.zeros((6, width), F32)
    dy1 = dr1.astype(BF)
    do1 = dot_nt(dy1, w_out[...]).astype(BF)
    for j in range(PAIRS):
        at = slice(j * LANES, (j + 1) * LANES)
        key_at = slice(width + j * LANES, width + (j + 1) * LANES)
        value_at = slice(2 * width + j * LANES, 2 * width + (j + 1) * LANES)
        q2 = stack_heads(joined[:, at], first, FACTOR)
        g2 = stack_heads(do1[:, at], first, 1.0)
        key, value = joined[:, key_at], joined[:, value_at]
        scores = dot_nt(q2, key)
        power = jnp.exp(scores - jnp.max(scores, axis=1, keepdims=True))
        prob = power / jnp.sum(power, axis=1, keepdims=True)
        d_prob = dot_nt(g2, value)
        d_scores = (prob * (d_prob - jnp.sum(d_prob * prob, axis=1, keepdims=True))).astype(BF)
        da_ref[:, at] = (unstack_heads(dot_nn(d_scores, key), first) * FACTOR).astype(BF)
        da_ref[:, key_at] = product_left(d_scores, q2).astype(BF)
        da_ref[:, value_at] = product_left(prob.astype(BF), g2).astype(BF)
    d_tok[...] = dr1 + dot_nt(da_ref[...], w_in[...])
    third = 3 * width // 4
    share = width // 4
    da = da_ref[...]
    for i in range(4):
        quarters[i, :, 0:third] = da[:, i * third : (i + 1) * third]
        quarters[i, :, third : third + share] = dy1[:, i * share : (i + 1) * share]
        quarters[i, :, width : width + share] = dqc[:, i * share : (i + 1) * share]
    for k, out in enumerate((out0, out1, out2, out3)):
        out[...] = quarters[rep ^ k]


def owner_backward(where_ref, *refs):
    groups = 8
    qc_near, qc_far, do_near, do_far, kv, dkv, q_ref, g_ref, sum_ref = refs
    _, rows, width = qc_near.shape
    first = head_masks(rows)
    for k in range(groups):
        query = (qc_far if k % 2 else qc_near)[k // 2]
        extra = (do_far if k % 2 else do_near)[k // 2]
        sums = extra[rows : rows + 16, :].astype(F32)
        third = width // 3
        sum_ref[k] = sums[:, 0:third] + sums[:, third : 2 * third] + sums[:, 2 * third :]
        for j in range(PAIRS):
            at = slice(j * LANES, (j + 1) * LANES)
            q_ref[k, j] = stack_heads(query[:, at], first, FACTOR)
            g_ref[k, j] = stack_heads(extra[0:rows, at], first, 1.0)
    blocks = kv.shape[0] // BLK

    def one_block(b, carry):
        group = where_ref[b]
        row = pl.multiple_of(b * BLK, BLK)
        for j in range(PAIRS):
            key_at = slice(j * LANES, (j + 1) * LANES)
            value_at = slice(width + j * LANES, width + (j + 1) * LANES)
            key = kv[pl.ds(row, BLK), key_at]
            value = kv[pl.ds(row, BLK), value_at]
            q2 = q_ref[group, j]
            g2 = g_ref[group, j]
            log_sum = sum_ref[group, j : j + 1, :]
            delta = sum_ref[group, 8 + j : 9 + j, :]
            prob = jnp.exp(dot_nt(key, q2) - log_sum)
            grad = (prob * (dot_nt(value, g2) - delta)).astype(BF)
            dkv[pl.ds(row, BLK), key_at] = dot_nn(grad, q2).astype(BF)
            dkv[pl.ds(row, BLK), value_at] = dot_nn(prob.astype(BF), g2).astype(BF)
        return carry

    lax.fori_loop(0, blocks, one_block, 0)


def memory_weights(rep_ref, dkv, memory_turned, keep, send):
    quarter = dkv.shape[1] // 4
    rep = rep_ref[0]
    for k in range(4):
        at = pl.multiple_of((rep ^ k) * quarter, LANES)
        out = (keep, send)[k % 2]
        out[k // 2] = dot_nn(memory_turned[...], dkv[:, pl.ds(at, quarter)]).astype(BF)


def memory_backward(dkv, w_kv, d_memory):
    half = dkv.shape[0] // 2
    for i in range(2):
        span = slice(i * half, (i + 1) * half)
        d_memory[span, :] = dot_nt(dkv[span, :], w_kv[...]).astype(BF)


def own_keys(memory_ref, w_kv, kv, turned):
    kv[...] = dot_nn(memory_ref[...], w_kv[...]).astype(BF)
    turned[...] = memory_ref[...].T


def weight_blocks(plan, extra, bits_ref, *refs):
    outs, (left_all, right_all, product) = refs[-7:-3], refs[-3:]
    arrays = refs[:-7]
    width, depth = left_all.shape
    rows = depth // 4
    tall = width // 8

    def blocks_of(group):
        bit = bits_ref[group]
        for i in range(4):
            for out, b in ((outs[2 * group], 1 - bit), (outs[2 * group + 1], bit)):
                if group == 0:
                    yield out, i, 2 * i + b
                else:
                    yield out, i, 4 * (i // 2) + 2 * b + i % 2

    for lefts, rights, turned, cols, group, to in plan:
        for k, ((a, row), (g, off)) in enumerate(zip(lefts, rights)):
            span = slice(k * rows, (k + 1) * rows)
            left_all[:, span] = arrays[a][row : row + width, :]
            right = arrays[g][off : off + cols, :].T if turned else arrays[g][:, off : off + cols]
            right_all[span, 0:cols] = right
        product[:, 0:cols] = dot_nn(left_all[...], right_all[:, 0:cols])
        for out, i, block in blocks_of(group):
            at = pl.multiple_of(block * tall, 16)
            out[i, 0:tall, to : to + cols] = product[pl.ds(at, tall), 0:cols].astype(BF)
    if extra is not None:
        for group in range(2):
            for out, i, block in blocks_of(group):
                out[i, tall:, :] = jnp.zeros_like(out[i, tall:, :])
                if group == 0:
                    out[i, tall:, 0:LANES] = arrays[extra][block].astype(BF)


def fold_two(bits_ref, kept0, got0, kept1, got1, give0, mine0, give1, mine1):
    for bit, kept, got, give, mine in (
        (bits_ref[1], kept0, got0, give0, mine0),
        (bits_ref[0], kept1, got1, give1, mine1),
    ):
        for i in range(2):
            for out, at in ((give, 2 * i + 1 - bit), (mine, 2 * i + bit)):
                out[i] = (kept[at].astype(F32) + got[at].astype(F32)).astype(BF)


def fold_high(bits_ref, *refs):
    (give, mine), arrays = refs[-2:], refs[:-2]
    bit = bits_ref[2]
    for g in range(len(arrays) // 2):
        kept, got = arrays[2 * g], arrays[2 * g + 1]
        for out, at in ((give, 1 - bit), (mine, bit)):
            out[g] = (kept[at].astype(F32) + got[at].astype(F32)).astype(BF)


def fold_one(bits_ref, kept, got, give, mine):
    bit = bits_ref[1]
    for i in range(2):
        for out, at in ((give, 2 * i + 1 - bit), (mine, 2 * i + bit)):
            out[i] = (kept[at].astype(F32) + got[at].astype(F32)).astype(BF)


def fold_last(kept, got, out):
    out[...] = (kept[...].astype(F32) + got[...].astype(F32)).astype(BF)


def fold_core(kept, got, near, far):
    near[...] = kept[0].astype(F32) + got[0].astype(F32)
    far[...] = (kept[1].astype(F32) + got[1].astype(F32)).astype(BF)


def fold_rep(bits_ref, near, got, send, keep):
    y = bits_ref[0]
    tall = send.shape[1]
    for z in range(4):
        for out, bit in ((send, 1 - y), (keep, y)):
            at = pl.multiple_of((2 * z + bit) * tall, 16)
            out[z] = (near[pl.ds(at, tall), :] + got[pl.ds(at, tall), :].astype(F32)).astype(BF)


def lay_columns(plan, rep_ref, *refs):
    pieces, outs, held = refs[0:4], refs[4:-1], refs[-1]
    rep = rep_ref[0]
    for k in range(4):
        held[k] = pieces[k][...]
    for (group, start, cols, how), out in zip(plan, outs):
        if how == "sum":
            tall = out.shape[0]
            total = None
            for k in range(4):
                part = pieces[k][group, pieces[k].shape[1] - tall :, start : start + cols].astype(F32)
                total = part if total is None else total + part
            out[...] = total
            continue
        tall = out.shape[0] if how == "side" else out.shape[0] // 4
        for q in range(4):
            part = held[rep ^ q, group, 0:tall, start : start + cols].astype(F32)
            if how == "side":
                out[:, q * cols : (q + 1) * cols] = part
            else:
                out[q * tall : (q + 1) * tall, :] = part


def fast_on_device(
    queries, memory, routes, w_self, w_self_out, w_cross_q, w_cross_kv, w_cross_out, w_up, b_up,
    w_down, b_down, gain_one, shift_one, gain_two, shift_two, gain_three, shift_three, cotangent,
):
    streams, reps = lax.axis_size("stream"), lax.axis_size("rep")
    me, rep = lax.axis_index("stream"), lax.axis_index("rep")
    width = w_self_out.shape[0]
    hidden = w_up.shape[1]
    quarter, share, tall = hidden // 4, width // 4, width // streams
    tokens = queries[0]
    rows = tokens.shape[0]
    memory_rows = memory[0]
    rep_scalar = rep.reshape(1).astype(jnp.int32)
    bits = jnp.stack([me % 2, (me // 2) % 2, me // 4]).astype(jnp.int32)
    row_of = lambda v: v.reshape(1, -1)
    last = []

    def after(first, *others):
        return lax.optimization_barrier((first, others))[0]

    def run(body, outs, arrays, done=(), **more):
        held = last + list(done)
        if held:
            arrays = [after(arrays[0], *held)] + list(arrays[1:])
        results = local_kernel(body, outs, arrays=arrays, **more)
        last[:] = results[:1]
        return results

    def hop(array, stream_flip=0, rep_flip=0):
        pairs = [
            (s * reps + r, (s ^ stream_flip) * reps + (r ^ rep_flip))
            for s in range(streams)
            for r in range(reps)
        ]
        return lax.ppermute(array, AXES, pairs)

    def stream_along(array):
        return [hop(array, k) for k in (2, 4, 6)]

    def stream_across(array, near):
        near = jnp.stack([array] + near)
        return [near, hop(near, 1)]

    def rep_full(array):
        far = hop(array, 0, 2)
        return [array, hop(array, 0, 1), far, hop(far, 0, 1)]

    def rep_each(parts):
        return [parts[0]] + [hop(parts[k], 0, k) for k in range(1, 4)]

    (parcels_out,) = run(
        deal_blocks,
        [like((streams, 2 * BLK + 16, width), BF)],
        [memory_rows],
        scalars=[routes],
    )
    parcels = lax.all_to_all(parcels_out, "stream", split_axis=0, concat_axis=0, tiled=True)
    joined, r1, h1, qc, turned1 = run(
        self_forward,
        [
            like((rows, 3 * width), BF),
            like((rows, width), F32),
            like((rows, width), BF),
            like((rows, width), BF),
            like((3 * width, rows), BF),
        ],
        [tokens, w_self, w_self_out, w_cross_q, row_of(gain_one), row_of(shift_one)],
        cost=5,
    )
    early = rep_full(turned1)
    kv_own, memory_turned = run(
        own_keys,
        [like((memory_rows.shape[0], 2 * width), BF), like(memory_rows.shape[::-1], BF)],
        [memory_rows, w_cross_kv],
        cost=6,
    )
    keys = streams * 2 * BLK
    o2, kv, sums = run(
        cross_forward,
        [like((rows, width), BF), like((keys, 2 * width), BF), like((2 * rows, LANES), F32)],
        [qc, parcels, w_cross_kv],
        done=early,
        scratch=[
            pltpu.VMEM((2 * rows, keys), F32),
            pltpu.VMEM((2 * rows, keys), BF),
            pltpu.VMEM((8, keys), F32),
        ],
        cost=17,
    )

    qc_near = stream_along(after(qc, parcels))
    qc_all = stream_across(qc, qc_near)

    vec = jnp.concatenate([row_of(v) for v in (gain_two, shift_two, gain_three, shift_three)])
    each = 2 * quarter + share
    layer_out, dr2, do2, sums2, small_ff, small_up, *parts = run(
        feed_forward,
        [
            like((rows, width), BF),
            like((rows, width), F32),
            like((rows + 16, width), BF),
            like((2 * rows, LANES), F32),
            like((8, width), F32),
            like((1, hidden), F32),
        ]
        + [like((each + base, rows), BF) for base in (0, 3 * width, 3 * width, 0)],
        [
            o2, h1, sums, w_cross_out, w_up, w_down, row_of(b_up), row_of(b_down), vec,
            cotangent[0],
        ],
        done=qc_near,
        scalars=[rep_scalar],
        scratch=[
            pltpu.VMEM((rows, hidden), F32),
            pltpu.VMEM((hidden, rows), BF),
            pltpu.VMEM((hidden, rows), BF),
        ],
        cost=12,
    )
    far = hop(parts[2], 0, 2)
    do2_near = stream_along(do2)

    (dqc,) = run(
        cross_backward,
        [like((rows, width), BF)],
        [qc, do2, kv, parcels, sums2],
        scratch=[pltpu.VMEM((8, keys), F32)],
        cost=13,
    )
    near, other = hop(after(parts[1], dqc), 0, 1), hop(after(parts[3], dqc), 0, 3)
    do2_all = stream_across(do2, do2_near)
    d_tokens, small_self, *exports = run(
        self_backward,
        [like((rows, width), F32), like((8, width), F32)]
        + [like((rows, width + share), BF)] * 4,
        [dqc, dr2, r1, joined, w_cross_q, w_self_out, w_self, row_of(gain_one)],
        done=[qc_all[1]] + do2_near,
        scalars=[rep_scalar],
        scratch=[
            pltpu.VMEM((rows, 3 * width), BF),
            pltpu.VMEM((4, rows, width + share), BF),
        ],
        cost=9,
    )
    grads_all = rep_each(exports)
    far_full = hop(after(far, small_self), 0, 1)

    shared = [parts[1], near, far, far_full, parts[0], other]

    def full_at(row):
        return tuple((a, row) for a in (0, 1, 2, 3))

    def each_at(row):
        return ((4, row), (1, 3 * width + row), (2, 3 * width + row), (5, row))

    def blocks_of(plan, arrays, size, wide, extra=None):
        return run(
            functools.partial(weight_blocks, plan, extra),
            [like((4, size, wide), BF)] * 4,
            arrays,
            scalars=[bits],
            scratch=[
                pltpu.VMEM((width, 4 * rows), BF),
                pltpu.VMEM((4 * rows, width), BF),
                pltpu.VMEM((width, width), F32),
            ],
            cost=5,
        )

    def first_hops(blocks):
        send0, keep0, send1, keep1 = blocks
        return [keep0, hop(send0, 1), keep1, hop(send1, 2)]

    def second_hops(arrays):
        give0, mine0, give1, mine1 = run(
            fold_two,
            [like((2,) + arrays[0].shape[1:], BF)] * 4,
            arrays,
            scalars=[bits],
        )
        return [mine0, hop(give0, 2), mine1, hop(give1, 1)]

    def third_hop(arrays):
        give, mine = run(
            fold_high,
            [like((len(arrays) // 2,) + arrays[0].shape[1:], BF)] * 2,
            arrays,
            scalars=[bits],
        )
        return [mine, hop(give, 4)]

    def last_hops(arrays):
        (piece,) = run(fold_last, [like(arrays[0].shape, BF)], arrays)
        return rep_full(piece)

    def gathered(pieces, plan, shapes):
        return run(
            functools.partial(lay_columns, plan),
            [like(shape, F32) for shape in shapes],
            pieces,
            scalars=[rep_scalar],
            scratch=[pltpu.VMEM((4,) + pieces[0].shape, BF)],
        )

    ff = first_hops(
        blocks_of(
            [
                (full_at(0), each_at(quarter), True, quarter, 0, 0),
                (each_at(0), full_at(2 * width), True, width, 1, 0),
            ],
            shared,
            tall,
            width,
        )
    )

    (dkv,) = run(
        owner_backward,
        [like((memory_rows.shape[0], 2 * width), BF)],
        qc_all + do2_all + [kv_own],
        scalars=[(routes[0] ^ me).astype(jnp.int32)],
        scratch=[
            pltpu.VMEM((streams, PAIRS, 2 * rows, LANES), BF),
            pltpu.VMEM((streams, PAIRS, 2 * rows, LANES), BF),
            pltpu.VMEM((streams, 16, 2 * rows), F32),
        ],
        cost=12,
    )
    ff = second_hops(ff)
    vectors = jnp.concatenate([small_ff[0:5], small_self[0:2]]).reshape(7, streams, tall)
    vectors = jnp.pad(vectors.transpose(1, 0, 2), ((0, 0), (0, 0), (0, LANES - tall)))
    vectors = jnp.concatenate(
        [
            vectors,
            small_up.reshape(streams, -1, LANES),
            jnp.zeros((streams, 9 - hidden // streams // LANES, LANES), F32),
        ],
        axis=1,
    )
    own = len(shared)
    early_at = lambda row: tuple((own + k, row) for k in range(4))
    grads_at = lambda col: tuple((own + 4 + k, col) for k in range(4))
    rest = first_hops(
        blocks_of(
            [
                (early_at(0), grads_at(0), False, 3 * share, 0, 0),
                (early_at(width), grads_at(3 * share), False, share, 1, 0),
                (early_at(2 * width), grads_at(4 * share), False, share, 1, share),
                (full_at(width), each_at(2 * quarter), True, share, 1, 2 * share),
            ],
            shared + early + grads_all + [vectors],
            tall + 16,
            3 * share,
            own + 8,
        )
    )
    ff = third_hop(ff)
    kv_wide = 2 * width // 4
    kv_keep, kv_send = run(
        memory_weights,
        [like((2, width, kv_wide), BF)] * 2,
        [dkv, memory_turned],
        scalars=[rep_scalar],
        cost=7,
    )
    kv_core = hop(kv_send, 0, 1)
    (d_memory,) = run(
        memory_backward,
        [like(memory_rows.shape, BF)],
        [dkv, w_cross_kv],
        cost=6,
    )
    near_sum, far_sum = run(
        fold_core,
        [like((width, kv_wide), F32), like((width, kv_wide), BF)],
        [kv_keep, kv_core],
    )
    kv_far = hop(far_sum, 0, 2)
    rest = second_hops(rest)
    ff = last_hops(ff)
    send, keep = run(
        fold_rep,
        [like((4, tall, kv_wide), BF)] * 2,
        [near_sum, kv_far],
        scalars=[bits],
    )
    kv_part = [keep, hop(send, 1)]
    rest = third_hop(rest)
    give, mine = run(
        fold_one, [like((2, tall, kv_wide), BF)] * 2, kv_part, scalars=[bits]
    )
    kv_part = [mine, hop(give, 2)]
    g_up, g_down = gathered(
        ff,
        [(0, 0, quarter, "side"), (1, 0, width, "below")],
        [(tall, hidden), (hidden // streams, width)],
    )
    kv_part = third_hop(kv_part)
    rest = last_hops(rest)
    kv_part = last_hops(kv_part)
    g_self, g_self_out, g_query, g_out, g_vec = gathered(
        rest,
        [
            (0, 0, 3 * share, "side"),
            (1, 0, share, "side"),
            (1, share, share, "side"),
            (1, 2 * share, share, "side"),
            (0, 0, LANES, "sum"),
        ],
        [(tall, 3 * width), (tall, width), (tall, width), (tall, width), (16, LANES)],
    )
    (g_kv,) = gathered(kv_part, [(0, 0, kv_wide, "side")], [(tall, 2 * width)])
    piece = lambda row: g_vec[row, 0:tall]
    d_b_up = g_vec[7 : 7 + hidden // streams // LANES].reshape(-1)
    return (
        layer_out[None],
        d_tokens[None],
        d_memory[None],
        g_self,
        g_self_out,
        g_query,
        g_kv,
        g_out,
        g_up,
        d_b_up,
        g_down,
        piece(0),
        piece(5),
        piece(6),
        piece(1),
        piece(2),
        piece(3),
        piece(4),
    )


def solution(mesh):
    in_specs = (
        P("rep", "stream", None),
        P("rep", "stream", None),
        P("rep", "stream"),
        P(),
        P(),
        P(),
        P(),
        P(),
        P(),
        P(),
        P(),
        P(),
        P(),
        P(),
        P(),
        P(),
        P(),
        P(),
        P("rep", "stream", None),
    )
    out_specs = (
        P("rep", "stream", None),
        P("rep", "stream", None),
        P("rep", "stream", None),
        P("stream", None),
        P("stream", None),
        P("stream", None),
        P("stream", None),
        P("stream", None),
        P("stream", None),
        P("stream"),
        P("stream", None),
        P("stream"),
        P("stream"),
        P("stream"),
        P("stream"),
        P("stream"),
        P("stream"),
        P("stream"),
    )
    small_slice = (mesh.shape["stream"], mesh.shape["rep"]) == (8, 4)
    return jax.shard_map(
        fast_on_device if small_slice else on_device, mesh=mesh, in_specs=in_specs, out_specs=out_specs, check_vma=False
    )
```

```python
import functools

import jax
import jax.numpy as jnp
from jax import lax
from jax.experimental import pallas as pl
from jax.experimental.pallas import tpu as pltpu
from jax.sharding import PartitionSpec as P

HEADS = 12
HEAD_DIM = 64
BLK = 128


def matmul(left, right):
    return jnp.dot(left, right, preferred_element_type=jnp.float32)


def product_left(left, right):
    return lax.dot_general(
        left, right, (((0,), (0,)), ((), ())), preferred_element_type=jnp.float32
    )


def product_right(left, right):
    return lax.dot_general(
        left, right, (((1,), (1,)), ((), ())), preferred_element_type=jnp.float32
    )


def layer_norm(rows, gain, shift):
    centred = rows - jnp.mean(rows, axis=-1, keepdims=True)
    spread = jnp.mean(centred * centred, axis=-1, keepdims=True)
    return centred * lax.rsqrt(spread + 1e-05) * gain + shift


def split_heads(rows):
    return rows.reshape(rows.shape[0], HEADS, HEAD_DIM).transpose(1, 0, 2)


def join_heads(rows):
    return rows.transpose(1, 0, 2).reshape(rows.shape[1], HEADS * HEAD_DIM)


def masked_scores(query_head, key_head, key_ok):
    scores = product_right(query_head, key_head) * HEAD_DIM ** (-0.5)
    if key_ok is not None:
        scores = jnp.where(key_ok[None, :], scores, -1e30)
    return scores


def attend_forward(query, key_rows, value_rows, key_ok):

    def one_head(item):
        query_head, key_head, value_head = item
        scores = masked_scores(query_head, key_head, key_ok)
        row_max = jnp.max(scores, axis=1, keepdims=True)
        exponent = jnp.exp(scores - row_max)
        row_total = jnp.sum(exponent, axis=1, keepdims=True)
        probability = (exponent / row_total).astype(jnp.bfloat16)
        return (matmul(probability, value_head), (row_max + jnp.log(row_total))[:, 0])

    mixed, log_total = lax.map(
        one_head, (split_heads(query), split_heads(key_rows), split_heads(value_rows))
    )
    return (join_heads(mixed), log_total)


def attend_backward(query, key_rows, value_rows, key_ok, log_total, d_mixed):
    factor = HEAD_DIM ** (-0.5)

    def one_head(item):
        query_head, key_head, value_head, total_head, grad_head = item
        scores = masked_scores(query_head, key_head, key_ok)
        probability = jnp.exp(scores - total_head[:, None])
        d_prob = product_right(grad_head, value_head)
        d_scores = probability * (d_prob - jnp.sum(d_prob * probability, axis=1, keepdims=True))
        d_scores = d_scores.astype(jnp.bfloat16)
        d_query = matmul(d_scores, key_head) * factor
        d_key = product_left(d_scores, query_head) * factor
        d_value = product_left(probability.astype(jnp.bfloat16), grad_head)
        return (d_query, d_key, d_value)

    d_query, d_key, d_value = lax.map(
        one_head,
        (
            split_heads(query),
            split_heads(key_rows),
            split_heads(value_rows),
            log_total,
            split_heads(d_mixed),
        ),
    )
    return (join_heads(d_query), join_heads(d_key), join_heads(d_value))


def on_device(
    queries,
    memory,
    routes,
    w_self,
    w_self_out,
    w_cross_q,
    w_cross_kv,
    w_cross_out,
    w_up,
    b_up,
    w_down,
    b_down,
    gain_one,
    shift_one,
    gain_two,
    shift_two,
    gain_three,
    shift_three,
    cotangent,
):
    streams = lax.axis_size("stream")
    blocks = routes.shape[1]
    capacity = max(2, 2 * blocks // streams)
    slot_count = streams * capacity
    model_width = w_self_out.shape[0]
    target = routes[0]
    hit_table = (target[:, None] == jnp.arange(streams, dtype=jnp.int32)[None, :]).astype(jnp.int32)
    before = jnp.cumsum(hit_table, axis=0) - hit_table
    rank_in = jnp.sum(before * hit_table, axis=1)
    slot_of_block = target * capacity + rank_in
    matched = (slot_of_block[None, :] == jnp.arange(slot_count, dtype=jnp.int32)[:, None]).astype(
        jnp.int32
    )
    block_at = jnp.sum(matched * jnp.arange(blocks, dtype=jnp.int32)[None, :], axis=1)
    live_slot = jnp.sum(matched, axis=1)
    live_grid = live_slot.reshape(streams, capacity)
    filled = (live_slot > 0)[:, None, None]
    nothing = jnp.zeros((), jnp.bfloat16)
    memory_rows = memory[0]
    projected = (
        matmul(memory_rows, w_cross_kv).astype(jnp.bfloat16).reshape(blocks, BLK, 2 * model_width)
    )
    outgoing = jnp.where(filled, jnp.take(projected, block_at, axis=0), nothing)
    arrived, arrived_live = (
        lax.all_to_all(
            outgoing.reshape(streams, capacity, BLK, 2 * model_width),
            "stream",
            split_axis=0,
            concat_axis=0,
            tiled=True,
        ),
        lax.all_to_all(live_grid, "stream", split_axis=0, concat_axis=0, tiled=True),
    )
    keys_values = arrived.reshape(-1, 2 * model_width)
    key_ok = jnp.repeat(arrived_live.reshape(-1), BLK) > 0
    key_cross = keys_values[:, :model_width]
    value_cross = keys_values[:, model_width:]
    gain_a = gain_one.astype(jnp.float32)
    shift_a = shift_one.astype(jnp.float32)
    gain_b = gain_two.astype(jnp.float32)
    shift_b = shift_two.astype(jnp.float32)
    gain_c = gain_three.astype(jnp.float32)
    shift_c = shift_three.astype(jnp.float32)
    tokens = queries[0]
    joined = matmul(tokens, w_self).astype(jnp.bfloat16)
    query_self = joined[:, :model_width]
    key_self = joined[:, model_width : 2 * model_width]
    value_self = joined[:, 2 * model_width :]
    mixed_self, total_self = attend_forward(query_self, key_self, value_self, None)
    mixed_self = mixed_self.astype(jnp.bfloat16)
    residual_one = tokens.astype(jnp.float32) + matmul(mixed_self, w_self_out)
    normed_one = layer_norm(residual_one, gain_a, shift_a).astype(jnp.bfloat16)
    query_cross = matmul(normed_one, w_cross_q).astype(jnp.bfloat16)
    mixed_cross, total_cross = attend_forward(query_cross, key_cross, value_cross, key_ok)
    mixed_cross = mixed_cross.astype(jnp.bfloat16)
    residual_two = normed_one.astype(jnp.float32) + matmul(mixed_cross, w_cross_out)
    normed_two = layer_norm(residual_two, gain_b, shift_b).astype(jnp.bfloat16)
    hidden_pre = matmul(normed_two, w_up) + b_up.astype(jnp.float32)
    hidden = jax.nn.gelu(hidden_pre, approximate=False).astype(jnp.bfloat16)
    residual_three = (
        normed_two.astype(jnp.float32) + matmul(hidden, w_down) + b_down.astype(jnp.float32)
    )
    layer_out = layer_norm(residual_three, gain_c, shift_c).astype(jnp.bfloat16)
    grad_out = cotangent[0].astype(jnp.float32)
    norm_three_pull = jax.vjp(layer_norm, residual_three, gain_c, shift_c)[1]
    d_residual_three, d_gain_c, d_shift_c = norm_three_pull(grad_out)
    d_branch_three = d_residual_three.astype(jnp.bfloat16)
    d_b_down = jnp.sum(d_branch_three.astype(jnp.float32), axis=0)
    d_w_down = product_left(hidden, d_branch_three)
    d_hidden = product_right(d_branch_three, w_down)
    gelu_pull = jax.vjp(lambda value: jax.nn.gelu(value, approximate=False), hidden_pre)[1]
    d_hidden_pre = gelu_pull(d_hidden)[0].astype(jnp.bfloat16)
    d_b_up = jnp.sum(d_hidden_pre.astype(jnp.float32), axis=0)
    d_w_up = product_left(normed_two, d_hidden_pre)
    d_normed_two = d_residual_three + product_right(d_hidden_pre, w_up)
    norm_two_pull = jax.vjp(layer_norm, residual_two, gain_b, shift_b)[1]
    d_residual_two, d_gain_b, d_shift_b = norm_two_pull(d_normed_two)
    d_branch_two = d_residual_two.astype(jnp.bfloat16)
    d_w_cross_out = product_left(mixed_cross, d_branch_two)
    d_mixed_cross = product_right(d_branch_two, w_cross_out).astype(jnp.bfloat16)
    d_query_cross, d_key_cross, d_value_cross = attend_backward(
        query_cross, key_cross, value_cross, key_ok, total_cross, d_mixed_cross
    )
    d_query_cross = d_query_cross.astype(jnp.bfloat16)
    d_keys_values = jnp.concatenate([d_key_cross, d_value_cross], axis=1).astype(jnp.bfloat16)
    d_w_cross_q = product_left(normed_one, d_query_cross)
    d_normed_one = d_residual_two + product_right(d_query_cross, w_cross_q)
    norm_one_pull = jax.vjp(layer_norm, residual_one, gain_a, shift_a)[1]
    d_residual_one, d_gain_a, d_shift_a = norm_one_pull(d_normed_one)
    d_branch_one = d_residual_one.astype(jnp.bfloat16)
    d_w_self_out = product_left(mixed_self, d_branch_one)
    d_mixed_self = product_right(d_branch_one, w_self_out).astype(jnp.bfloat16)
    d_query_self, d_key_self, d_value_self = attend_backward(
        query_self, key_self, value_self, None, total_self, d_mixed_self
    )
    d_joined = jnp.concatenate([d_query_self, d_key_self, d_value_self], axis=1).astype(
        jnp.bfloat16
    )
    d_w_self = product_left(tokens, d_joined)
    d_tokens = d_residual_one + product_right(d_joined, w_self)
    returned = lax.all_to_all(
        d_keys_values.reshape(streams, capacity, BLK, 2 * model_width),
        "stream",
        split_axis=0,
        concat_axis=0,
        tiled=True,
    )
    d_block_rows = jnp.take(
        returned.reshape(slot_count, BLK, 2 * model_width), slot_of_block, axis=0
    ).reshape(-1, 2 * model_width)
    d_w_cross_kv = product_left(memory_rows, d_block_rows)
    d_memory = product_right(d_block_rows, w_cross_kv).astype(jnp.bfloat16)
    gradients = (
        d_w_self,
        d_w_self_out,
        d_w_cross_q,
        d_w_cross_kv,
        d_w_cross_out,
        d_w_up,
        d_b_up,
        d_w_down,
        d_b_down,
        d_gain_a,
        d_shift_a,
        d_gain_b,
        d_shift_b,
        d_gain_c,
        d_shift_c,
    )
    shapes = [item.shape for item in gradients]
    flat = [item.reshape(-1) for item in gradients]
    (
        share_self,
        share_self_out,
        share_cross_q,
        share_cross_kv,
        share_cross_out,
        share_up,
        share_b_up,
        share_down,
        share_b_down,
        share_gain_a,
        share_shift_a,
        share_gain_b,
        share_shift_b,
        share_gain_c,
        share_shift_c,
    ) = (
        lax.psum_scatter(flat[0], "stream", scatter_dimension=0, tiled=True),
        lax.psum_scatter(flat[1], "stream", scatter_dimension=0, tiled=True),
        lax.psum_scatter(flat[2], "stream", scatter_dimension=0, tiled=True),
        lax.psum_scatter(flat[3], "stream", scatter_dimension=0, tiled=True),
        lax.psum_scatter(flat[4], "stream", scatter_dimension=0, tiled=True),
        lax.psum_scatter(flat[5], "stream", scatter_dimension=0, tiled=True),
        lax.psum_scatter(flat[6], "stream", scatter_dimension=0, tiled=True),
        lax.psum_scatter(flat[7], "stream", scatter_dimension=0, tiled=True),
        lax.psum_scatter(flat[8], "stream", scatter_dimension=0, tiled=True),
        lax.psum_scatter(flat[9], "stream", scatter_dimension=0, tiled=True),
        lax.psum_scatter(flat[10], "stream", scatter_dimension=0, tiled=True),
        lax.psum_scatter(flat[11], "stream", scatter_dimension=0, tiled=True),
        lax.psum_scatter(flat[12], "stream", scatter_dimension=0, tiled=True),
        lax.psum_scatter(flat[13], "stream", scatter_dimension=0, tiled=True),
        lax.psum_scatter(flat[14], "stream", scatter_dimension=0, tiled=True),
    )
    summed = (
        lax.psum(share_self.astype(jnp.bfloat16), "rep").astype(jnp.float32),
        lax.psum(share_self_out.astype(jnp.bfloat16), "rep").astype(jnp.float32),
        lax.psum(share_cross_q.astype(jnp.bfloat16), "rep").astype(jnp.float32),
        lax.psum(share_cross_kv.astype(jnp.bfloat16), "rep").astype(jnp.float32),
        lax.psum(share_cross_out.astype(jnp.bfloat16), "rep").astype(jnp.float32),
        lax.psum(share_up.astype(jnp.bfloat16), "rep").astype(jnp.float32),
        lax.psum(share_b_up.astype(jnp.bfloat16), "rep").astype(jnp.float32),
        lax.psum(share_down.astype(jnp.bfloat16), "rep").astype(jnp.float32),
        lax.psum(share_b_down.astype(jnp.bfloat16), "rep").astype(jnp.float32),
        lax.psum(share_gain_a.astype(jnp.bfloat16), "rep").astype(jnp.float32),
        lax.psum(share_shift_a.astype(jnp.bfloat16), "rep").astype(jnp.float32),
        lax.psum(share_gain_b.astype(jnp.bfloat16), "rep").astype(jnp.float32),
        lax.psum(share_shift_b.astype(jnp.bfloat16), "rep").astype(jnp.float32),
        lax.psum(share_gain_c.astype(jnp.bfloat16), "rep").astype(jnp.float32),
        lax.psum(share_shift_c.astype(jnp.bfloat16), "rep").astype(jnp.float32),
    )
    results = [
        part.reshape((shape[0] // streams,) + tuple(shape[1:]))
        for part, shape in zip(summed, shapes)
    ]
    return (
        layer_out[None],
        d_tokens[None],
        d_memory[None],
        results[0],
        results[1],
        results[2],
        results[3],
        results[4],
        results[5],
        results[6],
        results[7],
        results[8],
        results[9],
        results[10],
        results[11],
        results[12],
        results[13],
        results[14],
    )


PAIRS = HEADS // 2
LANES = 2 * HEAD_DIM
FACTOR = HEAD_DIM ** (-0.5)
BF = jnp.bfloat16
F32 = jnp.float32
AXES = ("stream", "rep")


def whole_in_vmem(count):
    return [pl.BlockSpec(memory_space=pltpu.VMEM)] * count


def local_kernel(body, out_shape, scalars=(), arrays=(), scratch=(), cost=2, limit=24):
    return pl.pallas_call(
        body,
        out_shape=list(out_shape),
        in_specs=[pl.BlockSpec(memory_space=pltpu.SMEM)] * len(scalars) + whole_in_vmem(len(arrays)),
        out_specs=whole_in_vmem(len(out_shape)),
        scratch_shapes=list(scratch),
        compiler_params=pltpu.CompilerParams(vmem_limit_bytes=limit * 1024 * 1024),
        cost_estimate=pl.CostEstimate(
            flops=int(cost * 1.15e9), bytes_accessed=int(cost * 1e5), transcendentals=0
        ),
    )(*scalars, *arrays)


def like(shape, dtype):
    return jax.ShapeDtypeStruct(shape, dtype)


def dot_nn(left, right):
    return lax.dot_general(left, right, (((1,), (0,)), ((), ())), preferred_element_type=F32)


def dot_nt(left, right):
    return lax.dot_general(left, right, (((1,), (1,)), ((), ())), preferred_element_type=F32)


def head_masks(rows):
    lane = lax.broadcasted_iota(jnp.int32, (rows, LANES), 1)
    return lane < HEAD_DIM


def stack_heads(pair, first, scale):
    one = jnp.where(first, scale, 0.0).astype(BF)
    two = jnp.where(first, 0.0, scale).astype(BF)
    return jnp.concatenate([pair * one, pair * two], axis=0)


def unstack_heads(both, first):
    rows = both.shape[0] // 2
    return jnp.where(first, both[:rows], both[rows:])


def norm_parts(rows):
    centred = rows - jnp.mean(rows, axis=1, keepdims=True)
    spread = jnp.mean(centred * centred, axis=1, keepdims=True)
    inverse = lax.rsqrt(spread + 1e-05)
    return centred * inverse, inverse


def norm_pull(grad, hat, inverse, gain):
    scaled = grad * gain
    inner = scaled - jnp.mean(scaled, axis=1, keepdims=True)
    inner = inner - hat * jnp.mean(scaled * hat, axis=1, keepdims=True)
    return (
        inverse * inner,
        jnp.sum(grad * hat, axis=0, keepdims=True),
        jnp.sum(grad, axis=0, keepdims=True),
    )


def deal_blocks(routes_ref, memory_ref, out_ref):
    out_ref[...] = jnp.zeros_like(out_ref)
    blocks = memory_ref.shape[0] // BLK
    width = memory_ref.shape[1]
    for b in range(blocks):
        group = routes_ref[0, b]
        rank = jnp.int32(0)
        for earlier in range(b):
            rank = rank + (routes_ref[0, earlier] == group).astype(jnp.int32)
        row = pl.multiple_of(rank * BLK, BLK)
        lane = pl.multiple_of(rank * (width // 2), LANES)
        out_ref[group, pl.ds(row, BLK), :] = memory_ref[b * BLK : (b + 1) * BLK, :]
        out_ref[group, 2 * BLK : 2 * BLK + 16, pl.ds(lane, width // 2)] = jnp.ones(
            (16, width // 2), BF
        )


def self_forward(tok, w_in, w_out, w_q, gain, shift, joined, r1, h1_out, qc, turned):
    width = tok.shape[1]
    rows = tok.shape[0]
    joined[...] = dot_nn(tok[...], w_in[...]).astype(BF)
    first = head_masks(rows)
    mixed = []
    for j in range(PAIRS):
        at = j * LANES
        q2 = stack_heads(joined[:, at : at + LANES], first, FACTOR)
        key = joined[:, width + at : width + at + LANES]
        value = joined[:, 2 * width + at : 2 * width + at + LANES]
        scores = dot_nt(q2, key)
        power = jnp.exp(scores - jnp.max(scores, axis=1, keepdims=True))
        prob = (power / jnp.sum(power, axis=1, keepdims=True)).astype(BF)
        mixed.append(unstack_heads(dot_nn(prob, value), first).astype(BF))
    o1 = jnp.concatenate(mixed, axis=1)
    res = tok[...].astype(F32) + dot_nn(o1, w_out[...])
    r1[...] = res
    hat, _ = norm_parts(res)
    h1 = (hat * gain[...].astype(F32) + shift[...].astype(F32)).astype(BF)
    h1_out[...] = h1
    qc[...] = dot_nn(h1, w_q[...]).astype(BF)
    turned[0:width, :] = tok[...].T
    turned[width : 2 * width, :] = o1.T
    turned[2 * width : 3 * width, :] = h1.T


def cross_forward(qc, parcels, w_kv, o2, kv, sums, s_ref, p_ref, bias_ref):
    width = qc.shape[1]
    rows = qc.shape[0]
    sources = parcels.shape[0]
    span = 2 * BLK
    first = head_masks(rows)
    for k in range(sources):
        kv[k * span : (k + 1) * span, :] = dot_nn(parcels[k, 0:span, :], w_kv[...]).astype(BF)
        for c in range(2):
            flag = parcels[k, span : span + 16, c * (width // 2) : c * (width // 2) + BLK]
            bias_ref[:, k * span + c * BLK : k * span + (c + 1) * BLK] = jnp.where(
                flag[0:8].astype(F32) > 0.5, 0.0, -1e30
            )
    lane = lax.broadcasted_iota(jnp.int32, (2 * rows, LANES), 1)
    sums[...] = jnp.zeros_like(sums)

    def one_pair(j, carry):
        at = pl.multiple_of(j * LANES, LANES)
        q2 = stack_heads(qc[:, pl.ds(at, LANES)], first, FACTOR)
        top = None
        for k in range(sources):
            key = kv[k * span : (k + 1) * span, pl.ds(at, LANES)]
            scores = dot_nt(q2, key) + bias_ref[0:1, k * span : (k + 1) * span]
            s_ref[:, k * span : (k + 1) * span] = scores
            most = jnp.maximum(scores[:, :LANES], scores[:, LANES:])
            top = most if top is None else jnp.maximum(top, most)
        peak = jnp.max(top, axis=1, keepdims=True)
        total = None
        for k in range(sources):
            power = jnp.exp(s_ref[:, k * span : (k + 1) * span] - peak)
            p_ref[:, k * span : (k + 1) * span] = power.astype(BF)
            part = power[:, :LANES] + power[:, LANES:]
            total = part if total is None else total + part
        total = jnp.sum(total, axis=1, keepdims=True)
        value = kv[:, pl.ds(pl.multiple_of(width + j * LANES, LANES), LANES)]
        both = dot_nn(p_ref[...], value) / total
        o2[:, pl.ds(at, LANES)] = unstack_heads(both, first).astype(BF)
        sums[...] = jnp.where(lane == j, peak + jnp.log(total), sums[...])
        return carry

    lax.fori_loop(0, PAIRS, one_pair, 0, unroll=PAIRS)


def feed_forward(
    rep_ref, o2, tok_h1, sums, w_co, w_up, w_down, b_up, b_down, vec, cot,
    layer_out, dr2, do2, both_sums, small, small_up, parcel0, parcel1, parcel2, parcel3,
    slope, acts, dus,
):
    width = o2.shape[1]
    rows = o2.shape[0]
    hidden = w_up.shape[1]
    quarter = hidden // 4
    rep = rep_ref[0]
    gain2, shift2, gain3, shift3 = (vec[i : i + 1, :].astype(F32) for i in range(4))
    res2 = tok_h1[...].astype(F32) + dot_nn(o2[...], w_co[...])
    hat2, inv2 = norm_parts(res2)
    h2 = (hat2 * gain2 + shift2).astype(BF)
    for parcel in (parcel1, parcel2):
        parcel[0:width, :] = h2.T
        parcel[width : 2 * width, :] = o2[...].T
    total = None
    for c in range(4):
        cols = slice(c * quarter, (c + 1) * quarter)
        u = dot_nn(h2, w_up[:, cols]) + b_up[:, cols].astype(F32)
        cdf = 0.5 + 0.5 * lax.erf(u * 0.7071067811865476)
        act = (u * cdf).astype(BF)
        slope[:, cols] = cdf + u * (jnp.exp(u * u * -0.5) * 0.3989422804014327)
        acts[cols, :] = act.T
        part = dot_nn(act, w_down[cols, :])
        total = part if total is None else total + part
    res3 = h2.astype(F32) + total + b_down[...].astype(F32)
    hat3, inv3 = norm_parts(res3)
    layer_out[...] = (hat3 * gain3 + shift3).astype(BF)
    dr3, d_gain3, d_shift3 = norm_pull(cot[...].astype(F32), hat3, inv3, gain3)
    dy3 = dr3.astype(BF)
    small[0:1, :] = jnp.sum(dy3.astype(F32), axis=0, keepdims=True)
    small[3:4, :] = d_gain3
    small[4:5, :] = d_shift3
    back = None
    for c in range(4):
        cols = slice(c * quarter, (c + 1) * quarter)
        du = (dot_nt(dy3, w_down[cols, :]) * slope[:, cols]).astype(BF)
        small_up[:, cols] = jnp.sum(du.astype(F32), axis=0, keepdims=True)
        dus[cols, :] = du.T
        part = dot_nt(du, w_up[:, cols])
        back = part if back is None else back + part
    grad2, d_gain2, d_shift2 = norm_pull(dr3 + back, hat2, inv2, gain2)
    small[1:2, :] = d_gain2
    small[2:3, :] = d_shift2
    small[5:8, :] = jnp.zeros((3, width), F32)
    dr2[...] = grad2
    dy2 = grad2.astype(BF)
    grad_mixed = dot_nt(dy2, w_co[...]).astype(BF)
    do2[0:rows, :] = grad_mixed
    lane = lax.broadcasted_iota(jnp.int32, (2 * rows, LANES), 1)
    first = head_masks(rows)
    packed = sums[...]
    for j in range(PAIRS):
        at = slice(j * LANES, (j + 1) * LANES)
        prod = grad_mixed[:, at].astype(F32) * o2[:, at].astype(F32)
        zero = jnp.zeros_like(prod)
        two = jnp.concatenate([jnp.where(first, prod, zero), jnp.where(first, zero, prod)], axis=0)
        packed = jnp.where(lane == 8 + j, jnp.sum(two, axis=1, keepdims=True), packed)
    both_sums[...] = packed
    turned = packed.T[0:16, :]
    high = turned.astype(BF)
    rest = turned - high.astype(F32)
    middle = rest.astype(BF)
    low = (rest - middle.astype(F32)).astype(BF)
    do2[rows : rows + 16, :] = jnp.concatenate([high, middle, low], axis=1)
    share = width // 4
    dy2_turned = dy2.T
    dy3_turned = dy3.T
    strip = quarter // 8
    for k, parcel in enumerate((parcel0, parcel1, parcel2, parcel3)):
        peer = rep ^ k
        base = 0
        if k in (1, 2):
            parcel[2 * width : 3 * width, :] = dy3_turned
            base = 3 * width
        for s in range(8):
            row = pl.multiple_of(s * 4 * strip + peer * strip, strip)
            parcel[base + s * strip : base + (s + 1) * strip, :] = acts[pl.ds(row, strip), :]
        row = pl.multiple_of(peer * quarter, quarter)
        parcel[base + quarter : base + 2 * quarter, :] = dus[pl.ds(row, quarter), :]
        piece = dy2_turned[0:share]
        for i in range(1, 4):
            piece = jnp.where(peer == i, dy2_turned[i * share : (i + 1) * share], piece)
        parcel[base + 2 * quarter : base + 2 * quarter + share, :] = piece


def cross_backward(qc, do2, kv, parcels, sums, dqc, bias_ref):
    width = qc.shape[1]
    rows = qc.shape[0]
    sources = parcels.shape[0]
    span = 2 * BLK
    first = head_masks(rows)
    for k in range(sources):
        for c in range(2):
            flag = parcels[k, span : span + 16, c * (width // 2) : c * (width // 2) + BLK]
            bias_ref[:, k * span + c * BLK : k * span + (c + 1) * BLK] = jnp.where(
                flag[0:8].astype(F32) > 0.5, 0.0, -1e30
            )
    lane = lax.broadcasted_iota(jnp.int32, (2 * rows, LANES), 1)

    def one_pair(j, carry):
        at = pl.multiple_of(j * LANES, LANES)
        q2 = stack_heads(qc[:, pl.ds(at, LANES)], first, FACTOR)
        g2 = stack_heads(do2[0:rows, pl.ds(at, LANES)], first, 1.0)
        packed = sums[...]
        log_sum = jnp.sum(jnp.where(lane == j, packed, 0.0), axis=1, keepdims=True)
        delta = jnp.sum(jnp.where(lane == j + 8, packed, 0.0), axis=1, keepdims=True)
        total = None
        for k in range(sources):
            key = kv[k * span : (k + 1) * span, pl.ds(at, LANES)]
            value = kv[
                k * span : (k + 1) * span, pl.ds(pl.multiple_of(width + j * LANES, LANES), LANES)
            ]
            scores = dot_nt(q2, key) + bias_ref[0:1, k * span : (k + 1) * span]
            prob = jnp.exp(scores - log_sum)
            grad = (prob * (dot_nt(g2, value) - delta)).astype(BF)
            part = dot_nn(grad, key)
            total = part if total is None else total + part
        dqc[:, pl.ds(at, LANES)] = (unstack_heads(total, first) * FACTOR).astype(BF)
        return carry

    lax.fori_loop(0, PAIRS, one_pair, 0, unroll=PAIRS)


def self_backward(
    rep_ref, dqc_ref, dr2, r1, joined, w_q, w_out, w_in, gain,
    d_tok, small, out0, out1, out2, out3,
    da_ref, quarters,
):
    rows, width = dqc_ref.shape
    rep = rep_ref[0]
    first = head_masks(rows)
    dqc = dqc_ref[...]
    grad1 = dr2[...] + dot_nt(dqc, w_q[...])
    hat1, inv1 = norm_parts(r1[...])
    dr1, d_gain1, d_shift1 = norm_pull(grad1, hat1, inv1, gain[...].astype(F32))
    small[0:1, :] = d_gain1
    small[1:2, :] = d_shift1
    small[2:8, :] = jnp.zeros((6, width), F32)
    dy1 = dr1.astype(BF)
    do1 = dot_nt(dy1, w_out[...]).astype(BF)
    for j in range(PAIRS):
        at = slice(j * LANES, (j + 1) * LANES)
        key_at = slice(width + j * LANES, width + (j + 1) * LANES)
        value_at = slice(2 * width + j * LANES, 2 * width + (j + 1) * LANES)
        q2 = stack_heads(joined[:, at], first, FACTOR)
        g2 = stack_heads(do1[:, at], first, 1.0)
        key, value = joined[:, key_at], joined[:, value_at]
        scores = dot_nt(q2, key)
        power = jnp.exp(scores - jnp.max(scores, axis=1, keepdims=True))
        prob = power / jnp.sum(power, axis=1, keepdims=True)
        d_prob = dot_nt(g2, value)
        d_scores = (prob * (d_prob - jnp.sum(d_prob * prob, axis=1, keepdims=True))).astype(BF)
        da_ref[:, at] = (unstack_heads(dot_nn(d_scores, key), first) * FACTOR).astype(BF)
        da_ref[:, key_at] = product_left(d_scores, q2).astype(BF)
        da_ref[:, value_at] = product_left(prob.astype(BF), g2).astype(BF)
    d_tok[...] = dr1 + dot_nt(da_ref[...], w_in[...])
    third = 3 * width // 4
    share = width // 4
    da = da_ref[...]
    for i in range(4):
        quarters[i, :, 0:third] = da[:, i * third : (i + 1) * third]
        quarters[i, :, third : third + share] = dy1[:, i * share : (i + 1) * share]
        quarters[i, :, width : width + share] = dqc[:, i * share : (i + 1) * share]
    for k, out in enumerate((out0, out1, out2, out3)):
        out[...] = quarters[rep ^ k]


def owner_backward(where_ref, *refs):
    groups = 8
    qc_near, qc_far, do_near, do_far, kv, dkv, q_ref, g_ref, sum_ref = refs
    _, rows, width = qc_near.shape
    first = head_masks(rows)
    for k in range(groups):
        query = (qc_far if k % 2 else qc_near)[k // 2]
        extra = (do_far if k % 2 else do_near)[k // 2]
        sums = extra[rows : rows + 16, :].astype(F32)
        third = width // 3
        sum_ref[k] = sums[:, 0:third] + sums[:, third : 2 * third] + sums[:, 2 * third :]
        for j in range(PAIRS):
            at = slice(j * LANES, (j + 1) * LANES)
            q_ref[k, j] = stack_heads(query[:, at], first, FACTOR)
            g_ref[k, j] = stack_heads(extra[0:rows, at], first, 1.0)
    blocks = kv.shape[0] // BLK

    def one_block(b, carry):
        group = where_ref[b]
        row = pl.multiple_of(b * BLK, BLK)
        for j in range(PAIRS):
            key_at = slice(j * LANES, (j + 1) * LANES)
            value_at = slice(width + j * LANES, width + (j + 1) * LANES)
            key = kv[pl.ds(row, BLK), key_at]
            value = kv[pl.ds(row, BLK), value_at]
            q2 = q_ref[group, j]
            g2 = g_ref[group, j]
            log_sum = sum_ref[group, j : j + 1, :]
            delta = sum_ref[group, 8 + j : 9 + j, :]
            prob = jnp.exp(dot_nt(key, q2) - log_sum)
            grad = (prob * (dot_nt(value, g2) - delta)).astype(BF)
            dkv[pl.ds(row, BLK), key_at] = dot_nn(grad, q2).astype(BF)
            dkv[pl.ds(row, BLK), value_at] = dot_nn(prob.astype(BF), g2).astype(BF)
        return carry

    lax.fori_loop(0, blocks, one_block, 0)


def memory_weights(rep_ref, dkv, memory_turned, keep, send):
    quarter = dkv.shape[1] // 4
    rep = rep_ref[0]
    for k in range(4):
        at = pl.multiple_of((rep ^ k) * quarter, LANES)
        out = (keep, send)[k % 2]
        out[k // 2] = dot_nn(memory_turned[...], dkv[:, pl.ds(at, quarter)]).astype(BF)


def memory_backward(dkv, w_kv, d_memory):
    half = dkv.shape[0] // 2
    for i in range(2):
        span = slice(i * half, (i + 1) * half)
        d_memory[span, :] = dot_nt(dkv[span, :], w_kv[...]).astype(BF)


def own_keys(memory_ref, w_kv, kv, turned):
    kv[...] = dot_nn(memory_ref[...], w_kv[...]).astype(BF)
    turned[...] = memory_ref[...].T


def weight_blocks(plan, extra, bits_ref, *refs):
    outs, (left_all, right_all, product) = refs[-7:-3], refs[-3:]
    arrays = refs[:-7]
    width, depth = left_all.shape
    rows = depth // 4
    tall = width // 8

    def blocks_of(group):
        bit = bits_ref[group]
        for i in range(4):
            for out, b in ((outs[2 * group], 1 - bit), (outs[2 * group + 1], bit)):
                if group == 0:
                    yield out, i, 2 * i + b
                else:
                    yield out, i, 4 * (i // 2) + 2 * b + i % 2

    for lefts, rights, turned, cols, group, to in plan:
        for k, ((a, row), (g, off)) in enumerate(zip(lefts, rights)):
            span = slice(k * rows, (k + 1) * rows)
            left_all[:, span] = arrays[a][row : row + width, :]
            right = arrays[g][off : off + cols, :].T if turned else arrays[g][:, off : off + cols]
            right_all[span, 0:cols] = right
        product[:, 0:cols] = dot_nn(left_all[...], right_all[:, 0:cols])
        for out, i, block in blocks_of(group):
            at = pl.multiple_of(block * tall, 16)
            out[i, 0:tall, to : to + cols] = product[pl.ds(at, tall), 0:cols].astype(BF)
    if extra is not None:
        for group in range(2):
            for out, i, block in blocks_of(group):
                out[i, tall:, :] = jnp.zeros_like(out[i, tall:, :])
                if group == 0:
                    out[i, tall:, 0:LANES] = arrays[extra][block].astype(BF)


def fold_two(bits_ref, kept0, got0, kept1, got1, give0, mine0, give1, mine1):
    for bit, kept, got, give, mine in (
        (bits_ref[1], kept0, got0, give0, mine0),
        (bits_ref[0], kept1, got1, give1, mine1),
    ):
        for i in range(2):
            for out, at in ((give, 2 * i + 1 - bit), (mine, 2 * i + bit)):
                out[i] = (kept[at].astype(F32) + got[at].astype(F32)).astype(BF)


def fold_high(bits_ref, *refs):
    (give, mine), arrays = refs[-2:], refs[:-2]
    bit = bits_ref[2]
    for g in range(len(arrays) // 2):
        kept, got = arrays[2 * g], arrays[2 * g + 1]
        for out, at in ((give, 1 - bit), (mine, bit)):
            out[g] = (kept[at].astype(F32) + got[at].astype(F32)).astype(BF)


def fold_one(bits_ref, kept, got, give, mine):
    bit = bits_ref[1]
    for i in range(2):
        for out, at in ((give, 2 * i + 1 - bit), (mine, 2 * i + bit)):
            out[i] = (kept[at].astype(F32) + got[at].astype(F32)).astype(BF)


def fold_last(kept, got, out):
    out[...] = (kept[...].astype(F32) + got[...].astype(F32)).astype(BF)


def fold_core(kept, got, near, far):
    near[...] = kept[0].astype(F32) + got[0].astype(F32)
    far[...] = (kept[1].astype(F32) + got[1].astype(F32)).astype(BF)


def fold_rep(bits_ref, near, got, send, keep):
    y = bits_ref[0]
    tall = send.shape[1]
    for z in range(4):
        for out, bit in ((send, 1 - y), (keep, y)):
            at = pl.multiple_of((2 * z + bit) * tall, 16)
            out[z] = (near[pl.ds(at, tall), :] + got[pl.ds(at, tall), :].astype(F32)).astype(BF)


def lay_columns(plan, rep_ref, *refs):
    pieces, outs, held = refs[0:4], refs[4:-1], refs[-1]
    rep = rep_ref[0]
    for k in range(4):
        held[k] = pieces[k][...]
    for (group, start, cols, how), out in zip(plan, outs):
        if how == "sum":
            tall = out.shape[0]
            total = None
            for k in range(4):
                part = pieces[k][group, pieces[k].shape[1] - tall :, start : start + cols].astype(F32)
                total = part if total is None else total + part
            out[...] = total
            continue
        tall = out.shape[0] if how == "side" else out.shape[0] // 4
        for q in range(4):
            part = held[rep ^ q, group, 0:tall, start : start + cols].astype(F32)
            if how == "side":
                out[:, q * cols : (q + 1) * cols] = part
            else:
                out[q * tall : (q + 1) * tall, :] = part


def fast_on_device(
    queries, memory, routes, w_self, w_self_out, w_cross_q, w_cross_kv, w_cross_out, w_up, b_up,
    w_down, b_down, gain_one, shift_one, gain_two, shift_two, gain_three, shift_three, cotangent,
):
    streams, reps = lax.axis_size("stream"), lax.axis_size("rep")
    me, rep = lax.axis_index("stream"), lax.axis_index("rep")
    width = w_self_out.shape[0]
    hidden = w_up.shape[1]
    quarter, share, tall = hidden // 4, width // 4, width // streams
    tokens = queries[0]
    rows = tokens.shape[0]
    memory_rows = memory[0]
    rep_scalar = rep.reshape(1).astype(jnp.int32)
    bits = jnp.stack([me % 2, (me // 2) % 2, me // 4]).astype(jnp.int32)
    row_of = lambda v: v.reshape(1, -1)
    last = []

    def after(first, *others):
        return lax.optimization_barrier((first, others))[0]

    def run(body, outs, arrays, done=(), **more):
        held = last + list(done)
        if held:
            arrays = [after(arrays[0], *held)] + list(arrays[1:])
        results = local_kernel(body, outs, arrays=arrays, **more)
        last[:] = results[:1]
        return results

    def hop(array, stream_flip=0, rep_flip=0):
        pairs = [
            (s * reps + r, (s ^ stream_flip) * reps + (r ^ rep_flip))
            for s in range(streams)
            for r in range(reps)
        ]
        return lax.ppermute(array, AXES, pairs)

    def stream_along(array):
        return [hop(array, k) for k in (2, 4, 6)]

    def stream_across(array, near):
        near = jnp.stack([array] + near)
        return [near, hop(near, 1)]

    def rep_full(array):
        far = hop(array, 0, 2)
        return [array, hop(array, 0, 1), far, hop(far, 0, 1)]

    def rep_each(parts):
        return [parts[0]] + [hop(parts[k], 0, k) for k in range(1, 4)]

    (parcels_out,) = run(
        deal_blocks,
        [like((streams, 2 * BLK + 16, width), BF)],
        [memory_rows],
        scalars=[routes],
    )
    parcels = lax.all_to_all(parcels_out, "stream", split_axis=0, concat_axis=0, tiled=True)
    joined, r1, h1, qc, turned1 = run(
        self_forward,
        [
            like((rows, 3 * width), BF),
            like((rows, width), F32),
            like((rows, width), BF),
            like((rows, width), BF),
            like((3 * width, rows), BF),
        ],
        [tokens, w_self, w_self_out, w_cross_q, row_of(gain_one), row_of(shift_one)],
        cost=5,
    )
    early = rep_full(turned1)
    kv_own, memory_turned = run(
        own_keys,
        [like((memory_rows.shape[0], 2 * width), BF), like(memory_rows.shape[::-1], BF)],
        [memory_rows, w_cross_kv],
        cost=6,
    )
    keys = streams * 2 * BLK
    o2, kv, sums = run(
        cross_forward,
        [like((rows, width), BF), like((keys, 2 * width), BF), like((2 * rows, LANES), F32)],
        [qc, parcels, w_cross_kv],
        done=early,
        scratch=[
            pltpu.VMEM((2 * rows, keys), F32),
            pltpu.VMEM((2 * rows, keys), BF),
            pltpu.VMEM((8, keys), F32),
        ],
        cost=17,
    )

    qc_near = stream_along(after(qc, parcels))
    qc_all = stream_across(qc, qc_near)

    vec = jnp.concatenate([row_of(v) for v in (gain_two, shift_two, gain_three, shift_three)])
    each = 2 * quarter + share
    layer_out, dr2, do2, sums2, small_ff, small_up, *parts = run(
        feed_forward,
        [
            like((rows, width), BF),
            like((rows, width), F32),
            like((rows + 16, width), BF),
            like((2 * rows, LANES), F32),
            like((8, width), F32),
            like((1, hidden), F32),
        ]
        + [like((each + base, rows), BF) for base in (0, 3 * width, 3 * width, 0)],
        [
            o2, h1, sums, w_cross_out, w_up, w_down, row_of(b_up), row_of(b_down), vec,
            cotangent[0],
        ],
        done=qc_near,
        scalars=[rep_scalar],
        scratch=[
            pltpu.VMEM((rows, hidden), F32),
            pltpu.VMEM((hidden, rows), BF),
            pltpu.VMEM((hidden, rows), BF),
        ],
        cost=12,
    )
    far = hop(parts[2], 0, 2)
    do2_near = stream_along(do2)

    (dqc,) = run(
        cross_backward,
        [like((rows, width), BF)],
        [qc, do2, kv, parcels, sums2],
        scratch=[pltpu.VMEM((8, keys), F32)],
        cost=13,
    )
    near, other = hop(after(parts[1], dqc), 0, 1), hop(after(parts[3], dqc), 0, 3)
    do2_all = stream_across(do2, do2_near)
    d_tokens, small_self, *exports = run(
        self_backward,
        [like((rows, width), F32), like((8, width), F32)]
        + [like((rows, width + share), BF)] * 4,
        [dqc, dr2, r1, joined, w_cross_q, w_self_out, w_self, row_of(gain_one)],
        done=[qc_all[1]] + do2_near,
        scalars=[rep_scalar],
        scratch=[
            pltpu.VMEM((rows, 3 * width), BF),
            pltpu.VMEM((4, rows, width + share), BF),
        ],
        cost=9,
    )
    grads_all = rep_each(exports)
    far_full = hop(after(far, small_self), 0, 1)

    shared = [parts[1], near, far, far_full, parts[0], other]

    def full_at(row):
        return tuple((a, row) for a in (0, 1, 2, 3))

    def each_at(row):
        return ((4, row), (1, 3 * width + row), (2, 3 * width + row), (5, row))

    def blocks_of(plan, arrays, size, wide, extra=None):
        return run(
            functools.partial(weight_blocks, plan, extra),
            [like((4, size, wide), BF)] * 4,
            arrays,
            scalars=[bits],
            scratch=[
                pltpu.VMEM((width, 4 * rows), BF),
                pltpu.VMEM((4 * rows, width), BF),
                pltpu.VMEM((width, width), F32),
            ],
            cost=5,
        )

    def first_hops(blocks):
        send0, keep0, send1, keep1 = blocks
        return [keep0, hop(send0, 1), keep1, hop(send1, 2)]

    def second_hops(arrays):
        give0, mine0, give1, mine1 = run(
            fold_two,
            [like((2,) + arrays[0].shape[1:], BF)] * 4,
            arrays,
            scalars=[bits],
        )
        return [mine0, hop(give0, 2), mine1, hop(give1, 1)]

    def third_hop(arrays):
        give, mine = run(
            fold_high,
            [like((len(arrays) // 2,) + arrays[0].shape[1:], BF)] * 2,
            arrays,
            scalars=[bits],
        )
        return [mine, hop(give, 4)]

    def last_hops(arrays):
        (piece,) = run(fold_last, [like(arrays[0].shape, BF)], arrays)
        return rep_full(piece)

    def gathered(pieces, plan, shapes):
        return run(
            functools.partial(lay_columns, plan),
            [like(shape, F32) for shape in shapes],
            pieces,
            scalars=[rep_scalar],
            scratch=[pltpu.VMEM((4,) + pieces[0].shape, BF)],
        )

    ff = first_hops(
        blocks_of(
            [
                (full_at(0), each_at(quarter), True, quarter, 0, 0),
                (each_at(0), full_at(2 * width), True, width, 1, 0),
            ],
            shared,
            tall,
            width,
        )
    )

    (dkv,) = run(
        owner_backward,
        [like((memory_rows.shape[0], 2 * width), BF)],
        qc_all + do2_all + [kv_own],
        scalars=[(routes[0] ^ me).astype(jnp.int32)],
        scratch=[
            pltpu.VMEM((streams, PAIRS, 2 * rows, LANES), BF),
            pltpu.VMEM((streams, PAIRS, 2 * rows, LANES), BF),
            pltpu.VMEM((streams, 16, 2 * rows), F32),
        ],
        cost=12,
    )
    ff = second_hops(ff)
    vectors = jnp.concatenate([small_ff[0:5], small_self[0:2]]).reshape(7, streams, tall)
    vectors = jnp.pad(vectors.transpose(1, 0, 2), ((0, 0), (0, 0), (0, LANES - tall)))
    vectors = jnp.concatenate(
        [
            vectors,
            small_up.reshape(streams, -1, LANES),
            jnp.zeros((streams, 9 - hidden // streams // LANES, LANES), F32),
        ],
        axis=1,
    )
    own = len(shared)
    early_at = lambda row: tuple((own + k, row) for k in range(4))
    grads_at = lambda col: tuple((own + 4 + k, col) for k in range(4))
    rest = first_hops(
        blocks_of(
            [
                (early_at(0), grads_at(0), False, 3 * share, 0, 0),
                (early_at(width), grads_at(3 * share), False, share, 1, 0),
                (early_at(2 * width), grads_at(4 * share), False, share, 1, share),
                (full_at(width), each_at(2 * quarter), True, share, 1, 2 * share),
            ],
            shared + early + grads_all + [vectors],
            tall + 16,
            3 * share,
            own + 8,
        )
    )
    ff = third_hop(ff)
    kv_wide = 2 * width // 4
    kv_keep, kv_send = run(
        memory_weights,
        [like((2, width, kv_wide), BF)] * 2,
        [dkv, memory_turned],
        scalars=[rep_scalar],
        cost=7,
    )
    kv_core = hop(kv_send, 0, 1)
    (d_memory,) = run(
        memory_backward,
        [like(memory_rows.shape, BF)],
        [dkv, w_cross_kv],
        cost=6,
    )
    near_sum, far_sum = run(
        fold_core,
        [like((width, kv_wide), F32), like((width, kv_wide), BF)],
        [kv_keep, kv_core],
    )
    kv_far = hop(far_sum, 0, 2)
    rest = second_hops(rest)
    ff = last_hops(ff)
    send, keep = run(
        fold_rep,
        [like((4, tall, kv_wide), BF)] * 2,
        [near_sum, kv_far],
        scalars=[bits],
    )
    kv_part = [keep, hop(send, 1)]
    rest = third_hop(rest)
    give, mine = run(
        fold_one, [like((2, tall, kv_wide), BF)] * 2, kv_part, scalars=[bits]
    )
    kv_part = [mine, hop(give, 2)]
    g_up, g_down = gathered(
        ff,
        [(0, 0, quarter, "side"), (1, 0, width, "below")],
        [(tall, hidden), (hidden // streams, width)],
    )
    kv_part = third_hop(kv_part)
    rest = last_hops(rest)
    kv_part = last_hops(kv_part)
    g_self, g_self_out, g_query, g_out, g_vec = gathered(
        rest,
        [
            (0, 0, 3 * share, "side"),
            (1, 0, share, "side"),
            (1, share, share, "side"),
            (1, 2 * share, share, "side"),
            (0, 0, LANES, "sum"),
        ],
        [(tall, 3 * width), (tall, width), (tall, width), (tall, width), (16, LANES)],
    )
    (g_kv,) = gathered(kv_part, [(0, 0, kv_wide, "side")], [(tall, 2 * width)])
    piece = lambda row: g_vec[row, 0:tall]
    d_b_up = g_vec[7 : 7 + hidden // streams // LANES].reshape(-1)
    return (
        layer_out[None],
        d_tokens[None],
        d_memory[None],
        g_self,
        g_self_out,
        g_query,
        g_kv,
        g_out,
        g_up,
        d_b_up,
        g_down,
        piece(0),
        piece(5),
        piece(6),
        piece(1),
        piece(2),
        piece(3),
        piece(4),
    )


def solution(mesh):
    in_specs = (
        P("rep", "stream", None),
        P("rep", "stream", None),
        P("rep", "stream"),
        P(),
        P(),
        P(),
        P(),
        P(),
        P(),
        P(),
        P(),
        P(),
        P(),
        P(),
        P(),
        P(),
        P(),
        P(),
        P("rep", "stream", None),
    )
    out_specs = (
        P("rep", "stream", None),
        P("rep", "stream", None),
        P("rep", "stream", None),
        P("stream", None),
        P("stream", None),
        P("stream", None),
        P("stream", None),
        P("stream", None),
        P("stream", None),
        P("stream"),
        P("stream", None),
        P("stream"),
        P("stream"),
        P("stream"),
        P("stream"),
        P("stream"),
        P("stream"),
        P("stream"),
    )
    small_slice = (mesh.shape["stream"], mesh.shape["rep"]) == (8, 4)
    return jax.shard_map(
        fast_on_device if small_slice else on_device, mesh=mesh, in_specs=in_specs, out_specs=out_specs, check_vma=False
    )
```

```python
import functools

import jax
import jax.numpy as jnp
from jax import lax
from jax.experimental import pallas as pl
from jax.experimental.pallas import tpu as pltpu
from jax.sharding import PartitionSpec as P

HEADS = 12
HEAD_DIM = 64
BLK = 128


def matmul(left, right):
    return jnp.dot(left, right, preferred_element_type=jnp.float32)


def product_left(left, right):
    return lax.dot_general(
        left, right, (((0,), (0,)), ((), ())), preferred_element_type=jnp.float32
    )


def product_right(left, right):
    return lax.dot_general(
        left, right, (((1,), (1,)), ((), ())), preferred_element_type=jnp.float32
    )


def layer_norm(rows, gain, shift):
    centred = rows - jnp.mean(rows, axis=-1, keepdims=True)
    spread = jnp.mean(centred * centred, axis=-1, keepdims=True)
    return centred * lax.rsqrt(spread + 1e-05) * gain + shift


def split_heads(rows):
    return rows.reshape(rows.shape[0], HEADS, HEAD_DIM).transpose(1, 0, 2)


def join_heads(rows):
    return rows.transpose(1, 0, 2).reshape(rows.shape[1], HEADS * HEAD_DIM)


def masked_scores(query_head, key_head, key_ok):
    scores = product_right(query_head, key_head) * HEAD_DIM ** (-0.5)
    if key_ok is not None:
        scores = jnp.where(key_ok[None, :], scores, -1e30)
    return scores


def attend_forward(query, key_rows, value_rows, key_ok):

    def one_head(item):
        query_head, key_head, value_head = item
        scores = masked_scores(query_head, key_head, key_ok)
        row_max = jnp.max(scores, axis=1, keepdims=True)
        exponent = jnp.exp(scores - row_max)
        row_total = jnp.sum(exponent, axis=1, keepdims=True)
        probability = (exponent / row_total).astype(jnp.bfloat16)
        return (matmul(probability, value_head), (row_max + jnp.log(row_total))[:, 0])

    mixed, log_total = lax.map(
        one_head, (split_heads(query), split_heads(key_rows), split_heads(value_rows))
    )
    return (join_heads(mixed), log_total)


def attend_backward(query, key_rows, value_rows, key_ok, log_total, d_mixed):
    factor = HEAD_DIM ** (-0.5)

    def one_head(item):
        query_head, key_head, value_head, total_head, grad_head = item
        scores = masked_scores(query_head, key_head, key_ok)
        probability = jnp.exp(scores - total_head[:, None])
        d_prob = product_right(grad_head, value_head)
        d_scores = probability * (d_prob - jnp.sum(d_prob * probability, axis=1, keepdims=True))
        d_scores = d_scores.astype(jnp.bfloat16)
        d_query = matmul(d_scores, key_head) * factor
        d_key = product_left(d_scores, query_head) * factor
        d_value = product_left(probability.astype(jnp.bfloat16), grad_head)
        return (d_query, d_key, d_value)

    d_query, d_key, d_value = lax.map(
        one_head,
        (
            split_heads(query),
            split_heads(key_rows),
            split_heads(value_rows),
            log_total,
            split_heads(d_mixed),
        ),
    )
    return (join_heads(d_query), join_heads(d_key), join_heads(d_value))


def on_device(
    queries,
    memory,
    routes,
    w_self,
    w_self_out,
    w_cross_q,
    w_cross_kv,
    w_cross_out,
    w_up,
    b_up,
    w_down,
    b_down,
    gain_one,
    shift_one,
    gain_two,
    shift_two,
    gain_three,
    shift_three,
    cotangent,
):
    streams = lax.axis_size("stream")
    blocks = routes.shape[1]
    capacity = max(2, 2 * blocks // streams)
    slot_count = streams * capacity
    model_width = w_self_out.shape[0]
    target = routes[0]
    hit_table = (target[:, None] == jnp.arange(streams, dtype=jnp.int32)[None, :]).astype(jnp.int32)
    before = jnp.cumsum(hit_table, axis=0) - hit_table
    rank_in = jnp.sum(before * hit_table, axis=1)
    slot_of_block = target * capacity + rank_in
    matched = (slot_of_block[None, :] == jnp.arange(slot_count, dtype=jnp.int32)[:, None]).astype(
        jnp.int32
    )
    block_at = jnp.sum(matched * jnp.arange(blocks, dtype=jnp.int32)[None, :], axis=1)
    live_slot = jnp.sum(matched, axis=1)
    live_grid = live_slot.reshape(streams, capacity)
    filled = (live_slot > 0)[:, None, None]
    nothing = jnp.zeros((), jnp.bfloat16)
    memory_rows = memory[0]
    projected = (
        matmul(memory_rows, w_cross_kv).astype(jnp.bfloat16).reshape(blocks, BLK, 2 * model_width)
    )
    outgoing = jnp.where(filled, jnp.take(projected, block_at, axis=0), nothing)
    arrived, arrived_live = (
        lax.all_to_all(
            outgoing.reshape(streams, capacity, BLK, 2 * model_width),
            "stream",
            split_axis=0,
            concat_axis=0,
            tiled=True,
        ),
        lax.all_to_all(live_grid, "stream", split_axis=0, concat_axis=0, tiled=True),
    )
    keys_values = arrived.reshape(-1, 2 * model_width)
    key_ok = jnp.repeat(arrived_live.reshape(-1), BLK) > 0
    key_cross = keys_values[:, :model_width]
    value_cross = keys_values[:, model_width:]
    gain_a = gain_one.astype(jnp.float32)
    shift_a = shift_one.astype(jnp.float32)
    gain_b = gain_two.astype(jnp.float32)
    shift_b = shift_two.astype(jnp.float32)
    gain_c = gain_three.astype(jnp.float32)
    shift_c = shift_three.astype(jnp.float32)
    tokens = queries[0]
    joined = matmul(tokens, w_self).astype(jnp.bfloat16)
    query_self = joined[:, :model_width]
    key_self = joined[:, model_width : 2 * model_width]
    value_self = joined[:, 2 * model_width :]
    mixed_self, total_self = attend_forward(query_self, key_self, value_self, None)
    mixed_self = mixed_self.astype(jnp.bfloat16)
    residual_one = tokens.astype(jnp.float32) + matmul(mixed_self, w_self_out)
    normed_one = layer_norm(residual_one, gain_a, shift_a).astype(jnp.bfloat16)
    query_cross = matmul(normed_one, w_cross_q).astype(jnp.bfloat16)
    mixed_cross, total_cross = attend_forward(query_cross, key_cross, value_cross, key_ok)
    mixed_cross = mixed_cross.astype(jnp.bfloat16)
    residual_two = normed_one.astype(jnp.float32) + matmul(mixed_cross, w_cross_out)
    normed_two = layer_norm(residual_two, gain_b, shift_b).astype(jnp.bfloat16)
    hidden_pre = matmul(normed_two, w_up) + b_up.astype(jnp.float32)
    hidden = jax.nn.gelu(hidden_pre, approximate=False).astype(jnp.bfloat16)
    residual_three = (
        normed_two.astype(jnp.float32) + matmul(hidden, w_down) + b_down.astype(jnp.float32)
    )
    layer_out = layer_norm(residual_three, gain_c, shift_c).astype(jnp.bfloat16)
    grad_out = cotangent[0].astype(jnp.float32)
    norm_three_pull = jax.vjp(layer_norm, residual_three, gain_c, shift_c)[1]
    d_residual_three, d_gain_c, d_shift_c = norm_three_pull(grad_out)
    d_branch_three = d_residual_three.astype(jnp.bfloat16)
    d_b_down = jnp.sum(d_branch_three.astype(jnp.float32), axis=0)
    d_w_down = product_left(hidden, d_branch_three)
    d_hidden = product_right(d_branch_three, w_down)
    gelu_pull = jax.vjp(lambda value: jax.nn.gelu(value, approximate=False), hidden_pre)[1]
    d_hidden_pre = gelu_pull(d_hidden)[0].astype(jnp.bfloat16)
    d_b_up = jnp.sum(d_hidden_pre.astype(jnp.float32), axis=0)
    d_w_up = product_left(normed_two, d_hidden_pre)
    d_normed_two = d_residual_three + product_right(d_hidden_pre, w_up)
    norm_two_pull = jax.vjp(layer_norm, residual_two, gain_b, shift_b)[1]
    d_residual_two, d_gain_b, d_shift_b = norm_two_pull(d_normed_two)
    d_branch_two = d_residual_two.astype(jnp.bfloat16)
    d_w_cross_out = product_left(mixed_cross, d_branch_two)
    d_mixed_cross = product_right(d_branch_two, w_cross_out).astype(jnp.bfloat16)
    d_query_cross, d_key_cross, d_value_cross = attend_backward(
        query_cross, key_cross, value_cross, key_ok, total_cross, d_mixed_cross
    )
    d_query_cross = d_query_cross.astype(jnp.bfloat16)
    d_keys_values = jnp.concatenate([d_key_cross, d_value_cross], axis=1).astype(jnp.bfloat16)
    d_w_cross_q = product_left(normed_one, d_query_cross)
    d_normed_one = d_residual_two + product_right(d_query_cross, w_cross_q)
    norm_one_pull = jax.vjp(layer_norm, residual_one, gain_a, shift_a)[1]
    d_residual_one, d_gain_a, d_shift_a = norm_one_pull(d_normed_one)
    d_branch_one = d_residual_one.astype(jnp.bfloat16)
    d_w_self_out = product_left(mixed_self, d_branch_one)
    d_mixed_self = product_right(d_branch_one, w_self_out).astype(jnp.bfloat16)
    d_query_self, d_key_self, d_value_self = attend_backward(
        query_self, key_self, value_self, None, total_self, d_mixed_self
    )
    d_joined = jnp.concatenate([d_query_self, d_key_self, d_value_self], axis=1).astype(
        jnp.bfloat16
    )
    d_w_self = product_left(tokens, d_joined)
    d_tokens = d_residual_one + product_right(d_joined, w_self)
    returned = lax.all_to_all(
        d_keys_values.reshape(streams, capacity, BLK, 2 * model_width),
        "stream",
        split_axis=0,
        concat_axis=0,
        tiled=True,
    )
    d_block_rows = jnp.take(
        returned.reshape(slot_count, BLK, 2 * model_width), slot_of_block, axis=0
    ).reshape(-1, 2 * model_width)
    d_w_cross_kv = product_left(memory_rows, d_block_rows)
    d_memory = product_right(d_block_rows, w_cross_kv).astype(jnp.bfloat16)
    gradients = (
        d_w_self,
        d_w_self_out,
        d_w_cross_q,
        d_w_cross_kv,
        d_w_cross_out,
        d_w_up,
        d_b_up,
        d_w_down,
        d_b_down,
        d_gain_a,
        d_shift_a,
        d_gain_b,
        d_shift_b,
        d_gain_c,
        d_shift_c,
    )
    shapes = [item.shape for item in gradients]
    flat = [item.reshape(-1) for item in gradients]
    (
        share_self,
        share_self_out,
        share_cross_q,
        share_cross_kv,
        share_cross_out,
        share_up,
        share_b_up,
        share_down,
        share_b_down,
        share_gain_a,
        share_shift_a,
        share_gain_b,
        share_shift_b,
        share_gain_c,
        share_shift_c,
    ) = (
        lax.psum_scatter(flat[0], "stream", scatter_dimension=0, tiled=True),
        lax.psum_scatter(flat[1], "stream", scatter_dimension=0, tiled=True),
        lax.psum_scatter(flat[2], "stream", scatter_dimension=0, tiled=True),
        lax.psum_scatter(flat[3], "stream", scatter_dimension=0, tiled=True),
        lax.psum_scatter(flat[4], "stream", scatter_dimension=0, tiled=True),
        lax.psum_scatter(flat[5], "stream", scatter_dimension=0, tiled=True),
        lax.psum_scatter(flat[6], "stream", scatter_dimension=0, tiled=True),
        lax.psum_scatter(flat[7], "stream", scatter_dimension=0, tiled=True),
        lax.psum_scatter(flat[8], "stream", scatter_dimension=0, tiled=True),
        lax.psum_scatter(flat[9], "stream", scatter_dimension=0, tiled=True),
        lax.psum_scatter(flat[10], "stream", scatter_dimension=0, tiled=True),
        lax.psum_scatter(flat[11], "stream", scatter_dimension=0, tiled=True),
        lax.psum_scatter(flat[12], "stream", scatter_dimension=0, tiled=True),
        lax.psum_scatter(flat[13], "stream", scatter_dimension=0, tiled=True),
        lax.psum_scatter(flat[14], "stream", scatter_dimension=0, tiled=True),
    )
    summed = (
        lax.psum(share_self.astype(jnp.bfloat16), "rep").astype(jnp.float32),
        lax.psum(share_self_out.astype(jnp.bfloat16), "rep").astype(jnp.float32),
        lax.psum(share_cross_q.astype(jnp.bfloat16), "rep").astype(jnp.float32),
        lax.psum(share_cross_kv.astype(jnp.bfloat16), "rep").astype(jnp.float32),
        lax.psum(share_cross_out.astype(jnp.bfloat16), "rep").astype(jnp.float32),
        lax.psum(share_up.astype(jnp.bfloat16), "rep").astype(jnp.float32),
        lax.psum(share_b_up.astype(jnp.bfloat16), "rep").astype(jnp.float32),
        lax.psum(share_down.astype(jnp.bfloat16), "rep").astype(jnp.float32),
        lax.psum(share_b_down.astype(jnp.bfloat16), "rep").astype(jnp.float32),
        lax.psum(share_gain_a.astype(jnp.bfloat16), "rep").astype(jnp.float32),
        lax.psum(share_shift_a.astype(jnp.bfloat16), "rep").astype(jnp.float32),
        lax.psum(share_gain_b.astype(jnp.bfloat16), "rep").astype(jnp.float32),
        lax.psum(share_shift_b.astype(jnp.bfloat16), "rep").astype(jnp.float32),
        lax.psum(share_gain_c.astype(jnp.bfloat16), "rep").astype(jnp.float32),
        lax.psum(share_shift_c.astype(jnp.bfloat16), "rep").astype(jnp.float32),
    )
    results = [
        part.reshape((shape[0] // streams,) + tuple(shape[1:]))
        for part, shape in zip(summed, shapes)
    ]
    return (
        layer_out[None],
        d_tokens[None],
        d_memory[None],
        results[0],
        results[1],
        results[2],
        results[3],
        results[4],
        results[5],
        results[6],
        results[7],
        results[8],
        results[9],
        results[10],
        results[11],
        results[12],
        results[13],
        results[14],
    )


PAIRS = HEADS // 2
LANES = 2 * HEAD_DIM
FACTOR = HEAD_DIM ** (-0.5)
BF = jnp.bfloat16
F32 = jnp.float32
AXES = ("stream", "rep")


def whole_in_vmem(count):
    return [pl.BlockSpec(memory_space=pltpu.VMEM)] * count


def local_kernel(body, out_shape, scalars=(), arrays=(), scratch=(), cost=2, limit=24):
    return pl.pallas_call(
        body,
        out_shape=list(out_shape),
        in_specs=[pl.BlockSpec(memory_space=pltpu.SMEM)] * len(scalars) + whole_in_vmem(len(arrays)),
        out_specs=whole_in_vmem(len(out_shape)),
        scratch_shapes=list(scratch),
        compiler_params=pltpu.CompilerParams(vmem_limit_bytes=limit * 1024 * 1024),
        cost_estimate=pl.CostEstimate(
            flops=int(cost * 1.15e9), bytes_accessed=int(cost * 1e5), transcendentals=0
        ),
    )(*scalars, *arrays)


def like(shape, dtype):
    return jax.ShapeDtypeStruct(shape, dtype)


def dot_nn(left, right):
    return lax.dot_general(left, right, (((1,), (0,)), ((), ())), preferred_element_type=F32)


def dot_nt(left, right):
    return lax.dot_general(left, right, (((1,), (1,)), ((), ())), preferred_element_type=F32)


def head_masks(rows):
    lane = lax.broadcasted_iota(jnp.int32, (rows, LANES), 1)
    return lane < HEAD_DIM


def stack_heads(pair, first, scale):
    one = jnp.where(first, scale, 0.0).astype(BF)
    two = jnp.where(first, 0.0, scale).astype(BF)
    return jnp.concatenate([pair * one, pair * two], axis=0)


def unstack_heads(both, first):
    rows = both.shape[0] // 2
    return jnp.where(first, both[:rows], both[rows:])


def norm_parts(rows):
    centred = rows - jnp.mean(rows, axis=1, keepdims=True)
    spread = jnp.mean(centred * centred, axis=1, keepdims=True)
    inverse = lax.rsqrt(spread + 1e-05)
    return centred * inverse, inverse


def norm_pull(grad, hat, inverse, gain):
    scaled = grad * gain
    inner = scaled - jnp.mean(scaled, axis=1, keepdims=True)
    inner = inner - hat * jnp.mean(scaled * hat, axis=1, keepdims=True)
    return (
        inverse * inner,
        jnp.sum(grad * hat, axis=0, keepdims=True),
        jnp.sum(grad, axis=0, keepdims=True),
    )


def deal_blocks(routes_ref, memory_ref, out_ref):
    out_ref[...] = jnp.zeros_like(out_ref)
    blocks = memory_ref.shape[0] // BLK
    for b in range(blocks):
        group = routes_ref[0, b]
        rank = jnp.int32(0)
        for earlier in range(b):
            rank = rank + (routes_ref[0, earlier] == group).astype(jnp.int32)
        row = pl.multiple_of(rank * BLK, BLK)
        out_ref[group, pl.ds(row, BLK), :] = memory_ref[b * BLK : (b + 1) * BLK, :]


def self_forward(tok, w_in, w_out, w_q, gain, shift, joined, r1, h1_out, qc, turned):
    width = tok.shape[1]
    rows = tok.shape[0]
    joined[...] = dot_nn(tok[...], w_in[...]).astype(BF)
    first = head_masks(rows)
    mixed = []
    for j in range(PAIRS):
        at = j * LANES
        q2 = stack_heads(joined[:, at : at + LANES], first, FACTOR)
        key = joined[:, width + at : width + at + LANES]
        value = joined[:, 2 * width + at : 2 * width + at + LANES]
        scores = dot_nt(q2, key)
        power = jnp.exp(scores - jnp.max(scores, axis=1, keepdims=True))
        prob = (power / jnp.sum(power, axis=1, keepdims=True)).astype(BF)
        mixed.append(unstack_heads(dot_nn(prob, value), first).astype(BF))
    o1 = jnp.concatenate(mixed, axis=1)
    res = tok[...].astype(F32) + dot_nn(o1, w_out[...])
    r1[...] = res
    hat, _ = norm_parts(res)
    h1 = (hat * gain[...].astype(F32) + shift[...].astype(F32)).astype(BF)
    h1_out[...] = h1
    qc[...] = dot_nn(h1, w_q[...]).astype(BF)
    turned[0:width, :] = tok[...].T
    turned[width : 2 * width, :] = o1.T
    turned[2 * width : 3 * width, :] = h1.T


def cross_forward(routes_ref, me_ref, qc, parcels, w_kv, o2, kv, sums, bias_ref, s_ref, p_ref):
    width = qc.shape[1]
    rows = qc.shape[0]
    sources = parcels.shape[0]
    span = 2 * BLK
    first = head_masks(rows)
    for k in range(sources):
        kv[k * span : (k + 1) * span, :] = dot_nn(parcels[k, 0:span, :], w_kv[...]).astype(BF)
        count = jnp.int32(0)
        for b in range(routes_ref.shape[1]):
            count = count + (routes_ref[k, b] == me_ref[0]).astype(jnp.int32)
        for c in range(2):
            bias_ref[:, k * span + c * BLK : k * span + (c + 1) * BLK] = jnp.full(
                (8, BLK), jnp.where(count > c, 0.0, -1e30), F32
            )
    lane = lax.broadcasted_iota(jnp.int32, (2 * rows, LANES), 1)
    sums[...] = jnp.zeros_like(sums)

    def one_pair(j, carry):
        at = pl.multiple_of(j * LANES, LANES)
        q2 = stack_heads(qc[:, pl.ds(at, LANES)], first, FACTOR)
        top = None
        for k in range(sources):
            key = kv[k * span : (k + 1) * span, pl.ds(at, LANES)]
            scores = dot_nt(q2, key) + bias_ref[0:1, k * span : (k + 1) * span]
            s_ref[:, k * span : (k + 1) * span] = scores
            most = jnp.maximum(scores[:, :LANES], scores[:, LANES:])
            top = most if top is None else jnp.maximum(top, most)
        peak = jnp.max(top, axis=1, keepdims=True)
        total = None
        for k in range(sources):
            power = jnp.exp(s_ref[:, k * span : (k + 1) * span] - peak)
            p_ref[:, k * span : (k + 1) * span] = power.astype(BF)
            part = power[:, :LANES] + power[:, LANES:]
            total = part if total is None else total + part
        total = jnp.sum(total, axis=1, keepdims=True)
        value = kv[:, pl.ds(pl.multiple_of(width + j * LANES, LANES), LANES)]
        both = dot_nn(p_ref[...], value) / total
        o2[:, pl.ds(at, LANES)] = unstack_heads(both, first).astype(BF)
        sums[...] = jnp.where(lane == j, peak + jnp.log(total), sums[...])
        return carry

    lax.fori_loop(0, PAIRS, one_pair, 0, unroll=PAIRS)


def feed_forward(
    rep_ref, o2, tok_h1, sums, w_co, w_up, w_down, b_up, b_down, vec, cot,
    layer_out, dr2, do2, both_sums, small, small_up, parcel0, parcel1, parcel2,
    slope, acts, dus,
):
    width = o2.shape[1]
    rows = o2.shape[0]
    hidden = w_up.shape[1]
    quarter = hidden // 4
    rep = rep_ref[0]
    gain2, shift2, gain3, shift3 = (vec[i : i + 1, :].astype(F32) for i in range(4))
    res2 = tok_h1[...].astype(F32) + dot_nn(o2[...], w_co[...])
    hat2, inv2 = norm_parts(res2)
    h2 = (hat2 * gain2 + shift2).astype(BF)
    each = 2 * quarter + width // 4
    for parcel, base in ((parcel1, 0), (parcel2, each)):
        parcel[base : base + width, :] = h2.T
        parcel[base + width : base + 2 * width, :] = o2[...].T
    total = None
    for c in range(4):
        cols = slice(c * quarter, (c + 1) * quarter)
        u = dot_nn(h2, w_up[:, cols]) + b_up[:, cols].astype(F32)
        cdf = 0.5 + 0.5 * lax.erf(u * 0.7071067811865476)
        act = (u * cdf).astype(BF)
        slope[:, cols] = cdf + u * (jnp.exp(u * u * -0.5) * 0.3989422804014327)
        acts[cols, :] = act.T
        part = dot_nn(act, w_down[cols, :])
        total = part if total is None else total + part
    res3 = h2.astype(F32) + total + b_down[...].astype(F32)
    hat3, inv3 = norm_parts(res3)
    layer_out[...] = (hat3 * gain3 + shift3).astype(BF)
    dr3, d_gain3, d_shift3 = norm_pull(cot[...].astype(F32), hat3, inv3, gain3)
    dy3 = dr3.astype(BF)
    small[0:1, :] = jnp.sum(dy3.astype(F32), axis=0, keepdims=True)
    small[3:4, :] = d_gain3
    small[4:5, :] = d_shift3
    back = None
    for c in range(4):
        cols = slice(c * quarter, (c + 1) * quarter)
        du = (dot_nt(dy3, w_down[cols, :]) * slope[:, cols]).astype(BF)
        small_up[:, cols] = jnp.sum(du.astype(F32), axis=0, keepdims=True)
        dus[cols, :] = du.T
        part = dot_nt(du, w_up[:, cols])
        back = part if back is None else back + part
    grad2, d_gain2, d_shift2 = norm_pull(dr3 + back, hat2, inv2, gain2)
    small[1:2, :] = d_gain2
    small[2:3, :] = d_shift2
    small[5:8, :] = jnp.zeros((3, width), F32)
    dr2[...] = grad2
    dy2 = grad2.astype(BF)
    grad_mixed = dot_nt(dy2, w_co[...]).astype(BF)
    do2[0:rows, :] = grad_mixed
    lane = lax.broadcasted_iota(jnp.int32, (2 * rows, LANES), 1)
    first = head_masks(rows)
    packed = sums[...]
    for j in range(PAIRS):
        at = slice(j * LANES, (j + 1) * LANES)
        prod = grad_mixed[:, at].astype(F32) * o2[:, at].astype(F32)
        zero = jnp.zeros_like(prod)
        two = jnp.concatenate([jnp.where(first, prod, zero), jnp.where(first, zero, prod)], axis=0)
        packed = jnp.where(lane == 8 + j, jnp.sum(two, axis=1, keepdims=True), packed)
    both_sums[...] = packed
    turned = packed.T[0:16, :]
    high = turned.astype(BF)
    rest = turned - high.astype(F32)
    middle = rest.astype(BF)
    low = (rest - middle.astype(F32)).astype(BF)
    do2[rows : rows + 16, :] = jnp.concatenate([high, middle, low], axis=1)
    share = width // 4
    dy2_turned = dy2.T
    dy3_turned = dy3.T
    strip = quarter // 8
    parcel1[2 * width : 3 * width, :] = dy3_turned
    parcel2[each + 2 * width : each + 3 * width, :] = dy3_turned
    places = ((parcel0, 0), (parcel1, 3 * width), (parcel2, 0), (parcel2, each + 3 * width))
    for k, (parcel, base) in enumerate(places):
        peer = rep ^ k
        for s in range(8):
            row = pl.multiple_of(s * 4 * strip + peer * strip, strip)
            parcel[base + s * strip : base + (s + 1) * strip, :] = acts[pl.ds(row, strip), :]
        row = pl.multiple_of(peer * quarter, quarter)
        parcel[base + quarter : base + 2 * quarter, :] = dus[pl.ds(row, quarter), :]
        piece = dy2_turned[0:share]
        for i in range(1, 4):
            piece = jnp.where(peer == i, dy2_turned[i * share : (i + 1) * share], piece)
        parcel[base + 2 * quarter : base + 2 * quarter + share, :] = piece


def cross_backward(qc, do2, kv, bias_ref, sums, dqc):
    width = qc.shape[1]
    rows = qc.shape[0]
    span = 2 * BLK
    sources = kv.shape[0] // span
    first = head_masks(rows)
    lane = lax.broadcasted_iota(jnp.int32, (2 * rows, LANES), 1)

    def one_pair(j, carry):
        at = pl.multiple_of(j * LANES, LANES)
        q2 = stack_heads(qc[:, pl.ds(at, LANES)], first, FACTOR)
        g2 = stack_heads(do2[0:rows, pl.ds(at, LANES)], first, 1.0)
        packed = sums[...]
        log_sum = jnp.sum(jnp.where(lane == j, packed, 0.0), axis=1, keepdims=True)
        delta = jnp.sum(jnp.where(lane == j + 8, packed, 0.0), axis=1, keepdims=True)
        total = None
        for k in range(sources):
            key = kv[k * span : (k + 1) * span, pl.ds(at, LANES)]
            value = kv[
                k * span : (k + 1) * span, pl.ds(pl.multiple_of(width + j * LANES, LANES), LANES)
            ]
            scores = dot_nt(q2, key) + bias_ref[0:1, k * span : (k + 1) * span]
            prob = jnp.exp(scores - log_sum)
            grad = (prob * (dot_nt(g2, value) - delta)).astype(BF)
            part = dot_nn(grad, key)
            total = part if total is None else total + part
        dqc[:, pl.ds(at, LANES)] = (unstack_heads(total, first) * FACTOR).astype(BF)
        return carry

    lax.fori_loop(0, PAIRS, one_pair, 0, unroll=PAIRS)


def self_backward(
    rep_ref, dqc_ref, dr2, r1, joined, w_q, w_out, w_in, gain,
    d_tok, small, out0, out1, out2, out3,
    da_ref, quarters,
):
    rows, width = dqc_ref.shape
    rep = rep_ref[0]
    first = head_masks(rows)
    dqc = dqc_ref[...]
    grad1 = dr2[...] + dot_nt(dqc, w_q[...])
    hat1, inv1 = norm_parts(r1[...])
    dr1, d_gain1, d_shift1 = norm_pull(grad1, hat1, inv1, gain[...].astype(F32))
    small[0:1, :] = d_gain1
    small[1:2, :] = d_shift1
    small[2:8, :] = jnp.zeros((6, width), F32)
    dy1 = dr1.astype(BF)
    do1 = dot_nt(dy1, w_out[...]).astype(BF)
    for j in range(PAIRS):
        at = slice(j * LANES, (j + 1) * LANES)
        key_at = slice(width + j * LANES, width + (j + 1) * LANES)
        value_at = slice(2 * width + j * LANES, 2 * width + (j + 1) * LANES)
        q2 = stack_heads(joined[:, at], first, FACTOR)
        g2 = stack_heads(do1[:, at], first, 1.0)
        key, value = joined[:, key_at], joined[:, value_at]
        scores = dot_nt(q2, key)
        power = jnp.exp(scores - jnp.max(scores, axis=1, keepdims=True))
        prob = power / jnp.sum(power, axis=1, keepdims=True)
        d_prob = dot_nt(g2, value)
        d_scores = (prob * (d_prob - jnp.sum(d_prob * prob, axis=1, keepdims=True))).astype(BF)
        da_ref[:, at] = (unstack_heads(dot_nn(d_scores, key), first) * FACTOR).astype(BF)
        da_ref[:, key_at] = product_left(d_scores, q2).astype(BF)
        da_ref[:, value_at] = product_left(prob.astype(BF), g2).astype(BF)
    d_tok[...] = dr1 + dot_nt(da_ref[...], w_in[...])
    third = 3 * width // 4
    share = width // 4
    da = da_ref[...]
    for i in range(4):
        quarters[i, :, 0:third] = da[:, i * third : (i + 1) * third]
        quarters[i, :, third : third + share] = dy1[:, i * share : (i + 1) * share]
        quarters[i, :, width : width + share] = dqc[:, i * share : (i + 1) * share]
    for k, out in enumerate((out0, out1, out2, out3)):
        out[...] = quarters[rep ^ k]


def owner_backward(where_ref, *refs):
    groups = 8
    qc_near, qc_far, do_near, do_far, kv, dkv, q_ref, g_ref, sum_ref = refs
    _, rows, width = qc_near.shape
    first = head_masks(rows)
    for k in range(groups):
        query = (qc_far if k % 2 else qc_near)[k // 2]
        extra = (do_far if k % 2 else do_near)[k // 2]
        sums = extra[rows : rows + 16, :].astype(F32)
        third = width // 3
        sum_ref[k] = sums[:, 0:third] + sums[:, third : 2 * third] + sums[:, 2 * third :]
        for j in range(PAIRS):
            at = slice(j * LANES, (j + 1) * LANES)
            q_ref[k, j] = stack_heads(query[:, at], first, FACTOR)
            g_ref[k, j] = stack_heads(extra[0:rows, at], first, 1.0)
    blocks = kv.shape[0] // BLK

    def one_block(b, carry):
        group = where_ref[b]
        row = pl.multiple_of(b * BLK, BLK)
        for j in range(PAIRS):
            key_at = slice(j * LANES, (j + 1) * LANES)
            value_at = slice(width + j * LANES, width + (j + 1) * LANES)
            key = kv[pl.ds(row, BLK), key_at]
            value = kv[pl.ds(row, BLK), value_at]
            q2 = q_ref[group, j]
            g2 = g_ref[group, j]
            log_sum = sum_ref[group, j : j + 1, :]
            delta = sum_ref[group, 8 + j : 9 + j, :]
            prob = jnp.exp(dot_nt(key, q2) - log_sum)
            grad = (prob * (dot_nt(value, g2) - delta)).astype(BF)
            dkv[pl.ds(row, BLK), key_at] = dot_nn(grad, q2).astype(BF)
            dkv[pl.ds(row, BLK), value_at] = dot_nn(prob.astype(BF), g2).astype(BF)
        return carry

    lax.fori_loop(0, blocks, one_block, 0)


def memory_weights(rep_ref, dkv, memory_turned, keep, send):
    quarter = dkv.shape[1] // 4
    rep = rep_ref[0]
    for k in range(4):
        at = pl.multiple_of((rep ^ k) * quarter, LANES)
        out = (keep, send)[k % 2]
        out[k // 2] = dot_nn(memory_turned[...], dkv[:, pl.ds(at, quarter)]).astype(BF)


def memory_backward(dkv, w_kv, d_memory):
    half = dkv.shape[0] // 2
    for i in range(2):
        span = slice(i * half, (i + 1) * half)
        d_memory[span, :] = dot_nt(dkv[span, :], w_kv[...]).astype(BF)


def own_keys(memory_ref, w_kv, kv, turned):
    kv[...] = dot_nn(memory_ref[...], w_kv[...]).astype(BF)
    turned[...] = memory_ref[...].T


def weight_blocks(plan, whole, ready, extra, bits_ref, *refs):
    left_all, right_all, product = refs[-3:]
    count = 5 if whole else 4
    outs, arrays = refs[-3 - count : -3], refs[: -3 - count]
    width, depth = left_all.shape
    rows = depth // 4
    tall = width // 8

    def blocks_of(group):
        bit = bits_ref[group]
        for i in range(4):
            for out, b in ((outs[2 * group], 1 - bit), (outs[2 * group + 1], bit)):
                if group == 0:
                    yield out, i, 2 * i + b
                else:
                    yield out, i, 4 * (i // 2) + 2 * b + i % 2

    def multiply(lefts, rights, turned, cols):
        for k, ((a, row), (g, off)) in enumerate(zip(lefts, rights)):
            span = slice(k * rows, (k + 1) * rows)
            left_all[:, span] = arrays[a][row : row + width, :]
            right = arrays[g][off : off + cols, :].T if turned else arrays[g][:, off : off + cols]
            right_all[span, 0:cols] = right
        return dot_nn(left_all[...], right_all[:, 0:cols])

    for lefts, rights, turned, cols, group, to in plan:
        product[:, 0:cols] = multiply(lefts, rights, turned, cols)
        for out, i, block in blocks_of(group):
            at = pl.multiple_of(block * tall, 16)
            out[i, 0:tall, to : to + cols] = product[pl.ds(at, tall), 0:cols].astype(BF)
    if whole:
        outs[4][...] = multiply(*whole).astype(BF)
    if ready:
        source, group, to = ready
        cols = arrays[source].shape[1]
        for out, i, block in blocks_of(group):
            at = pl.multiple_of(block * tall, 16)
            out[i, 0:tall, to : to + cols] = arrays[source][pl.ds(at, tall), :]
    if extra is not None:
        for group in range(2):
            for out, i, block in blocks_of(group):
                out[i, tall:, :] = jnp.zeros_like(out[i, tall:, :])
                if group == 0:
                    out[i, tall:, 0:LANES] = arrays[extra][block].astype(BF)


def fold_two(bits_ref, kept0, got0, kept1, got1, give0, mine0, give1, mine1):
    for bit, kept, got, give, mine in (
        (bits_ref[1], kept0, got0, give0, mine0),
        (bits_ref[0], kept1, got1, give1, mine1),
    ):
        for i in range(2):
            for out, at in ((give, 2 * i + 1 - bit), (mine, 2 * i + bit)):
                out[i] = (kept[at].astype(F32) + got[at].astype(F32)).astype(BF)


def fold_high(bits_ref, *refs):
    (give, mine), arrays = refs[-2:], refs[:-2]
    bit = bits_ref[2]
    for g in range(len(arrays) // 2):
        kept, got = arrays[2 * g], arrays[2 * g + 1]
        for out, at in ((give, 1 - bit), (mine, bit)):
            out[g] = (kept[at].astype(F32) + got[at].astype(F32)).astype(BF)


def fold_one(bits_ref, kept, got, give, mine):
    bit = bits_ref[1]
    for i in range(2):
        for out, at in ((give, 2 * i + 1 - bit), (mine, 2 * i + bit)):
            out[i] = (kept[at].astype(F32) + got[at].astype(F32)).astype(BF)


def fold_last(kept, got, out):
    out[...] = (kept[...].astype(F32) + got[...].astype(F32)).astype(BF)


def fold_core(kept, got, near, far):
    near[...] = kept[0].astype(F32) + got[0].astype(F32)
    far[...] = (kept[1].astype(F32) + got[1].astype(F32)).astype(BF)


def fold_rep(bits_ref, near, got, send, keep):
    y = bits_ref[0]
    tall = send.shape[1]
    for z in range(4):
        for out, bit in ((send, 1 - y), (keep, y)):
            at = pl.multiple_of((2 * z + bit) * tall, 16)
            out[z] = (near[pl.ds(at, tall), :] + got[pl.ds(at, tall), :].astype(F32)).astype(BF)


def lay_columns(plan, rep_ref, *refs):
    pieces, outs, held = refs[0:4], refs[4:-1], refs[-1]
    rep = rep_ref[0]
    for k in range(4):
        held[k] = pieces[k][...]
    for (group, start, cols, how), out in zip(plan, outs):
        if how == "sum":
            tall = out.shape[0]
            total = None
            for k in range(4):
                part = pieces[k][group, pieces[k].shape[1] - tall :, start : start + cols].astype(F32)
                total = part if total is None else total + part
            out[...] = total
            continue
        tall = out.shape[0] if how == "side" else out.shape[0] // 4
        for q in range(4):
            part = held[rep ^ q, group, 0:tall, start : start + cols].astype(F32)
            if how == "side":
                out[:, q * cols : (q + 1) * cols] = part
            else:
                out[q * tall : (q + 1) * tall, :] = part


ORDER = ('dq', 'self', 'owner', 'ff1', 'kv0', 'rest1', 'kv1', 'ff2', 'memory', 'kv2', 'ff3', 'rest2', 'kv3', 'rest3', 'kv4', 'ff4', 'rest4', 'kv5', 'lay_ff', 'lay_rest', 'lay_kv')
BEFORE = {'cross': ('early',), 'ffn': ('qc_z',), 'self': ('qc_y', 'do_stack'), 'ff1': ('exports',)}
RELAY = ()
COSTS = {'deal': 2, 'self_forward': 5, 'own_keys': 6, 'cross': 17, 'ffn': 12, 'dq': 20, 'self': 12, 'ff1': 5, 'rest1': 5, 'owner': 12, 'kv0': 7, 'memory': 6}
LIMITS = {}


def fast_on_device(
    queries, memory, routes, w_self, w_self_out, w_cross_q, w_cross_kv, w_cross_out, w_up, b_up,
    w_down, b_down, gain_one, shift_one, gain_two, shift_two, gain_three, shift_three, cotangent,
):
    streams, reps = lax.axis_size("stream"), lax.axis_size("rep")
    me, rep = lax.axis_index("stream"), lax.axis_index("rep")
    width = w_self_out.shape[0]
    hidden = w_up.shape[1]
    quarter, share, tall = hidden // 4, width // 4, width // streams
    tokens = queries[0]
    rows = tokens.shape[0]
    memory_rows = memory[0]
    rep_scalar = rep.reshape(1).astype(jnp.int32)
    bits = jnp.stack([me % 2, (me // 2) % 2, me // 4]).astype(jnp.int32)
    row_of = lambda v: v.reshape(1, -1)
    last = []

    def after(first, *others):
        return lax.optimization_barrier((first, others))[0]

    moving = {}

    def run(name, body, outs, arrays, **more):
        held = last + [array for key in BEFORE.get(name, ()) for array in moving[key]]
        if held:
            arrays = [after(arrays[0], *held)] + list(arrays[1:])
        results = local_kernel(body, outs, arrays=arrays, cost=COSTS.get(name, 2), limit=LIMITS.get(name, 24), **more)
        last[:] = results[:1]
        return results

    def hop(array, stream_flip=0, rep_flip=0):
        pairs = [
            (s * reps + r, (s ^ stream_flip) * reps + (r ^ rep_flip))
            for s in range(streams)
            for r in range(reps)
        ]
        return lax.ppermute(array, AXES, pairs)

    def stream_along(array):
        return [hop(array, k) for k in (2, 4, 6)]

    def stream_across(array, near):
        near = jnp.stack([array] + near)
        return [near, hop(near, 1)]

    def rep_full(array):
        far = hop(array, 0, 2)
        return [array, hop(array, 0, 1), far, hop(far, 0, 1)]

    def rep_each(parts):
        return [parts[0]] + [hop(parts[k], 0, k) for k in range(1, 4)]

    (parcels_out,) = run(
        "deal",
        deal_blocks,
        [like((streams, 2 * BLK, width), BF)],
        [memory_rows],
        scalars=[routes],
    )
    parcels = lax.all_to_all(parcels_out, "stream", split_axis=0, concat_axis=0, tiled=True)
    joined, r1, h1, qc, turned1 = run(
        "self_forward",
        self_forward,
        [
            like((rows, 3 * width), BF),
            like((rows, width), F32),
            like((rows, width), BF),
            like((rows, width), BF),
            like((3 * width, rows), BF),
        ],
        [tokens, w_self, w_self_out, w_cross_q, row_of(gain_one), row_of(shift_one)],
    )
    early = rep_full(turned1)
    moving["early"] = early
    kv_own, memory_turned = run(
        "own_keys",
        own_keys,
        [like((memory_rows.shape[0], 2 * width), BF), like(memory_rows.shape[::-1], BF)],
        [memory_rows, w_cross_kv],
    )
    routes_all = lax.all_gather(
        after(routes[0], kv_own, *early), "stream", axis=0, tiled=False
    )
    keys = streams * 2 * BLK
    o2, kv, sums, bias = run(
        "cross",
        cross_forward,
        [
            like((rows, width), BF),
            like((keys, 2 * width), BF),
            like((2 * rows, LANES), F32),
            like((8, keys), F32),
        ],
        [qc, parcels, w_cross_kv],
        scalars=[routes_all, me.reshape(1).astype(jnp.int32)],
        scratch=[pltpu.VMEM((2 * rows, keys), F32), pltpu.VMEM((2 * rows, keys), BF)],
    )
    qc_near = stream_along(after(qc, parcels))
    qc_all = stream_across(qc, qc_near)
    moving["qc_z"], moving["qc_stack"], moving["qc_y"] = qc_near, qc_all[:1], qc_all[1:]

    vec = jnp.concatenate([row_of(v) for v in (gain_two, shift_two, gain_three, shift_three)])
    each = 2 * quarter + share
    layer_out, dr2, do2, sums2, small_ff, small_up, *parts = run(
        "ffn",
        feed_forward,
        [
            like((rows, width), BF),
            like((rows, width), F32),
            like((rows + 16, width), BF),
            like((2 * rows, LANES), F32),
            like((8, width), F32),
            like((1, hidden), F32),
            like((each, rows), BF),
            like((3 * width + each, rows), BF),
            like((3 * width + 2 * each, rows), BF),
        ],
        [
            o2, h1, sums, w_cross_out, w_up, w_down, row_of(b_up), row_of(b_down), vec,
            cotangent[0],
        ],
        scalars=[rep_scalar],
        scratch=[
            pltpu.VMEM((rows, hidden), F32),
            pltpu.VMEM((hidden, rows), BF),
            pltpu.VMEM((hidden, rows), BF),
        ],
    )
    near, far = hop(parts[1], 0, 1), hop(parts[2], 0, 2)
    do2_near = stream_along(do2)
    do2_all = stream_across(do2, do2_near)
    moving["do_z"], moving["do_stack"], moving["do_y"] = do2_near, do2_all[:1], do2_all[1:]
    moving["near"], moving["far"] = [near], [far]
    v = {}

    def step_dq():
        (v["dqc"],) = run(
            "dq", cross_backward, [like((rows, width), BF)], [qc, do2, kv, bias, sums2]
        )

    def step_self():
        v["d_tokens"], v["small_self"], *exports = run(
            "self",
            self_backward,
            [like((rows, width), F32), like((8, width), F32)]
            + [like((rows, width + share), BF)] * 4,
            [v["dqc"], dr2, r1, joined, w_cross_q, w_self_out, w_self, row_of(gain_one)],
            scalars=[rep_scalar],
            scratch=[
                pltpu.VMEM((rows, 3 * width), BF),
                pltpu.VMEM((4, rows, width + share), BF),
            ],
        )
        v["grads"] = rep_each(exports)
        moving["exports"] = v["grads"][1:]
        relayed = hop(after(far, v["small_self"], *[a for k in RELAY for a in moving[k]]), 0, 1)
        moving["relay"] = [relayed]
        v["shared"] = [parts[1], near, far, relayed, parts[0]]

    def full_at(row):
        return ((0, row), (1, row), (2, each + row), (3, each + row))

    def each_at(row):
        return ((4, row), (1, 3 * width + row), (2, row), (3, each + 3 * width + row))

    def blocks_of(name, plan, arrays, size, wide, whole=None, ready=None, extra=None):
        return run(
            name,
            functools.partial(weight_blocks, plan, whole, ready, extra),
            [like((4, size, wide), BF)] * 4 + ([like((width, whole[3]), BF)] if whole else []),
            arrays,
            scalars=[bits],
            scratch=[
                pltpu.VMEM((width, 4 * rows), BF),
                pltpu.VMEM((4 * rows, width), BF),
                pltpu.VMEM((width, width), F32),
            ],
        )

    def first_hops(key, blocks):
        send0, keep0, send1, keep1 = blocks
        v[key] = [keep0, hop(send0, 1), keep1, hop(send1, 2)]

    def second_hops(name, key):
        give0, mine0, give1, mine1 = run(
            name, fold_two, [like((2,) + v[key][0].shape[1:], BF)] * 4, v[key], scalars=[bits]
        )
        v[key] = [mine0, hop(give0, 2), mine1, hop(give1, 1)]

    def third_hop(name, key):
        arrays = v[key]
        give, mine = run(
            name,
            fold_high,
            [like((len(arrays) // 2,) + arrays[0].shape[1:], BF)] * 2,
            arrays,
            scalars=[bits],
        )
        v[key] = [mine, hop(give, 4)]

    def last_hops(name, key):
        (piece,) = run(name, fold_last, [like(v[key][0].shape, BF)], v[key])
        v[key] = rep_full(piece)

    def gathered(name, key, plan, shapes):
        return run(
            name,
            functools.partial(lay_columns, plan),
            [like(shape, F32) for shape in shapes],
            v[key],
            scalars=[rep_scalar],
            scratch=[pltpu.VMEM((4,) + v[key][0].shape, BF)],
        )

    def step_ff1():
        *blocks, v["cross_out"] = blocks_of(
            "ff1",
            [
                (full_at(0), each_at(quarter), True, quarter, 0, 0),
                (each_at(0), full_at(2 * width), True, width, 1, 0),
            ],
            v["shared"],
            tall,
            width,
            whole=(full_at(width), each_at(2 * quarter), True, share),
        )
        first_hops("ff", blocks)
        moving["ff_first"] = [v["ff"][1], v["ff"][3]]

    def step_rest1():
        vectors = jnp.concatenate([small_ff[0:5], v["small_self"][0:2]]).reshape(7, streams, tall)
        vectors = jnp.pad(vectors.transpose(1, 0, 2), ((0, 0), (0, 0), (0, LANES - tall)))
        vectors = jnp.concatenate(
            [
                vectors,
                small_up.reshape(streams, -1, LANES),
                jnp.zeros((streams, 9 - hidden // streams // LANES, LANES), F32),
            ],
            axis=1,
        )
        early_at = lambda row: tuple((k, row) for k in range(4))
        grads_at = lambda col: tuple((4 + k, col) for k in range(4))
        first_hops(
            "rest",
            blocks_of(
                "rest1",
                [
                    (early_at(0), grads_at(0), False, 3 * share, 0, 0),
                    (early_at(width), grads_at(3 * share), False, share, 1, 0),
                    (early_at(2 * width), grads_at(4 * share), False, share, 1, share),
                ],
                early + v["grads"] + [vectors, v["cross_out"]],
                tall + 16,
                3 * share,
                ready=(9, 1, 2 * share),
                extra=8,
            ),
        )
        moving["rest_first"] = [v["rest"][1], v["rest"][3]]

    kv_wide = 2 * width // 4

    def step_owner():
        (v["dkv"],) = run(
            "owner",
            owner_backward,
            [like((memory_rows.shape[0], 2 * width), BF)],
            qc_all + do2_all + [kv_own],
            scalars=[(routes[0] ^ me).astype(jnp.int32)],
            scratch=[
                pltpu.VMEM((streams, PAIRS, 2 * rows, LANES), BF),
                pltpu.VMEM((streams, PAIRS, 2 * rows, LANES), BF),
                pltpu.VMEM((streams, 16, 2 * rows), F32),
            ],
        )

    def step_kv0():
        kv_keep, kv_send = run(
            "kv0",
            memory_weights,
            [like((2, width, kv_wide), BF)] * 2,
            [v["dkv"], memory_turned],
            scalars=[rep_scalar],
        )
        v["kv"] = [kv_keep, hop(kv_send, 0, 1)]

    def step_kv1():
        near_sum, far_sum = run(
            "kv1", fold_core, [like((width, kv_wide), F32), like((width, kv_wide), BF)], v["kv"]
        )
        v["kv"] = [near_sum, hop(far_sum, 0, 2)]

    def step_kv2():
        send, keep = run(
            "kv2", fold_rep, [like((4, tall, kv_wide), BF)] * 2, v["kv"], scalars=[bits]
        )
        v["kv"] = [keep, hop(send, 1)]

    def step_kv3():
        give, mine = run(
            "kv3", fold_one, [like((2, tall, kv_wide), BF)] * 2, v["kv"], scalars=[bits]
        )
        v["kv"] = [mine, hop(give, 2)]

    def step_memory():
        (v["d_memory"],) = run(
            "memory", memory_backward, [like(memory_rows.shape, BF)], [v["dkv"], w_cross_kv]
        )

    def step_lay_ff():
        v["g_up"], v["g_down"] = gathered(
            "lay_ff",
            "ff",
            [(0, 0, quarter, "side"), (1, 0, width, "below")],
            [(tall, hidden), (hidden // streams, width)],
        )

    def step_lay_rest():
        v["g_self"], v["g_self_out"], v["g_query"], v["g_out"], v["g_vec"] = gathered(
            "lay_rest",
            "rest",
            [
                (0, 0, 3 * share, "side"),
                (1, 0, share, "side"),
                (1, share, share, "side"),
                (1, 2 * share, share, "side"),
                (0, 0, LANES, "sum"),
            ],
            [(tall, 3 * width), (tall, width), (tall, width), (tall, width), (16, LANES)],
        )

    def step_lay_kv():
        (v["g_kv"],) = gathered("lay_kv", "kv", [(0, 0, kv_wide, "side")], [(tall, 2 * width)])

    steps = {
        "dq": step_dq,
        "self": step_self,
        "ff1": step_ff1,
        "rest1": step_rest1,
        "owner": step_owner,
        "kv0": step_kv0,
        "kv1": step_kv1,
        "kv2": step_kv2,
        "kv3": step_kv3,
        "kv4": lambda: third_hop("kv4", "kv"),
        "kv5": lambda: last_hops("kv5", "kv"),
        "ff2": lambda: second_hops("ff2", "ff"),
        "ff3": lambda: third_hop("ff3", "ff"),
        "ff4": lambda: last_hops("ff4", "ff"),
        "rest2": lambda: second_hops("rest2", "rest"),
        "rest3": lambda: third_hop("rest3", "rest"),
        "rest4": lambda: last_hops("rest4", "rest"),
        "memory": step_memory,
        "lay_ff": step_lay_ff,
        "lay_rest": step_lay_rest,
        "lay_kv": step_lay_kv,
    }
    for name in ORDER:
        steps[name]()
    piece = lambda row: v["g_vec"][row, 0:tall]
    return (
        layer_out[None],
        v["d_tokens"][None],
        v["d_memory"][None],
        v["g_self"],
        v["g_self_out"],
        v["g_query"],
        v["g_kv"],
        v["g_out"],
        v["g_up"],
        v["g_vec"][7 : 7 + hidden // streams // LANES].reshape(-1),
        v["g_down"],
        piece(0),
        piece(5),
        piece(6),
        piece(1),
        piece(2),
        piece(3),
        piece(4),
    )


def solution(mesh):
    in_specs = (
        P("rep", "stream", None),
        P("rep", "stream", None),
        P("rep", "stream"),
        P(),
        P(),
        P(),
        P(),
        P(),
        P(),
        P(),
        P(),
        P(),
        P(),
        P(),
        P(),
        P(),
        P(),
        P(),
        P("rep", "stream", None),
    )
    out_specs = (
        P("rep", "stream", None),
        P("rep", "stream", None),
        P("rep", "stream", None),
        P("stream", None),
        P("stream", None),
        P("stream", None),
        P("stream", None),
        P("stream", None),
        P("stream", None),
        P("stream"),
        P("stream", None),
        P("stream"),
        P("stream"),
        P("stream"),
        P("stream"),
        P("stream"),
        P("stream"),
        P("stream"),
    )
    small_slice = (mesh.shape["stream"], mesh.shape["rep"]) == (8, 4)
    return jax.shard_map(
        fast_on_device if small_slice else on_device, mesh=mesh, in_specs=in_specs, out_specs=out_specs, check_vma=False
    )
```

```python
import functools

import jax
import jax.numpy as jnp
from jax import lax
from jax.experimental import pallas as pl
from jax.experimental.pallas import tpu as pltpu
from jax.sharding import PartitionSpec as P

HEADS = 12
HEAD_DIM = 64
BLK = 128


def matmul(left, right):
    return jnp.dot(left, right, preferred_element_type=jnp.float32)


def product_left(left, right):
    return lax.dot_general(
        left, right, (((0,), (0,)), ((), ())), preferred_element_type=jnp.float32
    )


def product_right(left, right):
    return lax.dot_general(
        left, right, (((1,), (1,)), ((), ())), preferred_element_type=jnp.float32
    )


def layer_norm(rows, gain, shift):
    centred = rows - jnp.mean(rows, axis=-1, keepdims=True)
    spread = jnp.mean(centred * centred, axis=-1, keepdims=True)
    return centred * lax.rsqrt(spread + 1e-05) * gain + shift


def split_heads(rows):
    return rows.reshape(rows.shape[0], HEADS, HEAD_DIM).transpose(1, 0, 2)


def join_heads(rows):
    return rows.transpose(1, 0, 2).reshape(rows.shape[1], HEADS * HEAD_DIM)


def masked_scores(query_head, key_head, key_ok):
    scores = product_right(query_head, key_head) * HEAD_DIM ** (-0.5)
    if key_ok is not None:
        scores = jnp.where(key_ok[None, :], scores, -1e30)
    return scores


def attend_forward(query, key_rows, value_rows, key_ok):

    def one_head(item):
        query_head, key_head, value_head = item
        scores = masked_scores(query_head, key_head, key_ok)
        row_max = jnp.max(scores, axis=1, keepdims=True)
        exponent = jnp.exp(scores - row_max)
        row_total = jnp.sum(exponent, axis=1, keepdims=True)
        probability = (exponent / row_total).astype(jnp.bfloat16)
        return (matmul(probability, value_head), (row_max + jnp.log(row_total))[:, 0])

    mixed, log_total = lax.map(
        one_head, (split_heads(query), split_heads(key_rows), split_heads(value_rows))
    )
    return (join_heads(mixed), log_total)


def attend_backward(query, key_rows, value_rows, key_ok, log_total, d_mixed):
    factor = HEAD_DIM ** (-0.5)

    def one_head(item):
        query_head, key_head, value_head, total_head, grad_head = item
        scores = masked_scores(query_head, key_head, key_ok)
        probability = jnp.exp(scores - total_head[:, None])
        d_prob = product_right(grad_head, value_head)
        d_scores = probability * (d_prob - jnp.sum(d_prob * probability, axis=1, keepdims=True))
        d_scores = d_scores.astype(jnp.bfloat16)
        d_query = matmul(d_scores, key_head) * factor
        d_key = product_left(d_scores, query_head) * factor
        d_value = product_left(probability.astype(jnp.bfloat16), grad_head)
        return (d_query, d_key, d_value)

    d_query, d_key, d_value = lax.map(
        one_head,
        (
            split_heads(query),
            split_heads(key_rows),
            split_heads(value_rows),
            log_total,
            split_heads(d_mixed),
        ),
    )
    return (join_heads(d_query), join_heads(d_key), join_heads(d_value))


def on_device(
    queries,
    memory,
    routes,
    w_self,
    w_self_out,
    w_cross_q,
    w_cross_kv,
    w_cross_out,
    w_up,
    b_up,
    w_down,
    b_down,
    gain_one,
    shift_one,
    gain_two,
    shift_two,
    gain_three,
    shift_three,
    cotangent,
):
    streams = lax.axis_size("stream")
    blocks = routes.shape[1]
    capacity = max(2, 2 * blocks // streams)
    slot_count = streams * capacity
    model_width = w_self_out.shape[0]
    target = routes[0]
    hit_table = (target[:, None] == jnp.arange(streams, dtype=jnp.int32)[None, :]).astype(jnp.int32)
    before = jnp.cumsum(hit_table, axis=0) - hit_table
    rank_in = jnp.sum(before * hit_table, axis=1)
    slot_of_block = target * capacity + rank_in
    matched = (slot_of_block[None, :] == jnp.arange(slot_count, dtype=jnp.int32)[:, None]).astype(
        jnp.int32
    )
    block_at = jnp.sum(matched * jnp.arange(blocks, dtype=jnp.int32)[None, :], axis=1)
    live_slot = jnp.sum(matched, axis=1)
    live_grid = live_slot.reshape(streams, capacity)
    filled = (live_slot > 0)[:, None, None]
    nothing = jnp.zeros((), jnp.bfloat16)
    memory_rows = memory[0]
    projected = (
        matmul(memory_rows, w_cross_kv).astype(jnp.bfloat16).reshape(blocks, BLK, 2 * model_width)
    )
    outgoing = jnp.where(filled, jnp.take(projected, block_at, axis=0), nothing)
    arrived, arrived_live = (
        lax.all_to_all(
            outgoing.reshape(streams, capacity, BLK, 2 * model_width),
            "stream",
            split_axis=0,
            concat_axis=0,
            tiled=True,
        ),
        lax.all_to_all(live_grid, "stream", split_axis=0, concat_axis=0, tiled=True),
    )
    keys_values = arrived.reshape(-1, 2 * model_width)
    key_ok = jnp.repeat(arrived_live.reshape(-1), BLK) > 0
    key_cross = keys_values[:, :model_width]
    value_cross = keys_values[:, model_width:]
    gain_a = gain_one.astype(jnp.float32)
    shift_a = shift_one.astype(jnp.float32)
    gain_b = gain_two.astype(jnp.float32)
    shift_b = shift_two.astype(jnp.float32)
    gain_c = gain_three.astype(jnp.float32)
    shift_c = shift_three.astype(jnp.float32)
    tokens = queries[0]
    joined = matmul(tokens, w_self).astype(jnp.bfloat16)
    query_self = joined[:, :model_width]
    key_self = joined[:, model_width : 2 * model_width]
    value_self = joined[:, 2 * model_width :]
    mixed_self, total_self = attend_forward(query_self, key_self, value_self, None)
    mixed_self = mixed_self.astype(jnp.bfloat16)
    residual_one = tokens.astype(jnp.float32) + matmul(mixed_self, w_self_out)
    normed_one = layer_norm(residual_one, gain_a, shift_a).astype(jnp.bfloat16)
    query_cross = matmul(normed_one, w_cross_q).astype(jnp.bfloat16)
    mixed_cross, total_cross = attend_forward(query_cross, key_cross, value_cross, key_ok)
    mixed_cross = mixed_cross.astype(jnp.bfloat16)
    residual_two = normed_one.astype(jnp.float32) + matmul(mixed_cross, w_cross_out)
    normed_two = layer_norm(residual_two, gain_b, shift_b).astype(jnp.bfloat16)
    hidden_pre = matmul(normed_two, w_up) + b_up.astype(jnp.float32)
    hidden = jax.nn.gelu(hidden_pre, approximate=False).astype(jnp.bfloat16)
    residual_three = (
        normed_two.astype(jnp.float32) + matmul(hidden, w_down) + b_down.astype(jnp.float32)
    )
    layer_out = layer_norm(residual_three, gain_c, shift_c).astype(jnp.bfloat16)
    grad_out = cotangent[0].astype(jnp.float32)
    norm_three_pull = jax.vjp(layer_norm, residual_three, gain_c, shift_c)[1]
    d_residual_three, d_gain_c, d_shift_c = norm_three_pull(grad_out)
    d_branch_three = d_residual_three.astype(jnp.bfloat16)
    d_b_down = jnp.sum(d_branch_three.astype(jnp.float32), axis=0)
    d_w_down = product_left(hidden, d_branch_three)
    d_hidden = product_right(d_branch_three, w_down)
    gelu_pull = jax.vjp(lambda value: jax.nn.gelu(value, approximate=False), hidden_pre)[1]
    d_hidden_pre = gelu_pull(d_hidden)[0].astype(jnp.bfloat16)
    d_b_up = jnp.sum(d_hidden_pre.astype(jnp.float32), axis=0)
    d_w_up = product_left(normed_two, d_hidden_pre)
    d_normed_two = d_residual_three + product_right(d_hidden_pre, w_up)
    norm_two_pull = jax.vjp(layer_norm, residual_two, gain_b, shift_b)[1]
    d_residual_two, d_gain_b, d_shift_b = norm_two_pull(d_normed_two)
    d_branch_two = d_residual_two.astype(jnp.bfloat16)
    d_w_cross_out = product_left(mixed_cross, d_branch_two)
    d_mixed_cross = product_right(d_branch_two, w_cross_out).astype(jnp.bfloat16)
    d_query_cross, d_key_cross, d_value_cross = attend_backward(
        query_cross, key_cross, value_cross, key_ok, total_cross, d_mixed_cross
    )
    d_query_cross = d_query_cross.astype(jnp.bfloat16)
    d_keys_values = jnp.concatenate([d_key_cross, d_value_cross], axis=1).astype(jnp.bfloat16)
    d_w_cross_q = product_left(normed_one, d_query_cross)
    d_normed_one = d_residual_two + product_right(d_query_cross, w_cross_q)
    norm_one_pull = jax.vjp(layer_norm, residual_one, gain_a, shift_a)[1]
    d_residual_one, d_gain_a, d_shift_a = norm_one_pull(d_normed_one)
    d_branch_one = d_residual_one.astype(jnp.bfloat16)
    d_w_self_out = product_left(mixed_self, d_branch_one)
    d_mixed_self = product_right(d_branch_one, w_self_out).astype(jnp.bfloat16)
    d_query_self, d_key_self, d_value_self = attend_backward(
        query_self, key_self, value_self, None, total_self, d_mixed_self
    )
    d_joined = jnp.concatenate([d_query_self, d_key_self, d_value_self], axis=1).astype(
        jnp.bfloat16
    )
    d_w_self = product_left(tokens, d_joined)
    d_tokens = d_residual_one + product_right(d_joined, w_self)
    returned = lax.all_to_all(
        d_keys_values.reshape(streams, capacity, BLK, 2 * model_width),
        "stream",
        split_axis=0,
        concat_axis=0,
        tiled=True,
    )
    d_block_rows = jnp.take(
        returned.reshape(slot_count, BLK, 2 * model_width), slot_of_block, axis=0
    ).reshape(-1, 2 * model_width)
    d_w_cross_kv = product_left(memory_rows, d_block_rows)
    d_memory = product_right(d_block_rows, w_cross_kv).astype(jnp.bfloat16)
    gradients = (
        d_w_self,
        d_w_self_out,
        d_w_cross_q,
        d_w_cross_kv,
        d_w_cross_out,
        d_w_up,
        d_b_up,
        d_w_down,
        d_b_down,
        d_gain_a,
        d_shift_a,
        d_gain_b,
        d_shift_b,
        d_gain_c,
        d_shift_c,
    )
    shapes = [item.shape for item in gradients]
    flat = [item.reshape(-1) for item in gradients]
    (
        share_self,
        share_self_out,
        share_cross_q,
        share_cross_kv,
        share_cross_out,
        share_up,
        share_b_up,
        share_down,
        share_b_down,
        share_gain_a,
        share_shift_a,
        share_gain_b,
        share_shift_b,
        share_gain_c,
        share_shift_c,
    ) = (
        lax.psum_scatter(flat[0], "stream", scatter_dimension=0, tiled=True),
        lax.psum_scatter(flat[1], "stream", scatter_dimension=0, tiled=True),
        lax.psum_scatter(flat[2], "stream", scatter_dimension=0, tiled=True),
        lax.psum_scatter(flat[3], "stream", scatter_dimension=0, tiled=True),
        lax.psum_scatter(flat[4], "stream", scatter_dimension=0, tiled=True),
        lax.psum_scatter(flat[5], "stream", scatter_dimension=0, tiled=True),
        lax.psum_scatter(flat[6], "stream", scatter_dimension=0, tiled=True),
        lax.psum_scatter(flat[7], "stream", scatter_dimension=0, tiled=True),
        lax.psum_scatter(flat[8], "stream", scatter_dimension=0, tiled=True),
        lax.psum_scatter(flat[9], "stream", scatter_dimension=0, tiled=True),
        lax.psum_scatter(flat[10], "stream", scatter_dimension=0, tiled=True),
        lax.psum_scatter(flat[11], "stream", scatter_dimension=0, tiled=True),
        lax.psum_scatter(flat[12], "stream", scatter_dimension=0, tiled=True),
        lax.psum_scatter(flat[13], "stream", scatter_dimension=0, tiled=True),
        lax.psum_scatter(flat[14], "stream", scatter_dimension=0, tiled=True),
    )
    summed = (
        lax.psum(share_self.astype(jnp.bfloat16), "rep").astype(jnp.float32),
        lax.psum(share_self_out.astype(jnp.bfloat16), "rep").astype(jnp.float32),
        lax.psum(share_cross_q.astype(jnp.bfloat16), "rep").astype(jnp.float32),
        lax.psum(share_cross_kv.astype(jnp.bfloat16), "rep").astype(jnp.float32),
        lax.psum(share_cross_out.astype(jnp.bfloat16), "rep").astype(jnp.float32),
        lax.psum(share_up.astype(jnp.bfloat16), "rep").astype(jnp.float32),
        lax.psum(share_b_up.astype(jnp.bfloat16), "rep").astype(jnp.float32),
        lax.psum(share_down.astype(jnp.bfloat16), "rep").astype(jnp.float32),
        lax.psum(share_b_down.astype(jnp.bfloat16), "rep").astype(jnp.float32),
        lax.psum(share_gain_a.astype(jnp.bfloat16), "rep").astype(jnp.float32),
        lax.psum(share_shift_a.astype(jnp.bfloat16), "rep").astype(jnp.float32),
        lax.psum(share_gain_b.astype(jnp.bfloat16), "rep").astype(jnp.float32),
        lax.psum(share_shift_b.astype(jnp.bfloat16), "rep").astype(jnp.float32),
        lax.psum(share_gain_c.astype(jnp.bfloat16), "rep").astype(jnp.float32),
        lax.psum(share_shift_c.astype(jnp.bfloat16), "rep").astype(jnp.float32),
    )
    results = [
        part.reshape((shape[0] // streams,) + tuple(shape[1:]))
        for part, shape in zip(summed, shapes)
    ]
    return (
        layer_out[None],
        d_tokens[None],
        d_memory[None],
        results[0],
        results[1],
        results[2],
        results[3],
        results[4],
        results[5],
        results[6],
        results[7],
        results[8],
        results[9],
        results[10],
        results[11],
        results[12],
        results[13],
        results[14],
    )


PAIRS = HEADS // 2
LANES = 2 * HEAD_DIM
FACTOR = HEAD_DIM ** (-0.5)
BF = jnp.bfloat16
F32 = jnp.float32
AXES = ("stream", "rep")


def whole_in_vmem(count):
    return [pl.BlockSpec(memory_space=pltpu.VMEM)] * count


def local_kernel(body, out_shape, scalars=(), arrays=(), scratch=(), cost=2, limit=24):
    return pl.pallas_call(
        body,
        out_shape=list(out_shape),
        in_specs=[pl.BlockSpec(memory_space=pltpu.SMEM)] * len(scalars) + whole_in_vmem(len(arrays)),
        out_specs=whole_in_vmem(len(out_shape)),
        scratch_shapes=list(scratch),
        compiler_params=pltpu.CompilerParams(vmem_limit_bytes=limit * 1024 * 1024),
        cost_estimate=pl.CostEstimate(
            flops=int(cost * 1.15e9), bytes_accessed=int(cost * 1e5), transcendentals=0
        ),
    )(*scalars, *arrays)


def like(shape, dtype):
    return jax.ShapeDtypeStruct(shape, dtype)


def dot_nn(left, right):
    return lax.dot_general(left, right, (((1,), (0,)), ((), ())), preferred_element_type=F32)


def dot_nt(left, right):
    return lax.dot_general(left, right, (((1,), (1,)), ((), ())), preferred_element_type=F32)


def head_masks(rows):
    lane = lax.broadcasted_iota(jnp.int32, (rows, LANES), 1)
    return lane < HEAD_DIM


def stack_heads(pair, first, scale):
    one = jnp.where(first, scale, 0.0).astype(BF)
    two = jnp.where(first, 0.0, scale).astype(BF)
    return jnp.concatenate([pair * one, pair * two], axis=0)


def unstack_heads(both, first):
    rows = both.shape[0] // 2
    return jnp.where(first, both[:rows], both[rows:])


def norm_parts(rows):
    centred = rows - jnp.mean(rows, axis=1, keepdims=True)
    spread = jnp.mean(centred * centred, axis=1, keepdims=True)
    inverse = lax.rsqrt(spread + 1e-05)
    return centred * inverse, inverse


def norm_pull(grad, hat, inverse, gain):
    scaled = grad * gain
    inner = scaled - jnp.mean(scaled, axis=1, keepdims=True)
    inner = inner - hat * jnp.mean(scaled * hat, axis=1, keepdims=True)
    return (
        inverse * inner,
        jnp.sum(grad * hat, axis=0, keepdims=True),
        jnp.sum(grad, axis=0, keepdims=True),
    )


def deal_blocks(routes_ref, memory_ref, out_ref):
    out_ref[...] = jnp.zeros_like(out_ref)
    blocks = memory_ref.shape[0] // BLK
    for b in range(blocks):
        group = routes_ref[0, b]
        rank = jnp.int32(0)
        for earlier in range(b):
            rank = rank + (routes_ref[0, earlier] == group).astype(jnp.int32)
        row = pl.multiple_of(rank * BLK, BLK)
        out_ref[group, pl.ds(row, BLK), :] = memory_ref[b * BLK : (b + 1) * BLK, :]


def self_forward(tok, w_in, w_out, w_q, gain, shift, joined, r1, h1_out, qc, turned):
    width = tok.shape[1]
    rows = tok.shape[0]
    joined[...] = dot_nn(tok[...], w_in[...]).astype(BF)
    first = head_masks(rows)
    mixed = []
    for j in range(PAIRS):
        at = j * LANES
        q2 = stack_heads(joined[:, at : at + LANES], first, FACTOR)
        key = joined[:, width + at : width + at + LANES]
        value = joined[:, 2 * width + at : 2 * width + at + LANES]
        scores = dot_nt(q2, key)
        power = jnp.exp(scores - jnp.max(scores, axis=1, keepdims=True))
        prob = (power / jnp.sum(power, axis=1, keepdims=True)).astype(BF)
        mixed.append(unstack_heads(dot_nn(prob, value), first).astype(BF))
    o1 = jnp.concatenate(mixed, axis=1)
    res = tok[...].astype(F32) + dot_nn(o1, w_out[...])
    r1[...] = res
    hat, _ = norm_parts(res)
    h1 = (hat * gain[...].astype(F32) + shift[...].astype(F32)).astype(BF)
    h1_out[...] = h1
    qc[...] = dot_nn(h1, w_q[...]).astype(BF)
    turned[0:width, :] = tok[...].T
    turned[width : 2 * width, :] = o1.T
    turned[2 * width : 3 * width, :] = h1.T


def cross_forward(routes_ref, me_ref, qc, parcels, w_kv, o2, kv, sums, bias_ref, s_ref, p_ref):
    width = qc.shape[1]
    rows = qc.shape[0]
    sources = parcels.shape[0]
    span = 2 * BLK
    first = head_masks(rows)
    for k in range(sources):
        kv[k * span : (k + 1) * span, :] = dot_nn(parcels[k, 0:span, :], w_kv[...]).astype(BF)
        count = jnp.int32(0)
        for b in range(routes_ref.shape[1]):
            count = count + (routes_ref[k, b] == me_ref[0]).astype(jnp.int32)
        for c in range(2):
            bias_ref[:, k * span + c * BLK : k * span + (c + 1) * BLK] = jnp.full(
                (8, BLK), jnp.where(count > c, 0.0, -1e30), F32
            )
    lane = lax.broadcasted_iota(jnp.int32, (2 * rows, LANES), 1)
    sums[...] = jnp.zeros_like(sums)

    def one_pair(j, carry):
        at = pl.multiple_of(j * LANES, LANES)
        q2 = stack_heads(qc[:, pl.ds(at, LANES)], first, FACTOR)
        top = None
        for k in range(sources):
            key = kv[k * span : (k + 1) * span, pl.ds(at, LANES)]
            scores = dot_nt(q2, key) + bias_ref[0:1, k * span : (k + 1) * span]
            s_ref[:, k * span : (k + 1) * span] = scores
            most = jnp.maximum(scores[:, :LANES], scores[:, LANES:])
            top = most if top is None else jnp.maximum(top, most)
        peak = jnp.max(top, axis=1, keepdims=True)
        total = None
        for k in range(sources):
            power = jnp.exp(s_ref[:, k * span : (k + 1) * span] - peak)
            p_ref[:, k * span : (k + 1) * span] = power.astype(BF)
            part = power[:, :LANES] + power[:, LANES:]
            total = part if total is None else total + part
        total = jnp.sum(total, axis=1, keepdims=True)
        value = kv[:, pl.ds(pl.multiple_of(width + j * LANES, LANES), LANES)]
        both = dot_nn(p_ref[...], value) / total
        o2[:, pl.ds(at, LANES)] = unstack_heads(both, first).astype(BF)
        sums[...] = jnp.where(lane == j, peak + jnp.log(total), sums[...])
        return carry

    lax.fori_loop(0, PAIRS, one_pair, 0, unroll=PAIRS)


def feed_forward(
    rep_ref, o2, tok_h1, sums, w_co, w_up, w_down, b_up, b_down, vec, cot,
    layer_out, dr2, do2, both_sums, small, small_up, parcel0, parcel1, parcel2,
    slope, acts, dus,
):
    width = o2.shape[1]
    rows = o2.shape[0]
    hidden = w_up.shape[1]
    quarter = hidden // 4
    rep = rep_ref[0]
    gain2, shift2, gain3, shift3 = (vec[i : i + 1, :].astype(F32) for i in range(4))
    res2 = tok_h1[...].astype(F32) + dot_nn(o2[...], w_co[...])
    hat2, inv2 = norm_parts(res2)
    h2 = (hat2 * gain2 + shift2).astype(BF)
    each = 2 * quarter + width // 4
    for parcel, base in ((parcel1, 0), (parcel2, each)):
        parcel[base : base + width, :] = h2.T
        parcel[base + width : base + 2 * width, :] = o2[...].T
    total = None
    for c in range(4):
        cols = slice(c * quarter, (c + 1) * quarter)
        u = dot_nn(h2, w_up[:, cols]) + b_up[:, cols].astype(F32)
        cdf = 0.5 + 0.5 * lax.erf(u * 0.7071067811865476)
        act = (u * cdf).astype(BF)
        slope[:, cols] = cdf + u * (jnp.exp(u * u * -0.5) * 0.3989422804014327)
        acts[cols, :] = act.T
        part = dot_nn(act, w_down[cols, :])
        total = part if total is None else total + part
    res3 = h2.astype(F32) + total + b_down[...].astype(F32)
    hat3, inv3 = norm_parts(res3)
    layer_out[...] = (hat3 * gain3 + shift3).astype(BF)
    dr3, d_gain3, d_shift3 = norm_pull(cot[...].astype(F32), hat3, inv3, gain3)
    dy3 = dr3.astype(BF)
    small[0:1, :] = jnp.sum(dy3.astype(F32), axis=0, keepdims=True)
    small[3:4, :] = d_gain3
    small[4:5, :] = d_shift3
    back = None
    for c in range(4):
        cols = slice(c * quarter, (c + 1) * quarter)
        du = (dot_nt(dy3, w_down[cols, :]) * slope[:, cols]).astype(BF)
        small_up[:, cols] = jnp.sum(du.astype(F32), axis=0, keepdims=True)
        dus[cols, :] = du.T
        part = dot_nt(du, w_up[:, cols])
        back = part if back is None else back + part
    grad2, d_gain2, d_shift2 = norm_pull(dr3 + back, hat2, inv2, gain2)
    small[1:2, :] = d_gain2
    small[2:3, :] = d_shift2
    small[5:8, :] = jnp.zeros((3, width), F32)
    dr2[...] = grad2
    dy2 = grad2.astype(BF)
    grad_mixed = dot_nt(dy2, w_co[...]).astype(BF)
    do2[0:rows, :] = grad_mixed
    lane = lax.broadcasted_iota(jnp.int32, (2 * rows, LANES), 1)
    first = head_masks(rows)
    packed = sums[...]
    for j in range(PAIRS):
        at = slice(j * LANES, (j + 1) * LANES)
        prod = grad_mixed[:, at].astype(F32) * o2[:, at].astype(F32)
        zero = jnp.zeros_like(prod)
        two = jnp.concatenate([jnp.where(first, prod, zero), jnp.where(first, zero, prod)], axis=0)
        packed = jnp.where(lane == 8 + j, jnp.sum(two, axis=1, keepdims=True), packed)
    both_sums[...] = packed
    turned = packed.T[0:16, :]
    high = turned.astype(BF)
    rest = turned - high.astype(F32)
    middle = rest.astype(BF)
    low = (rest - middle.astype(F32)).astype(BF)
    do2[rows : rows + 16, :] = jnp.concatenate([high, middle, low], axis=1)
    share = width // 4
    dy2_turned = dy2.T
    dy3_turned = dy3.T
    strip = quarter // 8
    parcel1[2 * width : 3 * width, :] = dy3_turned
    parcel2[each + 2 * width : each + 3 * width, :] = dy3_turned
    places = ((parcel0, 0), (parcel1, 3 * width), (parcel2, 0), (parcel2, each + 3 * width))
    for k, (parcel, base) in enumerate(places):
        peer = rep ^ k
        for s in range(8):
            row = pl.multiple_of(s * 4 * strip + peer * strip, strip)
            parcel[base + s * strip : base + (s + 1) * strip, :] = acts[pl.ds(row, strip), :]
        row = pl.multiple_of(peer * quarter, quarter)
        parcel[base + quarter : base + 2 * quarter, :] = dus[pl.ds(row, quarter), :]
        piece = dy2_turned[0:share]
        for i in range(1, 4):
            piece = jnp.where(peer == i, dy2_turned[i * share : (i + 1) * share], piece)
        parcel[base + 2 * quarter : base + 2 * quarter + share, :] = piece


def cross_backward(qc, do2, kv, bias_ref, sums, dqc):
    width = qc.shape[1]
    rows = qc.shape[0]
    span = 2 * BLK
    sources = kv.shape[0] // span
    first = head_masks(rows)
    lane = lax.broadcasted_iota(jnp.int32, (2 * rows, LANES), 1)

    def one_pair(j, carry):
        at = pl.multiple_of(j * LANES, LANES)
        q2 = stack_heads(qc[:, pl.ds(at, LANES)], first, FACTOR)
        g2 = stack_heads(do2[0:rows, pl.ds(at, LANES)], first, 1.0)
        packed = sums[...]
        log_sum = jnp.sum(jnp.where(lane == j, packed, 0.0), axis=1, keepdims=True)
        delta = jnp.sum(jnp.where(lane == j + 8, packed, 0.0), axis=1, keepdims=True)
        total = None
        for k in range(sources):
            key = kv[k * span : (k + 1) * span, pl.ds(at, LANES)]
            value = kv[
                k * span : (k + 1) * span, pl.ds(pl.multiple_of(width + j * LANES, LANES), LANES)
            ]
            scores = dot_nt(q2, key) + bias_ref[0:1, k * span : (k + 1) * span]
            prob = jnp.exp(scores - log_sum)
            grad = (prob * (dot_nt(g2, value) - delta)).astype(BF)
            part = dot_nn(grad, key)
            total = part if total is None else total + part
        dqc[:, pl.ds(at, LANES)] = (unstack_heads(total, first) * FACTOR).astype(BF)
        return carry

    lax.fori_loop(0, PAIRS, one_pair, 0, unroll=PAIRS)


def self_backward(
    rep_ref, dqc_ref, dr2, r1, joined, w_q, w_out, w_in, gain,
    d_tok, small, out0, out1, out2, out3,
    da_ref, quarters,
):
    rows, width = dqc_ref.shape
    rep = rep_ref[0]
    first = head_masks(rows)
    dqc = dqc_ref[...]
    grad1 = dr2[...] + dot_nt(dqc, w_q[...])
    hat1, inv1 = norm_parts(r1[...])
    dr1, d_gain1, d_shift1 = norm_pull(grad1, hat1, inv1, gain[...].astype(F32))
    small[0:1, :] = d_gain1
    small[1:2, :] = d_shift1
    small[2:8, :] = jnp.zeros((6, width), F32)
    dy1 = dr1.astype(BF)
    do1 = dot_nt(dy1, w_out[...]).astype(BF)
    for j in range(PAIRS):
        at = slice(j * LANES, (j + 1) * LANES)
        key_at = slice(width + j * LANES, width + (j + 1) * LANES)
        value_at = slice(2 * width + j * LANES, 2 * width + (j + 1) * LANES)
        q2 = stack_heads(joined[:, at], first, FACTOR)
        g2 = stack_heads(do1[:, at], first, 1.0)
        key, value = joined[:, key_at], joined[:, value_at]
        scores = dot_nt(q2, key)
        power = jnp.exp(scores - jnp.max(scores, axis=1, keepdims=True))
        prob = power / jnp.sum(power, axis=1, keepdims=True)
        d_prob = dot_nt(g2, value)
        d_scores = (prob * (d_prob - jnp.sum(d_prob * prob, axis=1, keepdims=True))).astype(BF)
        da_ref[:, at] = (unstack_heads(dot_nn(d_scores, key), first) * FACTOR).astype(BF)
        da_ref[:, key_at] = product_left(d_scores, q2).astype(BF)
        da_ref[:, value_at] = product_left(prob.astype(BF), g2).astype(BF)
    d_tok[...] = dr1 + dot_nt(da_ref[...], w_in[...])
    third = 3 * width // 4
    share = width // 4
    da = da_ref[...]
    for i in range(4):
        quarters[i, :, 0:third] = da[:, i * third : (i + 1) * third]
        quarters[i, :, third : third + share] = dy1[:, i * share : (i + 1) * share]
        quarters[i, :, width : width + share] = dqc[:, i * share : (i + 1) * share]
    for k, out in enumerate((out0, out1, out2, out3)):
        out[...] = quarters[rep ^ k]


def owner_backward(where_ref, *refs):
    groups = 8
    qc_near, qc_far, do_near, do_far, kv, dkv, q_ref, g_ref, sum_ref = refs
    _, rows, width = qc_near.shape
    first = head_masks(rows)
    for k in range(groups):
        query = (qc_far if k % 2 else qc_near)[k // 2]
        extra = (do_far if k % 2 else do_near)[k // 2]
        sums = extra[rows : rows + 16, :].astype(F32)
        third = width // 3
        sum_ref[k] = sums[:, 0:third] + sums[:, third : 2 * third] + sums[:, 2 * third :]
        for j in range(PAIRS):
            at = slice(j * LANES, (j + 1) * LANES)
            q_ref[k, j] = stack_heads(query[:, at], first, FACTOR)
            g_ref[k, j] = stack_heads(extra[0:rows, at], first, 1.0)
    blocks = kv.shape[0] // BLK

    def one_block(b, carry):
        group = where_ref[b]
        row = pl.multiple_of(b * BLK, BLK)
        for j in range(PAIRS):
            key_at = slice(j * LANES, (j + 1) * LANES)
            value_at = slice(width + j * LANES, width + (j + 1) * LANES)
            key = kv[pl.ds(row, BLK), key_at]
            value = kv[pl.ds(row, BLK), value_at]
            q2 = q_ref[group, j]
            g2 = g_ref[group, j]
            log_sum = sum_ref[group, j : j + 1, :]
            delta = sum_ref[group, 8 + j : 9 + j, :]
            prob = jnp.exp(dot_nt(key, q2) - log_sum)
            grad = (prob * (dot_nt(value, g2) - delta)).astype(BF)
            dkv[pl.ds(row, BLK), key_at] = dot_nn(grad, q2).astype(BF)
            dkv[pl.ds(row, BLK), value_at] = dot_nn(prob.astype(BF), g2).astype(BF)
        return carry

    lax.fori_loop(0, blocks, one_block, 0)


def memory_weights(rep_ref, dkv, memory_turned, keep, send):
    quarter = dkv.shape[1] // 4
    rep = rep_ref[0]
    for k in range(4):
        at = pl.multiple_of((rep ^ k) * quarter, LANES)
        out = (keep, send)[k % 2]
        out[k // 2] = dot_nn(memory_turned[...], dkv[:, pl.ds(at, quarter)]).astype(BF)


def memory_backward(dkv, w_kv, d_memory):
    half = dkv.shape[0] // 2
    for i in range(2):
        span = slice(i * half, (i + 1) * half)
        d_memory[span, :] = dot_nt(dkv[span, :], w_kv[...]).astype(BF)


def own_keys(memory_ref, w_kv, kv, turned):
    kv[...] = dot_nn(memory_ref[...], w_kv[...]).astype(BF)
    turned[...] = memory_ref[...].T


def weight_blocks(plan, whole, ready, extra, bits_ref, *refs):
    left_all, right_all, product = refs[-3:]
    count = 5 if whole else 4
    outs, arrays = refs[-3 - count : -3], refs[: -3 - count]
    width, depth = left_all.shape
    rows = depth // 4
    tall = width // 8

    def blocks_of(group):
        bit = bits_ref[group]
        for i in range(4):
            for out, b in ((outs[2 * group], 1 - bit), (outs[2 * group + 1], bit)):
                if group == 0:
                    yield out, i, 2 * i + b
                else:
                    yield out, i, 4 * (i // 2) + 2 * b + i % 2

    def multiply(lefts, rights, turned, cols):
        for k, ((a, row), (g, off)) in enumerate(zip(lefts, rights)):
            span = slice(k * rows, (k + 1) * rows)
            left_all[:, span] = arrays[a][row : row + width, :]
            right = arrays[g][off : off + cols, :].T if turned else arrays[g][:, off : off + cols]
            right_all[span, 0:cols] = right
        return dot_nn(left_all[...], right_all[:, 0:cols])

    for lefts, rights, turned, cols, group, to in plan:
        product[:, 0:cols] = multiply(lefts, rights, turned, cols)
        for out, i, block in blocks_of(group):
            at = pl.multiple_of(block * tall, 16)
            out[i, 0:tall, to : to + cols] = product[pl.ds(at, tall), 0:cols].astype(BF)
    if whole:
        outs[4][...] = multiply(*whole).astype(BF)
    if ready:
        source, group, to = ready
        cols = arrays[source].shape[1]
        for out, i, block in blocks_of(group):
            at = pl.multiple_of(block * tall, 16)
            out[i, 0:tall, to : to + cols] = arrays[source][pl.ds(at, tall), :]
    if extra is not None:
        for group in range(2):
            for out, i, block in blocks_of(group):
                out[i, tall:, :] = jnp.zeros_like(out[i, tall:, :])
                if group == 0:
                    out[i, tall:, 0:LANES] = arrays[extra][block].astype(BF)


def fold_two(bits_ref, kept0, got0, kept1, got1, give0, mine0, give1, mine1):
    for bit, kept, got, give, mine in (
        (bits_ref[1], kept0, got0, give0, mine0),
        (bits_ref[0], kept1, got1, give1, mine1),
    ):
        for i in range(2):
            for out, at in ((give, 2 * i + 1 - bit), (mine, 2 * i + bit)):
                out[i] = (kept[at].astype(F32) + got[at].astype(F32)).astype(BF)


def fold_high(bits_ref, *refs):
    (give, mine), arrays = refs[-2:], refs[:-2]
    bit = bits_ref[2]
    for g in range(len(arrays) // 2):
        kept, got = arrays[2 * g], arrays[2 * g + 1]
        for out, at in ((give, 1 - bit), (mine, bit)):
            out[g] = (kept[at].astype(F32) + got[at].astype(F32)).astype(BF)


def fold_one(bits_ref, kept, got, give, mine):
    bit = bits_ref[1]
    for i in range(2):
        for out, at in ((give, 2 * i + 1 - bit), (mine, 2 * i + bit)):
            out[i] = (kept[at].astype(F32) + got[at].astype(F32)).astype(BF)


def fold_last(kept, got, out):
    out[...] = (kept[...].astype(F32) + got[...].astype(F32)).astype(BF)


def fold_core(kept, got, near, far):
    near[...] = kept[0].astype(F32) + got[0].astype(F32)
    far[...] = (kept[1].astype(F32) + got[1].astype(F32)).astype(BF)


def fold_rep(bits_ref, near, got, send, keep):
    y = bits_ref[0]
    tall = send.shape[1]
    for z in range(4):
        for out, bit in ((send, 1 - y), (keep, y)):
            at = pl.multiple_of((2 * z + bit) * tall, 16)
            out[z] = (near[pl.ds(at, tall), :] + got[pl.ds(at, tall), :].astype(F32)).astype(BF)


def lay_columns(plan, rep_ref, *refs):
    pieces, outs, held = refs[0:4], refs[4:-1], refs[-1]
    rep = rep_ref[0]
    for k in range(4):
        held[k] = pieces[k][...]
    for (group, start, cols, how), out in zip(plan, outs):
        if how == "sum":
            tall = out.shape[0]
            total = None
            for k in range(4):
                part = pieces[k][group, pieces[k].shape[1] - tall :, start : start + cols].astype(F32)
                total = part if total is None else total + part
            out[...] = total
            continue
        tall = out.shape[0] if how == "side" else out.shape[0] // 4
        for q in range(4):
            part = held[rep ^ q, group, 0:tall, start : start + cols].astype(F32)
            if how == "side":
                out[:, q * cols : (q + 1) * cols] = part
            else:
                out[q * tall : (q + 1) * tall, :] = part


ORDER = ('dq', 'self', 'owner', 'ff1', 'kv0', 'rest1', 'kv1', 'ff2', 'kv2', 'ff3', 'rest2', 'kv3', 'memory', 'rest3', 'kv4', 'ff4', 'rest4', 'kv5', 'lay_ff', 'lay_rest', 'lay_kv')
BEFORE = {'cross': ('early',), 'ffn': ('qc_z',), 'self': ('qc_y', 'do_stack'), 'ff1': ('exports',)}
RELAY = ()
COSTS = {'deal': 2, 'self_forward': 5, 'own_keys': 6, 'cross': 17, 'ffn': 12, 'dq': 20, 'self': 12, 'ff1': 5, 'rest1': 5, 'owner': 12, 'kv0': 7, 'memory': 6}
LIMITS = {'self': 46}


def fast_on_device(
    queries, memory, routes, w_self, w_self_out, w_cross_q, w_cross_kv, w_cross_out, w_up, b_up,
    w_down, b_down, gain_one, shift_one, gain_two, shift_two, gain_three, shift_three, cotangent,
):
    streams, reps = lax.axis_size("stream"), lax.axis_size("rep")
    me, rep = lax.axis_index("stream"), lax.axis_index("rep")
    width = w_self_out.shape[0]
    hidden = w_up.shape[1]
    quarter, share, tall = hidden // 4, width // 4, width // streams
    tokens = queries[0]
    rows = tokens.shape[0]
    memory_rows = memory[0]
    rep_scalar = rep.reshape(1).astype(jnp.int32)
    bits = jnp.stack([me % 2, (me // 2) % 2, me // 4]).astype(jnp.int32)
    row_of = lambda v: v.reshape(1, -1)
    last = []

    def after(first, *others):
        return lax.optimization_barrier((first, others))[0]

    moving = {}

    def run(name, body, outs, arrays, **more):
        held = last + [array for key in BEFORE.get(name, ()) for array in moving[key]]
        if held:
            arrays = [after(arrays[0], *held)] + list(arrays[1:])
        results = local_kernel(body, outs, arrays=arrays, cost=COSTS.get(name, 2), limit=LIMITS.get(name, 24), **more)
        last[:] = results[:1]
        return results

    def hop(array, stream_flip=0, rep_flip=0):
        pairs = [
            (s * reps + r, (s ^ stream_flip) * reps + (r ^ rep_flip))
            for s in range(streams)
            for r in range(reps)
        ]
        return lax.ppermute(array, AXES, pairs)

    def stream_along(array):
        return [hop(array, k) for k in (2, 4, 6)]

    def stream_across(array, near):
        near = jnp.stack([array] + near)
        return [near, hop(near, 1)]

    def rep_full(array):
        far = hop(array, 0, 2)
        return [array, hop(array, 0, 1), far, hop(far, 0, 1)]

    def rep_each(parts):
        return [parts[0]] + [hop(parts[k], 0, k) for k in range(1, 4)]

    (parcels_out,) = run(
        "deal",
        deal_blocks,
        [like((streams, 2 * BLK, width), BF)],
        [memory_rows],
        scalars=[routes],
    )
    parcels = lax.all_to_all(parcels_out, "stream", split_axis=0, concat_axis=0, tiled=True)
    joined, r1, h1, qc, turned1 = run(
        "self_forward",
        self_forward,
        [
            like((rows, 3 * width), BF),
            like((rows, width), F32),
            like((rows, width), BF),
            like((rows, width), BF),
            like((3 * width, rows), BF),
        ],
        [tokens, w_self, w_self_out, w_cross_q, row_of(gain_one), row_of(shift_one)],
    )
    early = rep_full(turned1)
    moving["early"] = early
    kv_own, memory_turned = run(
        "own_keys",
        own_keys,
        [like((memory_rows.shape[0], 2 * width), BF), like(memory_rows.shape[::-1], BF)],
        [memory_rows, w_cross_kv],
    )
    routes_all = lax.all_gather(
        after(routes[0], kv_own, *early), "stream", axis=0, tiled=False
    )
    keys = streams * 2 * BLK
    o2, kv, sums, bias = run(
        "cross",
        cross_forward,
        [
            like((rows, width), BF),
            like((keys, 2 * width), BF),
            like((2 * rows, LANES), F32),
            like((8, keys), F32),
        ],
        [qc, parcels, w_cross_kv],
        scalars=[routes_all, me.reshape(1).astype(jnp.int32)],
        scratch=[pltpu.VMEM((2 * rows, keys), F32), pltpu.VMEM((2 * rows, keys), BF)],
    )
    qc_near = stream_along(after(qc, parcels))
    qc_all = stream_across(qc, qc_near)
    moving["qc_z"], moving["qc_stack"], moving["qc_y"] = qc_near, qc_all[:1], qc_all[1:]

    vec = jnp.concatenate([row_of(v) for v in (gain_two, shift_two, gain_three, shift_three)])
    each = 2 * quarter + share
    layer_out, dr2, do2, sums2, small_ff, small_up, *parts = run(
        "ffn",
        feed_forward,
        [
            like((rows, width), BF),
            like((rows, width), F32),
            like((rows + 16, width), BF),
            like((2 * rows, LANES), F32),
            like((8, width), F32),
            like((1, hidden), F32),
            like((each, rows), BF),
            like((3 * width + each, rows), BF),
            like((3 * width + 2 * each, rows), BF),
        ],
        [
            o2, h1, sums, w_cross_out, w_up, w_down, row_of(b_up), row_of(b_down), vec,
            cotangent[0],
        ],
        scalars=[rep_scalar],
        scratch=[
            pltpu.VMEM((rows, hidden), F32),
            pltpu.VMEM((hidden, rows), BF),
            pltpu.VMEM((hidden, rows), BF),
        ],
    )
    near, far = hop(parts[1], 0, 1), hop(parts[2], 0, 2)
    do2_near = stream_along(do2)
    do2_all = stream_across(do2, do2_near)
    moving["do_z"], moving["do_stack"], moving["do_y"] = do2_near, do2_all[:1], do2_all[1:]
    moving["near"], moving["far"] = [near], [far]
    v = {}

    def step_dq():
        (v["dqc"],) = run(
            "dq", cross_backward, [like((rows, width), BF)], [qc, do2, kv, bias, sums2]
        )

    def step_self():
        v["d_tokens"], v["small_self"], *exports = run(
            "self",
            self_backward,
            [like((rows, width), F32), like((8, width), F32)]
            + [like((rows, width + share), BF)] * 4,
            [v["dqc"], dr2, r1, joined, w_cross_q, w_self_out, w_self, row_of(gain_one)],
            scalars=[rep_scalar],
            scratch=[
                pltpu.VMEM((rows, 3 * width), BF),
                pltpu.VMEM((4, rows, width + share), BF),
            ],
        )
        v["grads"] = rep_each(exports)
        moving["exports"] = v["grads"][1:]
        relayed = hop(after(far, v["small_self"], *[a for k in RELAY for a in moving[k]]), 0, 1)
        moving["relay"] = [relayed]
        v["shared"] = [parts[1], near, far, relayed, parts[0]]

    def full_at(row):
        return ((0, row), (1, row), (2, each + row), (3, each + row))

    def each_at(row):
        return ((4, row), (1, 3 * width + row), (2, row), (3, each + 3 * width + row))

    def blocks_of(name, plan, arrays, size, wide, whole=None, ready=None, extra=None):
        return run(
            name,
            functools.partial(weight_blocks, plan, whole, ready, extra),
            [like((4, size, wide), BF)] * 4 + ([like((width, whole[3]), BF)] if whole else []),
            arrays,
            scalars=[bits],
            scratch=[
                pltpu.VMEM((width, 4 * rows), BF),
                pltpu.VMEM((4 * rows, width), BF),
                pltpu.VMEM((width, width), F32),
            ],
        )

    def first_hops(key, blocks):
        send0, keep0, send1, keep1 = blocks
        v[key] = [keep0, hop(send0, 1), keep1, hop(send1, 2)]

    def second_hops(name, key):
        give0, mine0, give1, mine1 = run(
            name, fold_two, [like((2,) + v[key][0].shape[1:], BF)] * 4, v[key], scalars=[bits]
        )
        v[key] = [mine0, hop(give0, 2), mine1, hop(give1, 1)]

    def third_hop(name, key):
        arrays = v[key]
        give, mine = run(
            name,
            fold_high,
            [like((len(arrays) // 2,) + arrays[0].shape[1:], BF)] * 2,
            arrays,
            scalars=[bits],
        )
        v[key] = [mine, hop(give, 4)]

    def last_hops(name, key):
        (piece,) = run(name, fold_last, [like(v[key][0].shape, BF)], v[key])
        v[key] = rep_full(piece)

    def gathered(name, key, plan, shapes):
        return run(
            name,
            functools.partial(lay_columns, plan),
            [like(shape, F32) for shape in shapes],
            v[key],
            scalars=[rep_scalar],
            scratch=[pltpu.VMEM((4,) + v[key][0].shape, BF)],
        )

    def step_ff1():
        *blocks, v["cross_out"] = blocks_of(
            "ff1",
            [
                (full_at(0), each_at(quarter), True, quarter, 0, 0),
                (each_at(0), full_at(2 * width), True, width, 1, 0),
            ],
            v["shared"],
            tall,
            width,
            whole=(full_at(width), each_at(2 * quarter), True, share),
        )
        first_hops("ff", blocks)
        moving["ff_first"] = [v["ff"][1], v["ff"][3]]

    def step_rest1():
        vectors = jnp.concatenate([small_ff[0:5], v["small_self"][0:2]]).reshape(7, streams, tall)
        vectors = jnp.pad(vectors.transpose(1, 0, 2), ((0, 0), (0, 0), (0, LANES - tall)))
        vectors = jnp.concatenate(
            [
                vectors,
                small_up.reshape(streams, -1, LANES),
                jnp.zeros((streams, 9 - hidden // streams // LANES, LANES), F32),
            ],
            axis=1,
        )
        early_at = lambda row: tuple((k, row) for k in range(4))
        grads_at = lambda col: tuple((4 + k, col) for k in range(4))
        first_hops(
            "rest",
            blocks_of(
                "rest1",
                [
                    (early_at(0), grads_at(0), False, 3 * share, 0, 0),
                    (early_at(width), grads_at(3 * share), False, share, 1, 0),
                    (early_at(2 * width), grads_at(4 * share), False, share, 1, share),
                ],
                early + v["grads"] + [vectors, v["cross_out"]],
                tall + 16,
                3 * share,
                ready=(9, 1, 2 * share),
                extra=8,
            ),
        )
        moving["rest_first"] = [v["rest"][1], v["rest"][3]]

    kv_wide = 2 * width // 4

    def step_owner():
        (v["dkv"],) = run(
            "owner",
            owner_backward,
            [like((memory_rows.shape[0], 2 * width), BF)],
            qc_all + do2_all + [kv_own],
            scalars=[(routes[0] ^ me).astype(jnp.int32)],
            scratch=[
                pltpu.VMEM((streams, PAIRS, 2 * rows, LANES), BF),
                pltpu.VMEM((streams, PAIRS, 2 * rows, LANES), BF),
                pltpu.VMEM((streams, 16, 2 * rows), F32),
            ],
        )

    def step_kv0():
        kv_keep, kv_send = run(
            "kv0",
            memory_weights,
            [like((2, width, kv_wide), BF)] * 2,
            [v["dkv"], memory_turned],
            scalars=[rep_scalar],
        )
        v["kv"] = [kv_keep, hop(kv_send, 0, 1)]

    def step_kv1():
        near_sum, far_sum = run(
            "kv1", fold_core, [like((width, kv_wide), F32), like((width, kv_wide), BF)], v["kv"]
        )
        v["kv"] = [near_sum, hop(far_sum, 0, 2)]

    def step_kv2():
        send, keep = run(
            "kv2", fold_rep, [like((4, tall, kv_wide), BF)] * 2, v["kv"], scalars=[bits]
        )
        v["kv"] = [keep, hop(send, 1)]

    def step_kv3():
        give, mine = run(
            "kv3", fold_one, [like((2, tall, kv_wide), BF)] * 2, v["kv"], scalars=[bits]
        )
        v["kv"] = [mine, hop(give, 2)]

    def step_memory():
        (v["d_memory"],) = run(
            "memory", memory_backward, [like(memory_rows.shape, BF)], [v["dkv"], w_cross_kv]
        )

    def step_lay_ff():
        v["g_up"], v["g_down"] = gathered(
            "lay_ff",
            "ff",
            [(0, 0, quarter, "side"), (1, 0, width, "below")],
            [(tall, hidden), (hidden // streams, width)],
        )

    def step_lay_rest():
        v["g_self"], v["g_self_out"], v["g_query"], v["g_out"], v["g_vec"] = gathered(
            "lay_rest",
            "rest",
            [
                (0, 0, 3 * share, "side"),
                (1, 0, share, "side"),
                (1, share, share, "side"),
                (1, 2 * share, share, "side"),
                (0, 0, LANES, "sum"),
            ],
            [(tall, 3 * width), (tall, width), (tall, width), (tall, width), (16, LANES)],
        )

    def step_lay_kv():
        (v["g_kv"],) = gathered("lay_kv", "kv", [(0, 0, kv_wide, "side")], [(tall, 2 * width)])

    steps = {
        "dq": step_dq,
        "self": step_self,
        "ff1": step_ff1,
        "rest1": step_rest1,
        "owner": step_owner,
        "kv0": step_kv0,
        "kv1": step_kv1,
        "kv2": step_kv2,
        "kv3": step_kv3,
        "kv4": lambda: third_hop("kv4", "kv"),
        "kv5": lambda: last_hops("kv5", "kv"),
        "ff2": lambda: second_hops("ff2", "ff"),
        "ff3": lambda: third_hop("ff3", "ff"),
        "ff4": lambda: last_hops("ff4", "ff"),
        "rest2": lambda: second_hops("rest2", "rest"),
        "rest3": lambda: third_hop("rest3", "rest"),
        "rest4": lambda: last_hops("rest4", "rest"),
        "memory": step_memory,
        "lay_ff": step_lay_ff,
        "lay_rest": step_lay_rest,
        "lay_kv": step_lay_kv,
    }
    for name in ORDER:
        steps[name]()
    piece = lambda row: v["g_vec"][row, 0:tall]
    return (
        layer_out[None],
        v["d_tokens"][None],
        v["d_memory"][None],
        v["g_self"],
        v["g_self_out"],
        v["g_query"],
        v["g_kv"],
        v["g_out"],
        v["g_up"],
        v["g_vec"][7 : 7 + hidden // streams // LANES].reshape(-1),
        v["g_down"],
        piece(0),
        piece(5),
        piece(6),
        piece(1),
        piece(2),
        piece(3),
        piece(4),
    )


def solution(mesh):
    in_specs = (
        P("rep", "stream", None),
        P("rep", "stream", None),
        P("rep", "stream"),
        P(),
        P(),
        P(),
        P(),
        P(),
        P(),
        P(),
        P(),
        P(),
        P(),
        P(),
        P(),
        P(),
        P(),
        P(),
        P("rep", "stream", None),
    )
    out_specs = (
        P("rep", "stream", None),
        P("rep", "stream", None),
        P("rep", "stream", None),
        P("stream", None),
        P("stream", None),
        P("stream", None),
        P("stream", None),
        P("stream", None),
        P("stream", None),
        P("stream"),
        P("stream", None),
        P("stream"),
        P("stream"),
        P("stream"),
        P("stream"),
        P("stream"),
        P("stream"),
        P("stream"),
    )
    small_slice = (mesh.shape["stream"], mesh.shape["rep"]) == (8, 4)
    return jax.shard_map(
        fast_on_device if small_slice else on_device, mesh=mesh, in_specs=in_specs, out_specs=out_specs, check_vma=False
    )
```

```python
import functools

import jax
import jax.numpy as jnp
from jax import lax
from jax.experimental import pallas as pl
from jax.experimental.pallas import tpu as pltpu
from jax.sharding import PartitionSpec as P

HEADS = 12
HEAD_DIM = 64
BLK = 128


def matmul(left, right):
    return jnp.dot(left, right, preferred_element_type=jnp.float32)


def product_left(left, right):
    return lax.dot_general(
        left, right, (((0,), (0,)), ((), ())), preferred_element_type=jnp.float32
    )


def product_right(left, right):
    return lax.dot_general(
        left, right, (((1,), (1,)), ((), ())), preferred_element_type=jnp.float32
    )


def layer_norm(rows, gain, shift):
    centred = rows - jnp.mean(rows, axis=-1, keepdims=True)
    spread = jnp.mean(centred * centred, axis=-1, keepdims=True)
    return centred * lax.rsqrt(spread + 1e-05) * gain + shift


def split_heads(rows):
    return rows.reshape(rows.shape[0], HEADS, HEAD_DIM).transpose(1, 0, 2)


def join_heads(rows):
    return rows.transpose(1, 0, 2).reshape(rows.shape[1], HEADS * HEAD_DIM)


def masked_scores(query_head, key_head, key_ok):
    scores = product_right(query_head, key_head) * HEAD_DIM ** (-0.5)
    if key_ok is not None:
        scores = jnp.where(key_ok[None, :], scores, -1e30)
    return scores


def attend_forward(query, key_rows, value_rows, key_ok):

    def one_head(item):
        query_head, key_head, value_head = item
        scores = masked_scores(query_head, key_head, key_ok)
        row_max = jnp.max(scores, axis=1, keepdims=True)
        exponent = jnp.exp(scores - row_max)
        row_total = jnp.sum(exponent, axis=1, keepdims=True)
        probability = (exponent / row_total).astype(jnp.bfloat16)
        return (matmul(probability, value_head), (row_max + jnp.log(row_total))[:, 0])

    mixed, log_total = lax.map(
        one_head, (split_heads(query), split_heads(key_rows), split_heads(value_rows))
    )
    return (join_heads(mixed), log_total)


def attend_backward(query, key_rows, value_rows, key_ok, log_total, d_mixed):
    factor = HEAD_DIM ** (-0.5)

    def one_head(item):
        query_head, key_head, value_head, total_head, grad_head = item
        scores = masked_scores(query_head, key_head, key_ok)
        probability = jnp.exp(scores - total_head[:, None])
        d_prob = product_right(grad_head, value_head)
        d_scores = probability * (d_prob - jnp.sum(d_prob * probability, axis=1, keepdims=True))
        d_scores = d_scores.astype(jnp.bfloat16)
        d_query = matmul(d_scores, key_head) * factor
        d_key = product_left(d_scores, query_head) * factor
        d_value = product_left(probability.astype(jnp.bfloat16), grad_head)
        return (d_query, d_key, d_value)

    d_query, d_key, d_value = lax.map(
        one_head,
        (
            split_heads(query),
            split_heads(key_rows),
            split_heads(value_rows),
            log_total,
            split_heads(d_mixed),
        ),
    )
    return (join_heads(d_query), join_heads(d_key), join_heads(d_value))


def on_device(
    queries,
    memory,
    routes,
    w_self,
    w_self_out,
    w_cross_q,
    w_cross_kv,
    w_cross_out,
    w_up,
    b_up,
    w_down,
    b_down,
    gain_one,
    shift_one,
    gain_two,
    shift_two,
    gain_three,
    shift_three,
    cotangent,
):
    streams = lax.axis_size("stream")
    blocks = routes.shape[1]
    capacity = max(2, 2 * blocks // streams)
    slot_count = streams * capacity
    model_width = w_self_out.shape[0]
    target = routes[0]
    hit_table = (target[:, None] == jnp.arange(streams, dtype=jnp.int32)[None, :]).astype(jnp.int32)
    before = jnp.cumsum(hit_table, axis=0) - hit_table
    rank_in = jnp.sum(before * hit_table, axis=1)
    slot_of_block = target * capacity + rank_in
    matched = (slot_of_block[None, :] == jnp.arange(slot_count, dtype=jnp.int32)[:, None]).astype(
        jnp.int32
    )
    block_at = jnp.sum(matched * jnp.arange(blocks, dtype=jnp.int32)[None, :], axis=1)
    live_slot = jnp.sum(matched, axis=1)
    live_grid = live_slot.reshape(streams, capacity)
    filled = (live_slot > 0)[:, None, None]
    nothing = jnp.zeros((), jnp.bfloat16)
    memory_rows = memory[0]
    projected = (
        matmul(memory_rows, w_cross_kv).astype(jnp.bfloat16).reshape(blocks, BLK, 2 * model_width)
    )
    outgoing = jnp.where(filled, jnp.take(projected, block_at, axis=0), nothing)
    arrived, arrived_live = (
        lax.all_to_all(
            outgoing.reshape(streams, capacity, BLK, 2 * model_width),
            "stream",
            split_axis=0,
            concat_axis=0,
            tiled=True,
        ),
        lax.all_to_all(live_grid, "stream", split_axis=0, concat_axis=0, tiled=True),
    )
    keys_values = arrived.reshape(-1, 2 * model_width)
    key_ok = jnp.repeat(arrived_live.reshape(-1), BLK) > 0
    key_cross = keys_values[:, :model_width]
    value_cross = keys_values[:, model_width:]
    gain_a = gain_one.astype(jnp.float32)
    shift_a = shift_one.astype(jnp.float32)
    gain_b = gain_two.astype(jnp.float32)
    shift_b = shift_two.astype(jnp.float32)
    gain_c = gain_three.astype(jnp.float32)
    shift_c = shift_three.astype(jnp.float32)
    tokens = queries[0]
    joined = matmul(tokens, w_self).astype(jnp.bfloat16)
    query_self = joined[:, :model_width]
    key_self = joined[:, model_width : 2 * model_width]
    value_self = joined[:, 2 * model_width :]
    mixed_self, total_self = attend_forward(query_self, key_self, value_self, None)
    mixed_self = mixed_self.astype(jnp.bfloat16)
    residual_one = tokens.astype(jnp.float32) + matmul(mixed_self, w_self_out)
    normed_one = layer_norm(residual_one, gain_a, shift_a).astype(jnp.bfloat16)
    query_cross = matmul(normed_one, w_cross_q).astype(jnp.bfloat16)
    mixed_cross, total_cross = attend_forward(query_cross, key_cross, value_cross, key_ok)
    mixed_cross = mixed_cross.astype(jnp.bfloat16)
    residual_two = normed_one.astype(jnp.float32) + matmul(mixed_cross, w_cross_out)
    normed_two = layer_norm(residual_two, gain_b, shift_b).astype(jnp.bfloat16)
    hidden_pre = matmul(normed_two, w_up) + b_up.astype(jnp.float32)
    hidden = jax.nn.gelu(hidden_pre, approximate=False).astype(jnp.bfloat16)
    residual_three = (
        normed_two.astype(jnp.float32) + matmul(hidden, w_down) + b_down.astype(jnp.float32)
    )
    layer_out = layer_norm(residual_three, gain_c, shift_c).astype(jnp.bfloat16)
    grad_out = cotangent[0].astype(jnp.float32)
    norm_three_pull = jax.vjp(layer_norm, residual_three, gain_c, shift_c)[1]
    d_residual_three, d_gain_c, d_shift_c = norm_three_pull(grad_out)
    d_branch_three = d_residual_three.astype(jnp.bfloat16)
    d_b_down = jnp.sum(d_branch_three.astype(jnp.float32), axis=0)
    d_w_down = product_left(hidden, d_branch_three)
    d_hidden = product_right(d_branch_three, w_down)
    gelu_pull = jax.vjp(lambda value: jax.nn.gelu(value, approximate=False), hidden_pre)[1]
    d_hidden_pre = gelu_pull(d_hidden)[0].astype(jnp.bfloat16)
    d_b_up = jnp.sum(d_hidden_pre.astype(jnp.float32), axis=0)
    d_w_up = product_left(normed_two, d_hidden_pre)
    d_normed_two = d_residual_three + product_right(d_hidden_pre, w_up)
    norm_two_pull = jax.vjp(layer_norm, residual_two, gain_b, shift_b)[1]
    d_residual_two, d_gain_b, d_shift_b = norm_two_pull(d_normed_two)
    d_branch_two = d_residual_two.astype(jnp.bfloat16)
    d_w_cross_out = product_left(mixed_cross, d_branch_two)
    d_mixed_cross = product_right(d_branch_two, w_cross_out).astype(jnp.bfloat16)
    d_query_cross, d_key_cross, d_value_cross = attend_backward(
        query_cross, key_cross, value_cross, key_ok, total_cross, d_mixed_cross
    )
    d_query_cross = d_query_cross.astype(jnp.bfloat16)
    d_keys_values = jnp.concatenate([d_key_cross, d_value_cross], axis=1).astype(jnp.bfloat16)
    d_w_cross_q = product_left(normed_one, d_query_cross)
    d_normed_one = d_residual_two + product_right(d_query_cross, w_cross_q)
    norm_one_pull = jax.vjp(layer_norm, residual_one, gain_a, shift_a)[1]
    d_residual_one, d_gain_a, d_shift_a = norm_one_pull(d_normed_one)
    d_branch_one = d_residual_one.astype(jnp.bfloat16)
    d_w_self_out = product_left(mixed_self, d_branch_one)
    d_mixed_self = product_right(d_branch_one, w_self_out).astype(jnp.bfloat16)
    d_query_self, d_key_self, d_value_self = attend_backward(
        query_self, key_self, value_self, None, total_self, d_mixed_self
    )
    d_joined = jnp.concatenate([d_query_self, d_key_self, d_value_self], axis=1).astype(
        jnp.bfloat16
    )
    d_w_self = product_left(tokens, d_joined)
    d_tokens = d_residual_one + product_right(d_joined, w_self)
    returned = lax.all_to_all(
        d_keys_values.reshape(streams, capacity, BLK, 2 * model_width),
        "stream",
        split_axis=0,
        concat_axis=0,
        tiled=True,
    )
    d_block_rows = jnp.take(
        returned.reshape(slot_count, BLK, 2 * model_width), slot_of_block, axis=0
    ).reshape(-1, 2 * model_width)
    d_w_cross_kv = product_left(memory_rows, d_block_rows)
    d_memory = product_right(d_block_rows, w_cross_kv).astype(jnp.bfloat16)
    gradients = (
        d_w_self,
        d_w_self_out,
        d_w_cross_q,
        d_w_cross_kv,
        d_w_cross_out,
        d_w_up,
        d_b_up,
        d_w_down,
        d_b_down,
        d_gain_a,
        d_shift_a,
        d_gain_b,
        d_shift_b,
        d_gain_c,
        d_shift_c,
    )
    shapes = [item.shape for item in gradients]
    flat = [item.reshape(-1) for item in gradients]
    (
        share_self,
        share_self_out,
        share_cross_q,
        share_cross_kv,
        share_cross_out,
        share_up,
        share_b_up,
        share_down,
        share_b_down,
        share_gain_a,
        share_shift_a,
        share_gain_b,
        share_shift_b,
        share_gain_c,
        share_shift_c,
    ) = (
        lax.psum_scatter(flat[0], "stream", scatter_dimension=0, tiled=True),
        lax.psum_scatter(flat[1], "stream", scatter_dimension=0, tiled=True),
        lax.psum_scatter(flat[2], "stream", scatter_dimension=0, tiled=True),
        lax.psum_scatter(flat[3], "stream", scatter_dimension=0, tiled=True),
        lax.psum_scatter(flat[4], "stream", scatter_dimension=0, tiled=True),
        lax.psum_scatter(flat[5], "stream", scatter_dimension=0, tiled=True),
        lax.psum_scatter(flat[6], "stream", scatter_dimension=0, tiled=True),
        lax.psum_scatter(flat[7], "stream", scatter_dimension=0, tiled=True),
        lax.psum_scatter(flat[8], "stream", scatter_dimension=0, tiled=True),
        lax.psum_scatter(flat[9], "stream", scatter_dimension=0, tiled=True),
        lax.psum_scatter(flat[10], "stream", scatter_dimension=0, tiled=True),
        lax.psum_scatter(flat[11], "stream", scatter_dimension=0, tiled=True),
        lax.psum_scatter(flat[12], "stream", scatter_dimension=0, tiled=True),
        lax.psum_scatter(flat[13], "stream", scatter_dimension=0, tiled=True),
        lax.psum_scatter(flat[14], "stream", scatter_dimension=0, tiled=True),
    )
    summed = (
        lax.psum(share_self.astype(jnp.bfloat16), "rep").astype(jnp.float32),
        lax.psum(share_self_out.astype(jnp.bfloat16), "rep").astype(jnp.float32),
        lax.psum(share_cross_q.astype(jnp.bfloat16), "rep").astype(jnp.float32),
        lax.psum(share_cross_kv.astype(jnp.bfloat16), "rep").astype(jnp.float32),
        lax.psum(share_cross_out.astype(jnp.bfloat16), "rep").astype(jnp.float32),
        lax.psum(share_up.astype(jnp.bfloat16), "rep").astype(jnp.float32),
        lax.psum(share_b_up.astype(jnp.bfloat16), "rep").astype(jnp.float32),
        lax.psum(share_down.astype(jnp.bfloat16), "rep").astype(jnp.float32),
        lax.psum(share_b_down.astype(jnp.bfloat16), "rep").astype(jnp.float32),
        lax.psum(share_gain_a.astype(jnp.bfloat16), "rep").astype(jnp.float32),
        lax.psum(share_shift_a.astype(jnp.bfloat16), "rep").astype(jnp.float32),
        lax.psum(share_gain_b.astype(jnp.bfloat16), "rep").astype(jnp.float32),
        lax.psum(share_shift_b.astype(jnp.bfloat16), "rep").astype(jnp.float32),
        lax.psum(share_gain_c.astype(jnp.bfloat16), "rep").astype(jnp.float32),
        lax.psum(share_shift_c.astype(jnp.bfloat16), "rep").astype(jnp.float32),
    )
    results = [
        part.reshape((shape[0] // streams,) + tuple(shape[1:]))
        for part, shape in zip(summed, shapes)
    ]
    return (
        layer_out[None],
        d_tokens[None],
        d_memory[None],
        results[0],
        results[1],
        results[2],
        results[3],
        results[4],
        results[5],
        results[6],
        results[7],
        results[8],
        results[9],
        results[10],
        results[11],
        results[12],
        results[13],
        results[14],
    )


PAIRS = HEADS // 2
LANES = 2 * HEAD_DIM
FACTOR = HEAD_DIM ** (-0.5)
BF = jnp.bfloat16
F32 = jnp.float32
AXES = ("stream", "rep")


def whole_in_vmem(count):
    return [pl.BlockSpec(memory_space=pltpu.VMEM)] * count


def local_kernel(body, out_shape, scalars=(), arrays=(), scratch=(), cost=2, limit=24):
    return pl.pallas_call(
        body,
        out_shape=list(out_shape),
        in_specs=[pl.BlockSpec(memory_space=pltpu.SMEM)] * len(scalars) + whole_in_vmem(len(arrays)),
        out_specs=whole_in_vmem(len(out_shape)),
        scratch_shapes=list(scratch),
        compiler_params=pltpu.CompilerParams(vmem_limit_bytes=limit * 1024 * 1024),
        cost_estimate=pl.CostEstimate(
            flops=int(cost * 1.15e9), bytes_accessed=int(cost * 1e5), transcendentals=0
        ),
    )(*scalars, *arrays)


def like(shape, dtype):
    return jax.ShapeDtypeStruct(shape, dtype)


def dot_nn(left, right):
    return lax.dot_general(left, right, (((1,), (0,)), ((), ())), preferred_element_type=F32)


def dot_nt(left, right):
    return lax.dot_general(left, right, (((1,), (1,)), ((), ())), preferred_element_type=F32)


def head_masks(rows):
    lane = lax.broadcasted_iota(jnp.int32, (rows, LANES), 1)
    return lane < HEAD_DIM


def stack_heads(pair, first, scale):
    one = jnp.where(first, scale, 0.0).astype(BF)
    two = jnp.where(first, 0.0, scale).astype(BF)
    return jnp.concatenate([pair * one, pair * two], axis=0)


def unstack_heads(both, first):
    rows = both.shape[0] // 2
    return jnp.where(first, both[:rows], both[rows:])


def norm_parts(rows):
    centred = rows - jnp.mean(rows, axis=1, keepdims=True)
    spread = jnp.mean(centred * centred, axis=1, keepdims=True)
    inverse = lax.rsqrt(spread + 1e-05)
    return centred * inverse, inverse


def norm_pull(grad, hat, inverse, gain):
    scaled = grad * gain
    inner = scaled - jnp.mean(scaled, axis=1, keepdims=True)
    inner = inner - hat * jnp.mean(scaled * hat, axis=1, keepdims=True)
    return (
        inverse * inner,
        jnp.sum(grad * hat, axis=0, keepdims=True),
        jnp.sum(grad, axis=0, keepdims=True),
    )


def deal_blocks(routes_ref, memory_ref, out_ref):
    out_ref[...] = jnp.zeros_like(out_ref)
    blocks = memory_ref.shape[0] // BLK
    for b in range(blocks):
        group = routes_ref[0, b]
        rank = jnp.int32(0)
        for earlier in range(b):
            rank = rank + (routes_ref[0, earlier] == group).astype(jnp.int32)
        row = pl.multiple_of(rank * BLK, BLK)
        out_ref[group, pl.ds(row, BLK), :] = memory_ref[b * BLK : (b + 1) * BLK, :]


def self_forward(tok, w_in, w_out, w_q, gain, shift, joined, r1, h1_out, qc, turned):
    width = tok.shape[1]
    rows = tok.shape[0]
    joined[...] = dot_nn(tok[...], w_in[...]).astype(BF)
    first = head_masks(rows)
    mixed = []
    for j in range(PAIRS):
        at = j * LANES
        q2 = stack_heads(joined[:, at : at + LANES], first, FACTOR)
        key = joined[:, width + at : width + at + LANES]
        value = joined[:, 2 * width + at : 2 * width + at + LANES]
        scores = dot_nt(q2, key)
        power = jnp.exp(scores - jnp.max(scores, axis=1, keepdims=True))
        prob = (power / jnp.sum(power, axis=1, keepdims=True)).astype(BF)
        mixed.append(unstack_heads(dot_nn(prob, value), first).astype(BF))
    o1 = jnp.concatenate(mixed, axis=1)
    res = tok[...].astype(F32) + dot_nn(o1, w_out[...])
    r1[...] = res
    hat, _ = norm_parts(res)
    h1 = (hat * gain[...].astype(F32) + shift[...].astype(F32)).astype(BF)
    h1_out[...] = h1
    qc[...] = dot_nn(h1, w_q[...]).astype(BF)
    turned[0:width, :] = tok[...].T
    turned[width : 2 * width, :] = o1.T
    turned[2 * width : 3 * width, :] = h1.T


def cross_forward(routes_ref, me_ref, qc, parcels, w_kv, o2, kv, sums, bias_ref, s_ref, p_ref):
    width = qc.shape[1]
    rows = qc.shape[0]
    sources = parcels.shape[0]
    span = 2 * BLK
    first = head_masks(rows)
    for k in range(sources):
        kv[k * span : (k + 1) * span, :] = dot_nn(parcels[k, 0:span, :], w_kv[...]).astype(BF)
        count = jnp.int32(0)
        for b in range(routes_ref.shape[1]):
            count = count + (routes_ref[k, b] == me_ref[0]).astype(jnp.int32)
        for c in range(2):
            bias_ref[:, k * span + c * BLK : k * span + (c + 1) * BLK] = jnp.full(
                (8, BLK), jnp.where(count > c, 0.0, -1e30), F32
            )
    lane = lax.broadcasted_iota(jnp.int32, (2 * rows, LANES), 1)
    sums[...] = jnp.zeros_like(sums)

    def one_pair(j, carry):
        at = pl.multiple_of(j * LANES, LANES)
        q2 = stack_heads(qc[:, pl.ds(at, LANES)], first, FACTOR)
        top = None
        for k in range(sources):
            key = kv[k * span : (k + 1) * span, pl.ds(at, LANES)]
            scores = dot_nt(q2, key) + bias_ref[0:1, k * span : (k + 1) * span]
            s_ref[:, k * span : (k + 1) * span] = scores
            most = jnp.maximum(scores[:, :LANES], scores[:, LANES:])
            top = most if top is None else jnp.maximum(top, most)
        peak = jnp.max(top, axis=1, keepdims=True)
        total = None
        for k in range(sources):
            power = jnp.exp(s_ref[:, k * span : (k + 1) * span] - peak)
            p_ref[:, k * span : (k + 1) * span] = power.astype(BF)
            part = power[:, :LANES] + power[:, LANES:]
            total = part if total is None else total + part
        total = jnp.sum(total, axis=1, keepdims=True)
        value = kv[:, pl.ds(pl.multiple_of(width + j * LANES, LANES), LANES)]
        both = dot_nn(p_ref[...], value) / total
        o2[:, pl.ds(at, LANES)] = unstack_heads(both, first).astype(BF)
        sums[...] = jnp.where(lane == j, peak + jnp.log(total), sums[...])
        return carry

    lax.fori_loop(0, PAIRS, one_pair, 0, unroll=PAIRS)


def feed_forward(
    rep_ref, o2, tok_h1, sums, w_co, w_up, w_down, b_up, b_down, vec, cot,
    layer_out, dr2, do2, both_sums, small, small_up, parcel0, parcel1, parcel2,
    slope, acts, dus,
):
    width = o2.shape[1]
    rows = o2.shape[0]
    hidden = w_up.shape[1]
    quarter = hidden // 4
    rep = rep_ref[0]
    gain2, shift2, gain3, shift3 = (vec[i : i + 1, :].astype(F32) for i in range(4))
    res2 = tok_h1[...].astype(F32) + dot_nn(o2[...], w_co[...])
    hat2, inv2 = norm_parts(res2)
    h2 = (hat2 * gain2 + shift2).astype(BF)
    each = 2 * quarter + width // 4
    for parcel, base in ((parcel1, 0), (parcel2, each)):
        parcel[base : base + width, :] = h2.T
        parcel[base + width : base + 2 * width, :] = o2[...].T
    total = None
    for c in range(4):
        cols = slice(c * quarter, (c + 1) * quarter)
        u = dot_nn(h2, w_up[:, cols]) + b_up[:, cols].astype(F32)
        cdf = 0.5 + 0.5 * lax.erf(u * 0.7071067811865476)
        act = (u * cdf).astype(BF)
        slope[:, cols] = cdf + u * (jnp.exp(u * u * -0.5) * 0.3989422804014327)
        acts[cols, :] = act.T
        part = dot_nn(act, w_down[cols, :])
        total = part if total is None else total + part
    res3 = h2.astype(F32) + total + b_down[...].astype(F32)
    hat3, inv3 = norm_parts(res3)
    layer_out[...] = (hat3 * gain3 + shift3).astype(BF)
    dr3, d_gain3, d_shift3 = norm_pull(cot[...].astype(F32), hat3, inv3, gain3)
    dy3 = dr3.astype(BF)
    small[0:1, :] = jnp.sum(dy3.astype(F32), axis=0, keepdims=True)
    small[3:4, :] = d_gain3
    small[4:5, :] = d_shift3
    back = None
    for c in range(4):
        cols = slice(c * quarter, (c + 1) * quarter)
        du = (dot_nt(dy3, w_down[cols, :]) * slope[:, cols]).astype(BF)
        small_up[:, cols] = jnp.sum(du.astype(F32), axis=0, keepdims=True)
        dus[cols, :] = du.T
        part = dot_nt(du, w_up[:, cols])
        back = part if back is None else back + part
    grad2, d_gain2, d_shift2 = norm_pull(dr3 + back, hat2, inv2, gain2)
    small[1:2, :] = d_gain2
    small[2:3, :] = d_shift2
    small[5:8, :] = jnp.zeros((3, width), F32)
    dr2[...] = grad2
    dy2 = grad2.astype(BF)
    grad_mixed = dot_nt(dy2, w_co[...]).astype(BF)
    do2[0:rows, :] = grad_mixed
    lane = lax.broadcasted_iota(jnp.int32, (2 * rows, LANES), 1)
    first = head_masks(rows)
    packed = sums[...]
    for j in range(PAIRS):
        at = slice(j * LANES, (j + 1) * LANES)
        prod = grad_mixed[:, at].astype(F32) * o2[:, at].astype(F32)
        zero = jnp.zeros_like(prod)
        two = jnp.concatenate([jnp.where(first, prod, zero), jnp.where(first, zero, prod)], axis=0)
        packed = jnp.where(lane == 8 + j, jnp.sum(two, axis=1, keepdims=True), packed)
    both_sums[...] = packed
    turned = packed.T[0:16, :]
    high = turned.astype(BF)
    rest = turned - high.astype(F32)
    middle = rest.astype(BF)
    low = (rest - middle.astype(F32)).astype(BF)
    do2[rows : rows + 16, :] = jnp.concatenate([high, middle, low], axis=1)
    share = width // 4
    dy2_turned = dy2.T
    dy3_turned = dy3.T
    strip = quarter // 8
    parcel1[2 * width : 3 * width, :] = dy3_turned
    parcel2[each + 2 * width : each + 3 * width, :] = dy3_turned
    places = ((parcel0, 0), (parcel1, 3 * width), (parcel2, 0), (parcel2, each + 3 * width))
    for k, (parcel, base) in enumerate(places):
        peer = rep ^ k
        for s in range(8):
            row = pl.multiple_of(s * 4 * strip + peer * strip, strip)
            parcel[base + s * strip : base + (s + 1) * strip, :] = acts[pl.ds(row, strip), :]
        row = pl.multiple_of(peer * quarter, quarter)
        parcel[base + quarter : base + 2 * quarter, :] = dus[pl.ds(row, quarter), :]
        piece = dy2_turned[0:share]
        for i in range(1, 4):
            piece = jnp.where(peer == i, dy2_turned[i * share : (i + 1) * share], piece)
        parcel[base + 2 * quarter : base + 2 * quarter + share, :] = piece


def cross_backward(qc, do2, kv, bias_ref, sums, dqc):
    width = qc.shape[1]
    rows = qc.shape[0]
    span = 2 * BLK
    sources = kv.shape[0] // span
    first = head_masks(rows)
    lane = lax.broadcasted_iota(jnp.int32, (2 * rows, LANES), 1)

    def one_pair(j, carry):
        at = pl.multiple_of(j * LANES, LANES)
        q2 = stack_heads(qc[:, pl.ds(at, LANES)], first, FACTOR)
        g2 = stack_heads(do2[0:rows, pl.ds(at, LANES)], first, 1.0)
        packed = sums[...]
        log_sum = jnp.sum(jnp.where(lane == j, packed, 0.0), axis=1, keepdims=True)
        delta = jnp.sum(jnp.where(lane == j + 8, packed, 0.0), axis=1, keepdims=True)
        total = None
        for k in range(sources):
            key = kv[k * span : (k + 1) * span, pl.ds(at, LANES)]
            value = kv[
                k * span : (k + 1) * span, pl.ds(pl.multiple_of(width + j * LANES, LANES), LANES)
            ]
            scores = dot_nt(q2, key) + bias_ref[0:1, k * span : (k + 1) * span]
            prob = jnp.exp(scores - log_sum)
            grad = (prob * (dot_nt(g2, value) - delta)).astype(BF)
            part = dot_nn(grad, key)
            total = part if total is None else total + part
        dqc[:, pl.ds(at, LANES)] = (unstack_heads(total, first) * FACTOR).astype(BF)
        return carry

    lax.fori_loop(0, PAIRS, one_pair, 0, unroll=PAIRS)


def self_backward(
    rep_ref, dqc_ref, dr2, r1, joined, w_q, w_out, w_in, gain,
    d_tok, small, out0, out1, out2, out3,
    da_ref, quarters,
):
    rows, width = dqc_ref.shape
    rep = rep_ref[0]
    first = head_masks(rows)
    dqc = dqc_ref[...]
    grad1 = dr2[...] + dot_nt(dqc, w_q[...])
    hat1, inv1 = norm_parts(r1[...])
    dr1, d_gain1, d_shift1 = norm_pull(grad1, hat1, inv1, gain[...].astype(F32))
    small[0:1, :] = d_gain1
    small[1:2, :] = d_shift1
    small[2:8, :] = jnp.zeros((6, width), F32)
    dy1 = dr1.astype(BF)
    do1 = dot_nt(dy1, w_out[...]).astype(BF)
    for j in range(PAIRS):
        at = slice(j * LANES, (j + 1) * LANES)
        key_at = slice(width + j * LANES, width + (j + 1) * LANES)
        value_at = slice(2 * width + j * LANES, 2 * width + (j + 1) * LANES)
        q2 = stack_heads(joined[:, at], first, FACTOR)
        g2 = stack_heads(do1[:, at], first, 1.0)
        key, value = joined[:, key_at], joined[:, value_at]
        scores = dot_nt(q2, key)
        power = jnp.exp(scores - jnp.max(scores, axis=1, keepdims=True))
        prob = power / jnp.sum(power, axis=1, keepdims=True)
        d_prob = dot_nt(g2, value)
        d_scores = (prob * (d_prob - jnp.sum(d_prob * prob, axis=1, keepdims=True))).astype(BF)
        da_ref[:, at] = (unstack_heads(dot_nn(d_scores, key), first) * FACTOR).astype(BF)
        da_ref[:, key_at] = product_left(d_scores, q2).astype(BF)
        da_ref[:, value_at] = product_left(prob.astype(BF), g2).astype(BF)
    d_tok[...] = dr1 + dot_nt(da_ref[...], w_in[...])
    third = 3 * width // 4
    share = width // 4
    da = da_ref[...]
    for i in range(4):
        quarters[i, :, 0:third] = da[:, i * third : (i + 1) * third]
        quarters[i, :, third : third + share] = dy1[:, i * share : (i + 1) * share]
        quarters[i, :, width : width + share] = dqc[:, i * share : (i + 1) * share]
    for k, out in enumerate((out0, out1, out2, out3)):
        out[...] = quarters[rep ^ k]


def owner_backward(where_ref, *refs):
    groups = 8
    qc_near, qc_far, do_near, do_far, kv, dkv, q_ref, g_ref, sum_ref = refs
    _, rows, width = qc_near.shape
    first = head_masks(rows)
    for k in range(groups):
        query = (qc_far if k % 2 else qc_near)[k // 2]
        extra = (do_far if k % 2 else do_near)[k // 2]
        sums = extra[rows : rows + 16, :].astype(F32)
        third = width // 3
        sum_ref[k] = sums[:, 0:third] + sums[:, third : 2 * third] + sums[:, 2 * third :]
        for j in range(PAIRS):
            at = slice(j * LANES, (j + 1) * LANES)
            q_ref[k, j] = stack_heads(query[:, at], first, FACTOR)
            g_ref[k, j] = stack_heads(extra[0:rows, at], first, 1.0)
    blocks = kv.shape[0] // BLK

    def one_block(b, carry):
        group = where_ref[b]
        row = pl.multiple_of(b * BLK, BLK)
        for j in range(PAIRS):
            key_at = slice(j * LANES, (j + 1) * LANES)
            value_at = slice(width + j * LANES, width + (j + 1) * LANES)
            key = kv[pl.ds(row, BLK), key_at]
            value = kv[pl.ds(row, BLK), value_at]
            q2 = q_ref[group, j]
            g2 = g_ref[group, j]
            log_sum = sum_ref[group, j : j + 1, :]
            delta = sum_ref[group, 8 + j : 9 + j, :]
            prob = jnp.exp(dot_nt(key, q2) - log_sum)
            grad = (prob * (dot_nt(value, g2) - delta)).astype(BF)
            dkv[pl.ds(row, BLK), key_at] = dot_nn(grad, q2).astype(BF)
            dkv[pl.ds(row, BLK), value_at] = dot_nn(prob.astype(BF), g2).astype(BF)
        return carry

    lax.fori_loop(0, blocks, one_block, 0)


def memory_weights(rep_ref, dkv, memory_turned, keep, send):
    quarter = dkv.shape[1] // 4
    rep = rep_ref[0]
    for k in range(4):
        at = pl.multiple_of((rep ^ k) * quarter, LANES)
        out = (keep, send)[k % 2]
        out[k // 2] = dot_nn(memory_turned[...], dkv[:, pl.ds(at, quarter)]).astype(BF)


def memory_backward(dkv, w_kv, d_memory):
    half = dkv.shape[0] // 2
    for i in range(2):
        span = slice(i * half, (i + 1) * half)
        d_memory[span, :] = dot_nt(dkv[span, :], w_kv[...]).astype(BF)


def own_keys(memory_ref, w_kv, kv, turned):
    kv[...] = dot_nn(memory_ref[...], w_kv[...]).astype(BF)
    turned[...] = memory_ref[...].T


def weight_blocks(plan, whole, ready, extra, bits_ref, *refs):
    left_all, right_all, product = refs[-3:]
    count = 5 if whole else 4
    outs, arrays = refs[-3 - count : -3], refs[: -3 - count]
    width, depth = left_all.shape
    rows = depth // 4
    tall = width // 8

    def blocks_of(group):
        bit = bits_ref[group]
        for i in range(4):
            for out, b in ((outs[2 * group], 1 - bit), (outs[2 * group + 1], bit)):
                if group == 0:
                    yield out, i, 2 * i + b
                else:
                    yield out, i, 4 * (i // 2) + 2 * b + i % 2

    def multiply(lefts, rights, turned, cols):
        for k, ((a, row), (g, off)) in enumerate(zip(lefts, rights)):
            span = slice(k * rows, (k + 1) * rows)
            left_all[:, span] = arrays[a][row : row + width, :]
            right = arrays[g][off : off + cols, :].T if turned else arrays[g][:, off : off + cols]
            right_all[span, 0:cols] = right
        return dot_nn(left_all[...], right_all[:, 0:cols])

    for lefts, rights, turned, cols, group, to in plan:
        product[:, 0:cols] = multiply(lefts, rights, turned, cols)
        for out, i, block in blocks_of(group):
            at = pl.multiple_of(block * tall, 16)
            out[i, 0:tall, to : to + cols] = product[pl.ds(at, tall), 0:cols].astype(BF)
    if whole:
        outs[4][...] = multiply(*whole).astype(BF)
    if ready:
        source, group, to = ready
        cols = arrays[source].shape[1]
        for out, i, block in blocks_of(group):
            at = pl.multiple_of(block * tall, 16)
            out[i, 0:tall, to : to + cols] = arrays[source][pl.ds(at, tall), :]
    if extra is not None:
        for group in range(2):
            for out, i, block in blocks_of(group):
                out[i, tall:, :] = jnp.zeros_like(out[i, tall:, :])
                if group == 0:
                    out[i, tall:, 0:LANES] = arrays[extra][block].astype(BF)


def fold_two(bits_ref, kept0, got0, kept1, got1, give0, mine0, give1, mine1):
    for bit, kept, got, give, mine in (
        (bits_ref[1], kept0, got0, give0, mine0),
        (bits_ref[0], kept1, got1, give1, mine1),
    ):
        for i in range(2):
            for out, at in ((give, 2 * i + 1 - bit), (mine, 2 * i + bit)):
                out[i] = (kept[at].astype(F32) + got[at].astype(F32)).astype(BF)


def fold_high(bits_ref, *refs):
    (give, mine), arrays = refs[-2:], refs[:-2]
    bit = bits_ref[2]
    for g in range(len(arrays) // 2):
        kept, got = arrays[2 * g], arrays[2 * g + 1]
        for out, at in ((give, 1 - bit), (mine, bit)):
            out[g] = (kept[at].astype(F32) + got[at].astype(F32)).astype(BF)


def fold_one(bits_ref, kept, got, give, mine):
    bit = bits_ref[1]
    for i in range(2):
        for out, at in ((give, 2 * i + 1 - bit), (mine, 2 * i + bit)):
            out[i] = (kept[at].astype(F32) + got[at].astype(F32)).astype(BF)


def fold_last(kept, got, out):
    out[...] = (kept[...].astype(F32) + got[...].astype(F32)).astype(BF)


def fold_core(kept, got, near, far):
    near[...] = kept[0].astype(F32) + got[0].astype(F32)
    far[...] = (kept[1].astype(F32) + got[1].astype(F32)).astype(BF)


def fold_rep(bits_ref, near, got, send, keep):
    y = bits_ref[0]
    tall = send.shape[1]
    for z in range(4):
        for out, bit in ((send, 1 - y), (keep, y)):
            at = pl.multiple_of((2 * z + bit) * tall, 16)
            out[z] = (near[pl.ds(at, tall), :] + got[pl.ds(at, tall), :].astype(F32)).astype(BF)


def lay_columns(plan, rep_ref, *refs):
    pieces, outs, held = refs[0:4], refs[4:-1], refs[-1]
    rep = rep_ref[0]
    for k in range(4):
        held[k] = pieces[k][...]
    for (group, start, cols, how), out in zip(plan, outs):
        if how == "sum":
            tall = out.shape[0]
            total = None
            for k in range(4):
                part = pieces[k][group, pieces[k].shape[1] - tall :, start : start + cols].astype(F32)
                total = part if total is None else total + part
            out[...] = total
            continue
        tall = out.shape[0] if how == "side" else out.shape[0] // 4
        for q in range(4):
            part = held[rep ^ q, group, 0:tall, start : start + cols].astype(F32)
            if how == "side":
                out[:, q * cols : (q + 1) * cols] = part
            else:
                out[q * tall : (q + 1) * tall, :] = part


ORDER = ('dq', 'self', 'owner', 'ff1', 'kv0', 'rest1', 'kv1', 'ff2', 'kv2', 'ff3', 'rest2', 'kv3', 'memory', 'rest3', 'kv4', 'ff4', 'rest4', 'kv5', 'lay_ff', 'lay_rest', 'lay_kv')
BEFORE = {'cross': ('early',), 'ffn': ('qc_z',), 'self': ('qc_y', 'do_stack'), 'ff1': ('exports',)}
RELAY = ()
COSTS = {'deal': 2, 'self_forward': 5, 'own_keys': 6, 'cross': 17, 'ffn': 12, 'dq': 20, 'self': 12, 'ff1': 3, 'rest1': 3, 'owner': 12, 'kv0': 3, 'memory': 3}
LIMITS = {'self': 46}


def fast_on_device(
    queries, memory, routes, w_self, w_self_out, w_cross_q, w_cross_kv, w_cross_out, w_up, b_up,
    w_down, b_down, gain_one, shift_one, gain_two, shift_two, gain_three, shift_three, cotangent,
):
    streams, reps = lax.axis_size("stream"), lax.axis_size("rep")
    me, rep = lax.axis_index("stream"), lax.axis_index("rep")
    width = w_self_out.shape[0]
    hidden = w_up.shape[1]
    quarter, share, tall = hidden // 4, width // 4, width // streams
    tokens = queries[0]
    rows = tokens.shape[0]
    memory_rows = memory[0]
    rep_scalar = rep.reshape(1).astype(jnp.int32)
    bits = jnp.stack([me % 2, (me // 2) % 2, me // 4]).astype(jnp.int32)
    row_of = lambda v: v.reshape(1, -1)
    last = []

    def after(first, *others):
        return lax.optimization_barrier((first, others))[0]

    moving = {}

    def run(name, body, outs, arrays, **more):
        held = last + [array for key in BEFORE.get(name, ()) for array in moving[key]]
        if held:
            arrays = [after(arrays[0], *held)] + list(arrays[1:])
        results = local_kernel(body, outs, arrays=arrays, cost=COSTS.get(name, 2), limit=LIMITS.get(name, 24), **more)
        last[:] = results[:1]
        return results

    def hop(array, stream_flip=0, rep_flip=0):
        pairs = [
            (s * reps + r, (s ^ stream_flip) * reps + (r ^ rep_flip))
            for s in range(streams)
            for r in range(reps)
        ]
        return lax.ppermute(array, AXES, pairs)

    def stream_along(array):
        return [hop(array, k) for k in (2, 4, 6)]

    def stream_across(array, near):
        near = jnp.stack([array] + near)
        return [near, hop(near, 1)]

    def rep_full(array):
        far = hop(array, 0, 2)
        return [array, hop(array, 0, 1), far, hop(far, 0, 1)]

    def rep_each(parts):
        return [parts[0]] + [hop(parts[k], 0, k) for k in range(1, 4)]

    (parcels_out,) = run(
        "deal",
        deal_blocks,
        [like((streams, 2 * BLK, width), BF)],
        [memory_rows],
        scalars=[routes],
    )
    parcels = lax.all_to_all(parcels_out, "stream", split_axis=0, concat_axis=0, tiled=True)
    joined, r1, h1, qc, turned1 = run(
        "self_forward",
        self_forward,
        [
            like((rows, 3 * width), BF),
            like((rows, width), F32),
            like((rows, width), BF),
            like((rows, width), BF),
            like((3 * width, rows), BF),
        ],
        [tokens, w_self, w_self_out, w_cross_q, row_of(gain_one), row_of(shift_one)],
    )
    early = rep_full(turned1)
    moving["early"] = early
    kv_own, memory_turned = run(
        "own_keys",
        own_keys,
        [like((memory_rows.shape[0], 2 * width), BF), like(memory_rows.shape[::-1], BF)],
        [memory_rows, w_cross_kv],
    )
    routes_all = lax.all_gather(
        after(routes[0], kv_own, *early), "stream", axis=0, tiled=False
    )
    keys = streams * 2 * BLK
    o2, kv, sums, bias = run(
        "cross",
        cross_forward,
        [
            like((rows, width), BF),
            like((keys, 2 * width), BF),
            like((2 * rows, LANES), F32),
            like((8, keys), F32),
        ],
        [qc, parcels, w_cross_kv],
        scalars=[routes_all, me.reshape(1).astype(jnp.int32)],
        scratch=[pltpu.VMEM((2 * rows, keys), F32), pltpu.VMEM((2 * rows, keys), BF)],
    )
    qc_near = stream_along(after(qc, parcels))
    qc_all = stream_across(qc, qc_near)
    moving["qc_z"], moving["qc_stack"], moving["qc_y"] = qc_near, qc_all[:1], qc_all[1:]

    vec = jnp.concatenate([row_of(v) for v in (gain_two, shift_two, gain_three, shift_three)])
    each = 2 * quarter + share
    layer_out, dr2, do2, sums2, small_ff, small_up, *parts = run(
        "ffn",
        feed_forward,
        [
            like((rows, width), BF),
            like((rows, width), F32),
            like((rows + 16, width), BF),
            like((2 * rows, LANES), F32),
            like((8, width), F32),
            like((1, hidden), F32),
            like((each, rows), BF),
            like((3 * width + each, rows), BF),
            like((3 * width + 2 * each, rows), BF),
        ],
        [
            o2, h1, sums, w_cross_out, w_up, w_down, row_of(b_up), row_of(b_down), vec,
            cotangent[0],
        ],
        scalars=[rep_scalar],
        scratch=[
            pltpu.VMEM((rows, hidden), F32),
            pltpu.VMEM((hidden, rows), BF),
            pltpu.VMEM((hidden, rows), BF),
        ],
    )
    near, far = hop(parts[1], 0, 1), hop(parts[2], 0, 2)
    do2_near = stream_along(do2)
    do2_all = stream_across(do2, do2_near)
    moving["do_z"], moving["do_stack"], moving["do_y"] = do2_near, do2_all[:1], do2_all[1:]
    moving["near"], moving["far"] = [near], [far]
    v = {}

    def step_dq():
        (v["dqc"],) = run(
            "dq", cross_backward, [like((rows, width), BF)], [qc, do2, kv, bias, sums2]
        )

    def step_self():
        v["d_tokens"], v["small_self"], *exports = run(
            "self",
            self_backward,
            [like((rows, width), F32), like((8, width), F32)]
            + [like((rows, width + share), BF)] * 4,
            [v["dqc"], dr2, r1, joined, w_cross_q, w_self_out, w_self, row_of(gain_one)],
            scalars=[rep_scalar],
            scratch=[
                pltpu.VMEM((rows, 3 * width), BF),
                pltpu.VMEM((4, rows, width + share), BF),
            ],
        )
        v["grads"] = rep_each(exports)
        moving["exports"] = v["grads"][1:]
        relayed = hop(after(far, v["small_self"], *[a for k in RELAY for a in moving[k]]), 0, 1)
        moving["relay"] = [relayed]
        v["shared"] = [parts[1], near, far, relayed, parts[0]]

    def full_at(row):
        return ((0, row), (1, row), (2, each + row), (3, each + row))

    def each_at(row):
        return ((4, row), (1, 3 * width + row), (2, row), (3, each + 3 * width + row))

    def blocks_of(name, plan, arrays, size, wide, whole=None, ready=None, extra=None):
        return run(
            name,
            functools.partial(weight_blocks, plan, whole, ready, extra),
            [like((4, size, wide), BF)] * 4 + ([like((width, whole[3]), BF)] if whole else []),
            arrays,
            scalars=[bits],
            scratch=[
                pltpu.VMEM((width, 4 * rows), BF),
                pltpu.VMEM((4 * rows, width), BF),
                pltpu.VMEM((width, width), F32),
            ],
        )

    def first_hops(key, blocks):
        send0, keep0, send1, keep1 = blocks
        v[key] = [keep0, hop(send0, 1), keep1, hop(send1, 2)]

    def second_hops(name, key):
        give0, mine0, give1, mine1 = run(
            name, fold_two, [like((2,) + v[key][0].shape[1:], BF)] * 4, v[key], scalars=[bits]
        )
        v[key] = [mine0, hop(give0, 2), mine1, hop(give1, 1)]

    def third_hop(name, key):
        arrays = v[key]
        give, mine = run(
            name,
            fold_high,
            [like((len(arrays) // 2,) + arrays[0].shape[1:], BF)] * 2,
            arrays,
            scalars=[bits],
        )
        v[key] = [mine, hop(give, 4)]

    def last_hops(name, key):
        (piece,) = run(name, fold_last, [like(v[key][0].shape, BF)], v[key])
        v[key] = rep_full(piece)

    def gathered(name, key, plan, shapes):
        return run(
            name,
            functools.partial(lay_columns, plan),
            [like(shape, F32) for shape in shapes],
            v[key],
            scalars=[rep_scalar],
            scratch=[pltpu.VMEM((4,) + v[key][0].shape, BF)],
        )

    def step_ff1():
        *blocks, v["cross_out"] = blocks_of(
            "ff1",
            [
                (full_at(0), each_at(quarter), True, quarter, 0, 0),
                (each_at(0), full_at(2 * width), True, width, 1, 0),
            ],
            v["shared"],
            tall,
            width,
            whole=(full_at(width), each_at(2 * quarter), True, share),
        )
        first_hops("ff", blocks)
        moving["ff_first"] = [v["ff"][1], v["ff"][3]]

    def step_rest1():
        vectors = jnp.concatenate([small_ff[0:5], v["small_self"][0:2]]).reshape(7, streams, tall)
        vectors = jnp.pad(vectors.transpose(1, 0, 2), ((0, 0), (0, 0), (0, LANES - tall)))
        vectors = jnp.concatenate(
            [
                vectors,
                small_up.reshape(streams, -1, LANES),
                jnp.zeros((streams, 9 - hidden // streams // LANES, LANES), F32),
            ],
            axis=1,
        )
        early_at = lambda row: tuple((k, row) for k in range(4))
        grads_at = lambda col: tuple((4 + k, col) for k in range(4))
        first_hops(
            "rest",
            blocks_of(
                "rest1",
                [
                    (early_at(0), grads_at(0), False, 3 * share, 0, 0),
                    (early_at(width), grads_at(3 * share), False, share, 1, 0),
                    (early_at(2 * width), grads_at(4 * share), False, share, 1, share),
                ],
                early + v["grads"] + [vectors, v["cross_out"]],
                tall + 16,
                3 * share,
                ready=(9, 1, 2 * share),
                extra=8,
            ),
        )
        moving["rest_first"] = [v["rest"][1], v["rest"][3]]

    kv_wide = 2 * width // 4

    def step_owner():
        (v["dkv"],) = run(
            "owner",
            owner_backward,
            [like((memory_rows.shape[0], 2 * width), BF)],
            qc_all + do2_all + [kv_own],
            scalars=[(routes[0] ^ me).astype(jnp.int32)],
            scratch=[
                pltpu.VMEM((streams, PAIRS, 2 * rows, LANES), BF),
                pltpu.VMEM((streams, PAIRS, 2 * rows, LANES), BF),
                pltpu.VMEM((streams, 16, 2 * rows), F32),
            ],
        )

    def step_kv0():
        kv_keep, kv_send = run(
            "kv0",
            memory_weights,
            [like((2, width, kv_wide), BF)] * 2,
            [v["dkv"], memory_turned],
            scalars=[rep_scalar],
        )
        v["kv"] = [kv_keep, hop(kv_send, 0, 1)]

    def step_kv1():
        near_sum, far_sum = run(
            "kv1", fold_core, [like((width, kv_wide), F32), like((width, kv_wide), BF)], v["kv"]
        )
        v["kv"] = [near_sum, hop(far_sum, 0, 2)]

    def step_kv2():
        send, keep = run(
            "kv2", fold_rep, [like((4, tall, kv_wide), BF)] * 2, v["kv"], scalars=[bits]
        )
        v["kv"] = [keep, hop(send, 1)]

    def step_kv3():
        give, mine = run(
            "kv3", fold_one, [like((2, tall, kv_wide), BF)] * 2, v["kv"], scalars=[bits]
        )
        v["kv"] = [mine, hop(give, 2)]

    def step_memory():
        (v["d_memory"],) = run(
            "memory", memory_backward, [like(memory_rows.shape, BF)], [v["dkv"], w_cross_kv]
        )

    def step_lay_ff():
        v["g_up"], v["g_down"] = gathered(
            "lay_ff",
            "ff",
            [(0, 0, quarter, "side"), (1, 0, width, "below")],
            [(tall, hidden), (hidden // streams, width)],
        )

    def step_lay_rest():
        v["g_self"], v["g_self_out"], v["g_query"], v["g_out"], v["g_vec"] = gathered(
            "lay_rest",
            "rest",
            [
                (0, 0, 3 * share, "side"),
                (1, 0, share, "side"),
                (1, share, share, "side"),
                (1, 2 * share, share, "side"),
                (0, 0, LANES, "sum"),
            ],
            [(tall, 3 * width), (tall, width), (tall, width), (tall, width), (16, LANES)],
        )

    def step_lay_kv():
        (v["g_kv"],) = gathered("lay_kv", "kv", [(0, 0, kv_wide, "side")], [(tall, 2 * width)])

    steps = {
        "dq": step_dq,
        "self": step_self,
        "ff1": step_ff1,
        "rest1": step_rest1,
        "owner": step_owner,
        "kv0": step_kv0,
        "kv1": step_kv1,
        "kv2": step_kv2,
        "kv3": step_kv3,
        "kv4": lambda: third_hop("kv4", "kv"),
        "kv5": lambda: last_hops("kv5", "kv"),
        "ff2": lambda: second_hops("ff2", "ff"),
        "ff3": lambda: third_hop("ff3", "ff"),
        "ff4": lambda: last_hops("ff4", "ff"),
        "rest2": lambda: second_hops("rest2", "rest"),
        "rest3": lambda: third_hop("rest3", "rest"),
        "rest4": lambda: last_hops("rest4", "rest"),
        "memory": step_memory,
        "lay_ff": step_lay_ff,
        "lay_rest": step_lay_rest,
        "lay_kv": step_lay_kv,
    }
    for name in ORDER:
        steps[name]()
    piece = lambda row: v["g_vec"][row, 0:tall]
    return (
        layer_out[None],
        v["d_tokens"][None],
        v["d_memory"][None],
        v["g_self"],
        v["g_self_out"],
        v["g_query"],
        v["g_kv"],
        v["g_out"],
        v["g_up"],
        v["g_vec"][7 : 7 + hidden // streams // LANES].reshape(-1),
        v["g_down"],
        piece(0),
        piece(5),
        piece(6),
        piece(1),
        piece(2),
        piece(3),
        piece(4),
    )


def solution(mesh):
    in_specs = (
        P("rep", "stream", None),
        P("rep", "stream", None),
        P("rep", "stream"),
        P(),
        P(),
        P(),
        P(),
        P(),
        P(),
        P(),
        P(),
        P(),
        P(),
        P(),
        P(),
        P(),
        P(),
        P(),
        P("rep", "stream", None),
    )
    out_specs = (
        P("rep", "stream", None),
        P("rep", "stream", None),
        P("rep", "stream", None),
        P("stream", None),
        P("stream", None),
        P("stream", None),
        P("stream", None),
        P("stream", None),
        P("stream", None),
        P("stream"),
        P("stream", None),
        P("stream"),
        P("stream"),
        P("stream"),
        P("stream"),
        P("stream"),
        P("stream"),
        P("stream"),
    )
    small_slice = (mesh.shape["stream"], mesh.shape["rep"]) == (8, 4)
    return jax.shard_map(
        fast_on_device if small_slice else on_device, mesh=mesh, in_specs=in_specs, out_specs=out_specs, check_vma=False
    )
```
